32 devices in a mesh: ctx: 8 (over y, x, core), wsh: 4 (over z).
Axes of the slice: x: 2, y: 2, z: 4, core: 2. Of those that a mesh axis runs over, the one named last changes fastest.
Arguments:
- hidden_in: bfloat16 [4, 1024, 1536], P('wsh', 'ctx'), may hold values from -6 to 6
- routes: int32 [1, 4, 1024, 4], P(None, 'wsh', 'ctx'), may hold values from 0 to 7, all different within a row; in each aligned block of 128 rows (0 to 127, 128 to 255, ..., all dimensions but the last counted through in order) at most 128 rows name the same one
- cotangent: float32 [4, 1024, 1536], P('wsh', 'ctx'), may hold values from -6 to 6
- norm_attn: bfloat16 [1, 1536], P(None, ('ctx', 'wsh')), may hold values from 0.25 to 1.75
- w_query: bfloat16 [1, 1536, 1536], P(None, ('ctx', 'wsh')), may hold values from -0.15625 to 0.15625
- key_projection: bfloat16 [1, 1536, 256], P(None, ('ctx', 'wsh')), may hold values from -0.15625 to 0.15625
- value_projection: bfloat16 [1, 1536, 256], P(None, ('ctx', 'wsh')), may hold values from -0.15625 to 0.15625
- w_out: bfloat16 [1, 1536, 1536], P(None, ('ctx', 'wsh')), may hold values from -2 to 2
- norm_moe: bfloat16 [1, 1536], P(None, ('ctx', 'wsh')), may hold values from 0.25 to 1.75
- w_router: bfloat16 [1, 1536, 8], P(None, ('ctx', 'wsh')), may hold values from -0.078125 to 0.078125
- w_gate: bfloat16 [1, 1536, 8, 768], P(None, 'ctx', 'wsh'), may hold values from -0.15625 to 0.15625
- w_up: bfloat16 [1, 1536, 8, 768], P(None, 'ctx', 'wsh'), may hold values from -0.15625 to 0.15625
- w_down: bfloat16 [1, 1536, 8, 768], P(None, 'ctx', 'wsh'), may hold values from -0.625 to 0.625
Outputs:
- output: float32 [4, 1024, 1536], P('wsh', 'ctx')
- input_grad: float32 [4, 1024, 1536], P('wsh', 'ctx')
- grad_norm_attn: float32 [1, 1536], P(None, ('ctx', 'wsh'))
- grad_w_query: float32 [1, 1536, 1536], P(None, ('ctx', 'wsh'))
- grad_w_key: float32 [1, 1536, 256], P(None, ('ctx', 'wsh'))
- grad_w_value: float32 [1, 1536, 256], P(None, ('ctx', 'wsh'))
- grad_w_out: float32 [1, 1536, 1536], P(None, ('ctx', 'wsh'))
- grad_norm_moe: float32 [1, 1536], P(None, ('ctx', 'wsh'))
- grad_w_router: float32 [1, 1536, 8], P(None, ('ctx', 'wsh'))
- grad_w_gate: float32 [1, 1536, 8, 768], P(None, 'ctx', 'wsh')
- grad_w_up: float32 [1, 1536, 8, 768], P(None, 'ctx', 'wsh')
- grad_w_down: float32 [1, 1536, 8, 768], P(None, 'ctx', 'wsh')
The draws below stay inside these ranges and needn't reach their ends.
Inputs may be any that keep to these rules, and one draw needn't show every extreme that they name: `routes`: each token names 4 different experts in each layer. Within the 128 tokens of one device (aligned blocks of each sequence) no expert is named more than 128 times, and in some blocks one is named exactly 128 times.
All inputs are finite; a program needn't handle non-finite values.
Results may differ from the reference program's by a relative error of at most 0.02.
Values may be sent and summed in bfloat16 or wider, within the bound.
A program may use at most 192 MiB of HBM per device.

```python
import math
import jax
import jax.numpy as jnp
import numpy as np
from jax import lax

MODEL_DIM = 1536
QUERY_HEADS = 12
KEY_VALUE_HEADS = 2
HEAD_DIM = 128
FF = 768
EXPERTS = 8
TOP = 4
LAYER_COUNT = 1
TOK_DEV = 128
SEQUENCE_LENGTH = 1024
SEQUENCE_COUNT = 4
CAP = 128


def levels(key, dims, cuts, low, largest):
    level, own = 1.0, jax.random.fold_in(key, 6)
    for dim, shards_of in cuts:
        steps = jnp.exp(jax.random.uniform(jax.random.fold_in(own, dim), (shards_of,), jnp.float32, low / len(cuts), largest / len(cuts)))
        level = level * jnp.repeat(steps, dims[dim] // shards_of).reshape([-1 if axis == dim else 1 for axis in range(len(dims))])
    return level


def routed_block(rng, own, number, rows, amount, top, limit, skew):
    ranking = jax.random.permutation(rng, amount)
    crowded, usual = shares(amount, rows * top, limit, skew, True), shares(amount, rows * top, limit, skew, False)
    places = jnp.arange(amount)

    def named(lengths, rotation):
        used = int((lengths > 0).sum())
        fixed = max(1, used // 4)
        shifted = fixed + (places - fixed + rotation * (used - fixed)) % max(1, amount - fixed)
        return jnp.zeros((amount,), jnp.int32).at[ranking[jnp.where(places < fixed, places, shifted)]].set(jnp.asarray(lengths, jnp.int32))

    lengths = jnp.where(number % 4 == 0, named(crowded, number // 4), named(usual, number - number // 4 - 1))
    mixed = jax.random.permutation(jax.random.fold_in(own, 3), amount)
    donor, receiver = mixed[0:amount // 2 * 2:2], mixed[1:amount // 2 * 2:2]
    margin = jnp.minimum(lengths[donor] - 1, limit - lengths[receiver]) // 2
    margin = jnp.where((donor == ranking[0]) | (receiver == ranking[0]) | (lengths[receiver] == 0), 0, jnp.maximum(margin, 0))
    shifted = jax.random.randint(jax.random.fold_in(own, 4), (amount // 2,), 0, 1 << 20) % (margin + 1)
    lengths = lengths.at[donor].add(-shifted).at[receiver].add(shifted)
    items = jnp.searchsorted(jnp.cumsum(lengths), jnp.arange(rows * top), side="right").astype(jnp.int32)
    grid = items.reshape(top, rows).T
    grid = grid[jax.random.permutation(jax.random.fold_in(own, 1), rows)]
    rotation = jax.random.randint(jax.random.fold_in(own, 2), (rows, 1), 0, top)
    return jnp.take_along_axis(grid, (jnp.arange(top)[None, :] + rotation) % top, axis=1)


def shares(amount, total, bound, lean, full):
    portions = [(1 << 20) // math.isqrt(rank ** lean) + 1 for rank in range(1, amount + 1)]
    largest = bound if full else min(bound, max(-(-total // amount), total * portions[0] // sum(portions)))
    least = 1 if total - largest >= amount - 1 else 0
    counts, spare = [largest] + [least] * (amount - 1), total - largest - least * (amount - 1)
    while spare > 0:
        movable = [i for i in range(1, amount) if counts[i] < largest] or [i for i in range(1, amount) if counts[i] < bound]
        pool, left = sum([portions[i] for i in movable]), spare
        for i in movable:
            more = min(bound - counts[i], max(1, left * portions[i] // pool), spare)
            counts[i] = counts[i] + more
            spare = spare - more
    return np.array(counts)


def normal_values(own_key, dims, deviation, reach, cuts=(), held_as=jnp.bfloat16):
    drawn = deviation * jax.random.normal(own_key, dims, jnp.float32)
    if cuts:
        drawn = drawn * levels(own_key, dims, cuts, -0.22, 0.18)
    return jnp.clip(drawn, -reach, reach).astype(held_as)


def setup_inputs(seed: int = 0) -> dict:
    splits = jax.random.split(jax.random.key(seed), 14)
    hidden_in = normal_values(splits[0], (SEQUENCE_COUNT, SEQUENCE_LENGTH, MODEL_DIM), 1.0, 6.0, ((0, 4), (1, 8)))
    routes_keys = jax.random.split(jax.random.fold_in(splits[1], 1), LAYER_COUNT * SEQUENCE_COUNT * SEQUENCE_LENGTH // TOK_DEV)
    routes_turns = jax.random.permutation(jax.random.fold_in(splits[1], 3), LAYER_COUNT * SEQUENCE_COUNT * SEQUENCE_LENGTH // TOK_DEV)
    routes = jax.vmap(lambda own, number: routed_block(jax.random.fold_in(splits[1], 2), own, number, TOK_DEV, EXPERTS, TOP, CAP, 1))(routes_keys, routes_turns).reshape((LAYER_COUNT, SEQUENCE_COUNT, SEQUENCE_LENGTH, TOP))
    cotangent = normal_values(splits[2], (SEQUENCE_COUNT, SEQUENCE_LENGTH, MODEL_DIM), 1.0, 6.0, ((0, 4), (1, 8)), jnp.float32)
    norm_attn = jnp.clip(1.0 + 0.15 * jax.random.normal(splits[3], (LAYER_COUNT, MODEL_DIM), jnp.float32), 0.25, 1.75).astype(jnp.bfloat16)
    w_query = normal_values(splits[4], (LAYER_COUNT, MODEL_DIM, QUERY_HEADS * HEAD_DIM), MODEL_DIM ** -0.5, 0.15625, ((1, 32),))
    key_projection = normal_values(splits[5], (LAYER_COUNT, MODEL_DIM, KEY_VALUE_HEADS * HEAD_DIM), MODEL_DIM ** -0.5, 0.15625, ((1, 32),))
    value_projection = normal_values(splits[6], (LAYER_COUNT, MODEL_DIM, KEY_VALUE_HEADS * HEAD_DIM), MODEL_DIM ** -0.5, 0.15625, ((1, 32),))
    w_out = normal_values(splits[7], (LAYER_COUNT, MODEL_DIM, QUERY_HEADS * HEAD_DIM), (max(1, 5 * QUERY_HEADS * HEAD_DIM // SEQUENCE_LENGTH)) ** -0.5, 2.0, ((1, 32),))
    norm_moe = jnp.clip(1.0 + 0.15 * jax.random.normal(splits[8], (LAYER_COUNT, MODEL_DIM), jnp.float32), 0.25, 1.75).astype(jnp.bfloat16)
    w_router = normal_values(splits[9], (LAYER_COUNT, MODEL_DIM, EXPERTS), (4 * MODEL_DIM) ** -0.5, 0.078125, ((1, 32),))
    w_gate = normal_values(splits[10], (LAYER_COUNT, MODEL_DIM, EXPERTS, FF), MODEL_DIM ** -0.5, 0.15625, ((1, 8), (2, 4)))
    w_up = normal_values(splits[11], (LAYER_COUNT, MODEL_DIM, EXPERTS, FF), MODEL_DIM ** -0.5, 0.15625, ((1, 8), (2, 4)))
    w_down = normal_values(splits[12], (LAYER_COUNT, MODEL_DIM, EXPERTS, FF), (FF // 10) ** -0.5, 0.625, ((1, 8), (2, 4)))
    return {"hidden_in": hidden_in, "routes": routes, "cotangent": cotangent, "norm_attn": norm_attn, "w_query": w_query, "key_projection": key_projection, "value_projection": value_projection, "w_out": w_out, "norm_moe": norm_moe, "w_router": w_router, "w_gate": w_gate, "w_up": w_up, "w_down": w_down}


NORM_EPSILON = 1e-06
ROTARY_BASE = 1000000.0
FULL_PRECISION = lax.Precision.HIGHEST

@jax.custom_vjp
def low(v):
    return lax.optimization_barrier(v.astype(jnp.bfloat16)).astype(jnp.float32)

@jax.custom_vjp
def low_back(v):
    return v

def low_keep(v):
    return (low(v), None)

def low_pass(kept, grad):
    return (grad,)

def back_keep(v):
    return (v, None)

def back_low(kept, grad):
    return (low(grad),)
low.defvjp(low_keep, low_pass)
low_back.defvjp(back_keep, back_low)

def normalize(hidden_state, gain):
    return hidden_state * lax.rsqrt(lax.optimization_barrier(jnp.mean(hidden_state * hidden_state, axis=-1, keepdims=True)) + NORM_EPSILON) * gain

def apply_rotary(values_in, token_positions):
    half_size = values_in.shape[-1] // 2
    frequency = ROTARY_BASE ** (-jnp.arange(half_size, dtype=jnp.float32) * 2.0 / values_in.shape[-1])
    angles = token_positions.astype(jnp.float32)[:, None] * frequency[None, :]
    cosine = jnp.cos(angles)[:, None, :]
    sine_rows = jnp.sin(angles)[:, None, :]
    first_half = values_in[..., :half_size]
    second = values_in[..., half_size:]
    return jnp.concatenate([first_half * cosine - second * sine_rows, second * cosine + first_half * sine_rows], axis=-1)

def attend_sequence(inputs):
    query_seq, key_seq, value_seq = inputs
    block_row_list = min(512, SEQUENCE_LENGTH)
    block_count = SEQUENCE_LENGTH // block_row_list
    key_positions = jnp.arange(SEQUENCE_LENGTH, dtype=jnp.int32)
    score_scale = HEAD_DIM ** (-0.5)

    def one_block(block_in):
        query_tile, start = block_in
        grouped_heads = query_tile.reshape(block_row_list, KEY_VALUE_HEADS, QUERY_HEADS // KEY_VALUE_HEADS, HEAD_DIM)
        scores = low_back(jnp.einsum('qhgd,khd->hgqk', grouped_heads, key_seq, precision=FULL_PRECISION) * score_scale)
        query_positions = start + jnp.arange(block_row_list, dtype=jnp.int32)
        allowed = key_positions[None, :] <= query_positions[:, None]
        scores = jnp.where(allowed[None, None], scores, -1e+30)
        highest = lax.optimization_barrier(jnp.max(scores, axis=-1, keepdims=True))
        log_total = highest + jnp.log(lax.optimization_barrier(jnp.sum(jnp.exp(scores - highest), axis=-1, keepdims=True)))
        weights = low(jnp.exp(scores - log_total))
        attended = jnp.einsum('hgqk,khd->qhgd', weights, value_seq, precision=FULL_PRECISION)
        return attended.reshape(block_row_list, QUERY_HEADS * HEAD_DIM)
    starts = jnp.arange(block_count, dtype=jnp.int32) * block_row_list
    attended = lax.map(jax.checkpoint(one_block), (query_seq.reshape(block_count, block_row_list, QUERY_HEADS, HEAD_DIM), starts))
    return attended.reshape(SEQUENCE_LENGTH, QUERY_HEADS * HEAD_DIM)

def expert_layer(gate_w, up_w, down_w):

    def one_block(block_in):
        token_rows, picks_in, logit_rows = block_in
        expert_ids = jnp.arange(EXPERTS, dtype=jnp.int32)
        matches = picks_in[:, :, None] == expert_ids[None, None, :]
        chosen = lax.optimization_barrier(jnp.sum(jnp.where(matches, logit_rows[:, None, :], 0.0), axis=-1))
        gate_weights = jax.nn.softmax(chosen, axis=-1)
        flat_matches = matches.reshape(-1, EXPERTS).astype(jnp.int32)
        earlier = jnp.cumsum(flat_matches, axis=0) - flat_matches
        targets = picks_in.reshape(-1) * CAP + lax.optimization_barrier(jnp.sum(earlier * flat_matches, axis=1))
        sources = jnp.repeat(token_rows, TOP, axis=0)
        buffer = jnp.zeros((EXPERTS * CAP, MODEL_DIM), token_rows.dtype).at[targets].set(sources)
        buffer = low_back(buffer).reshape(EXPERTS, CAP, MODEL_DIM)
        gate_pre = low_back(jnp.einsum('ecd,def->ecf', buffer, gate_w, precision=FULL_PRECISION))
        up_pre = low_back(jnp.einsum('ecd,def->ecf', buffer, up_w, precision=FULL_PRECISION))
        activations = low(jax.nn.silu(gate_pre) * up_pre)
        produced = low(low_back(jnp.einsum('ecf,def->ecd', activations, down_w, precision=FULL_PRECISION)))
        picked = produced.reshape(EXPERTS * CAP, MODEL_DIM)[targets].reshape(TOK_DEV, TOP, MODEL_DIM)
        return lax.optimization_barrier(jnp.sum(gate_weights[:, :, None] * picked, axis=1))
    return jax.checkpoint(one_block)

def reference(hidden_in, routes, cotangent, norm_attn, w_query, key_projection, value_projection, w_out, norm_moe, w_router, w_gate, w_up, w_down):
    params = (norm_attn.astype(jnp.float32), w_query.astype(jnp.float32), key_projection.astype(jnp.float32), value_projection.astype(jnp.float32), w_out.astype(jnp.float32), norm_moe.astype(jnp.float32), w_router.astype(jnp.float32), w_gate.astype(jnp.float32), w_up.astype(jnp.float32), w_down.astype(jnp.float32))

    def forward(hidden_state, weight_set):
        gain_attn, query_matrix, key_matrix, value_matrix, output_matrix, gain_moe, router_matrix, gate_w, up_w, down_w = weight_set
        token_positions = jnp.arange(SEQUENCE_LENGTH, dtype=jnp.int32)
        block_total = SEQUENCE_COUNT * SEQUENCE_LENGTH // TOK_DEV
        for layer_number in range(LAYER_COUNT):
            attention_normed = low(normalize(hidden_state, gain_attn[layer_number]))
            query_unrotated = low_back(jnp.einsum('awk,kp->awp', attention_normed, query_matrix[layer_number], precision=FULL_PRECISION))
            key_unrotated = low_back(jnp.einsum('awk,kp->awp', attention_normed, key_matrix[layer_number], precision=FULL_PRECISION))
            value_unprojected = low_back(jnp.einsum('awk,kp->awp', attention_normed, value_matrix[layer_number], precision=FULL_PRECISION))
            query_all = low(apply_rotary(query_unrotated.reshape(SEQUENCE_COUNT, SEQUENCE_LENGTH, QUERY_HEADS, HEAD_DIM), token_positions))
            key_full = low(apply_rotary(key_unrotated.reshape(SEQUENCE_COUNT, SEQUENCE_LENGTH, KEY_VALUE_HEADS, HEAD_DIM), token_positions))
            value_full = low(value_unprojected.reshape(SEQUENCE_COUNT, SEQUENCE_LENGTH, KEY_VALUE_HEADS, HEAD_DIM))
            attended = lax.map(attend_sequence, (query_all, key_full, value_full))
            mixed_reduced = low(low_back(attended))
            post_attention = hidden_state + low_back(jnp.einsum('fhz,yz->fhy', mixed_reduced, output_matrix[layer_number], precision=FULL_PRECISION))
            expert_normed = low(normalize(post_attention, gain_moe[layer_number]))
            router_logits = low_back(jnp.einsum('tnx,xy->tny', expert_normed, router_matrix[layer_number], precision=FULL_PRECISION))
            expert_fn = expert_layer(gate_w[layer_number], up_w[layer_number], down_w[layer_number])
            moe_out = lax.map(expert_fn, (expert_normed.reshape(block_total, TOK_DEV, MODEL_DIM), routes[layer_number].reshape(block_total, TOK_DEV, TOP), router_logits.reshape(block_total, TOK_DEV, EXPERTS)))
            hidden_state = post_attention + moe_out.reshape(SEQUENCE_COUNT, SEQUENCE_LENGTH, MODEL_DIM)
        return hidden_state
    output, pullback = jax.vjp(forward, hidden_in.astype(jnp.float32), params)
    input_grad, weight_grads = pullback(cotangent)
    return (output, input_grad, weight_grads[0], weight_grads[1], weight_grads[2], weight_grads[3], weight_grads[4], weight_grads[5], weight_grads[6], weight_grads[7], weight_grads[8], weight_grads[9])
```

```python
import functools
import jax
import jax.numpy as jnp
from jax import lax
from jax.experimental import pallas as pl
from jax.experimental.pallas import tpu as pltpu
from jax.sharding import PartitionSpec as P

QUERY_HEADS = 12
KEY_VALUE_HEADS = 2
HEAD_DIM = 128
CAP = 128
NORM_EPSILON = 1e-06
ROTARY_BASE = 1000000.0
MESH = pl.DeviceIdType.MESH
HEAD = 128
TOP = 4
EPS = 1e-06
BASE = 1000000.0
F32 = jnp.float32
BF16 = jnp.bfloat16


def dot(a, b):
    return lax.dot_general(a, b, (((1,), (0,)), ((), ())), preferred_element_type=F32)


def dot_t(a, b):
    return lax.dot_general(a, b, (((1,), (1,)), ((), ())), preferred_element_type=F32)


def t_dot(a, b):
    return lax.dot_general(a, b, (((0,), (0,)), ((), ())), preferred_element_type=F32)


class Place:
    def __init__(self, nctx, nz):
        self.nctx, self.nz, self.nch = nctx, nz, nctx // 2
        self.c = lax.axis_index("ctx")
        self.z = lax.axis_index("wsh")
        self.chip = self.c // 2
        self.core = self.c % 2
        self.sib = self.chip * 2 + 1 - self.core
        self.square = self.nch == 4

    def xchip(self):
        return self.chip + 1 - 2 * (self.chip % 2)

    def ychip(self):
        return (self.chip + 2) % 4

    def zto(self, dz):
        return (self.z + dz) % self.nz

    def zfrom(self, dz):
        return (self.z + self.nz - dz) % self.nz


class Sends:
    def __init__(self, sems, count):
        self.sems, self.count, self.used, self.live = sems, count, 0, []

    def start(self, src, dst, rsem, dev):
        assert self.used < self.count
        cp = pltpu.make_async_remote_copy(
            src_ref=src,
            dst_ref=dst,
            send_sem=self.sems.at[self.used],
            recv_sem=rsem,
            device_id=dev,
            device_id_type=MESH,
        )
        cp.start()
        self.used += 1
        self.live.append(cp)
        return cp

    def local(self, src, dst):
        assert self.used < self.count
        cp = pltpu.make_async_copy(src, dst, self.sems.at[self.used])
        cp.start()
        self.used += 1
        return cp

    def drain(self):
        for cp in self.live:
            cp.wait_send()
        self.live = []


def arrived(ref, sem):
    pltpu.make_async_copy(ref, ref, sem).wait()


def greet(pl_, plane=True, column=True):
    bar = pltpu.get_barrier_semaphore()
    n = 0
    if plane:
        for k in range(1, pl_.nctx):
            pl.semaphore_signal(
                bar, inc=1, device_id=((pl_.c + k) % pl_.nctx, pl_.z), device_id_type=MESH
            )
            n += 1
    if column:
        for k in range(1, pl_.nz):
            pl.semaphore_signal(bar, inc=1, device_id=(pl_.c, pl_.zto(k)), device_id_type=MESH)
            n += 1
    pl.semaphore_wait(bar, n)


def rms(x, width):
    return lax.rsqrt(jnp.sum(x * x, axis=-1, keepdims=True) * (1.0 / width) + EPS)


def gain_row(extra, lane):
    pick = (lax.broadcasted_iota(jnp.int32, (16, extra.shape[1]), 1) == lane).astype(BF16)
    return dot_t(pick, extra)[0:1]


def rope(x, cos, sin):
    return x * cos + pltpu.roll(x, HEAD // 2, 1) * sin


def attend_kernel(
    cfg,
    h_ref, g_ref, mask_ref, cos_ref, sin_ref, pa_ref, pb_ref, we_ref,
    wa_out, wb_out, we_out, q_out, kv_out, lse_out, ob_out, xa_out, h1_out, xm_out, g_out, gt_out,
    wa, wb, za, zb, hbuf, xa, qs, kv, obs, part, pget, lses, xms, gts, xmall, gall, gtall,
    ssem, ra, rb, re, rza, rzb, rmisc, rkv, rxm, rxf,
):
    nctx, nz, width, rp, t0, heads, fc = cfg
    pc = Place(nctx, nz)
    nch = pc.nch
    t2 = 2 * t0
    qw = heads * HEAD
    kw = qw + 2 * HEAD
    dp = wa.shape[0]
    snd = Sends(ssem, ssem.shape[0])
    core, z, c, chip = pc.core, pc.z, pc.c, pc.chip
    greet(pc)

    for dz in range(1, nz):
        snd.start(pa_ref, za.at[z], rza.at[dz], (c, pc.zto(dz)))
    snd.start(h_ref, hbuf.at[core], rmisc.at[0], (pc.sib, z))
    for dz in range(1, nz):
        snd.start(pb_ref, zb.at[z], rzb.at[dz], (c, pc.zto(dz)))

    def rows(cc, s, count=1):
        return pl.ds(pl.multiple_of((cc * nz + s) * rp, 16), count * rp)

    def spread(src, dst, rs, s):
        here = dst.at[rows(c, s)]
        sem = rs.at[c * nz + s]
        snd.start(src.at[1 - core], here, sem, (pc.sib, z))
        if pc.square:
            chips = [pc.xchip(), pc.ychip()]
        else:
            chips = [(chip + k) % nch for k in range(1, nch)]
        for q in chips:
            for k in range(2):
                snd.start(src.at[k], here, sem, (q * 2 + k, z))

    def forward(dst, rs, s):
        for source, to in ((pc.ychip() * 2, pc.xchip()), (pc.xchip() * 2 + 1, pc.ychip())):
            here = dst.at[rows(source, s)]
            sem = rs.at[source * nz + s]
            arrived(here, sem)
            snd.start(here, here, sem, (to * 2 + core, z))

    def settle(dst, rs):
        for k in range(1, nctx):
            if pc.square:
                continue
            for s in range(nz):
                cc = (c + k) % nctx
                arrived(dst.at[rows(cc, s)], rs.at[cc * nz + s])
        if pc.square:
            xs, ys, ds = pc.xchip() * 2, pc.ychip() * 2, (3 - chip) * 2
            for cc in (pc.sib, xs, ys + 1, ds, ds + 1):
                for s in range(nz):
                    arrived(dst.at[rows(cc, s)], rs.at[cc * nz + s])

    own_a = snd.local(pa_ref.at[core], wa.at[rows(c, z)])
    own_b = snd.local(pb_ref.at[core], wb.at[rows(c, z)])
    spread(pa_ref, wa, ra, z)
    keep = [own_a, own_b]
    for dz in range(1, nz):
        s = pc.zfrom(dz)
        arrived(za.at[s], rza.at[dz])
        spread(za.at[s], wa, ra, s)
        keep.append(snd.local(za.at[s, core], wa.at[rows(c, s)]))
        if pc.square:
            forward(wa, ra, pc.zfrom(dz - 1))
    if pc.square:
        forward(wa, ra, pc.zfrom(nz - 1))
    spread(pb_ref, wb, rb, z)
    for dz in range(1, nz):
        s = pc.zfrom(dz)
        arrived(zb.at[s], rzb.at[dz])
        spread(zb.at[s], wb, rb, s)
        keep.append(snd.local(zb.at[s, core], wb.at[rows(c, s)]))
    gall[z, core] = g_ref[...]
    for dz in range(1, nz):
        snd.start(g_ref, gall.at[z, core], rxm.at[dz], (c, pc.zto(dz)))
    snd.start(g_ref, gall.at[z, core], rxf.at[0], (pc.sib, z))

    hbuf[core] = h_ref[...]
    arrived(hbuf.at[1 - core], rmisc.at[0])
    for cp in keep:
        cp.wait()
    settle(wa, ra)
    extra = wa[:, kw:]
    ga = gain_row(extra, 8)
    gm = gain_row(extra, 9)
    for k in range(2):
        hk = hbuf[k].astype(F32)
        xa[pl.ds(k * t0, t0)] = (hk * rms(hk, width) * ga).astype(BF16)
    cos, sin = cos_ref[...], sin_ref[...]
    mine = pl.ds(pl.multiple_of(chip * t2, t2), t2)
    xav = xa[...]
    kraw = dot(xav, wa[:, qw:kw])
    kv[mine, 0:HEAD] = rope(kraw[:, :HEAD], cos, sin).astype(BF16)
    kv[mine, HEAD:] = kraw[:, HEAD:].astype(BF16)
    for k in range(1, nch):
        snd.start(kv.at[mine], kv.at[mine], rkv.at[k], (((chip + k) % nch) * 2 + core, z))
    for hd in range(heads):
        cols = slice(hd * HEAD, (hd + 1) * HEAD)
        qs[:, cols] = rope(dot(xav, wa[:, cols]), cos, sin).astype(BF16)
    if pc.square:
        for dz in range(nz):
            forward(wb, rb, pc.zfrom(dz))
    def mats(m, cc):
        per = nz * rp
        return we_out.at[m, pl.ds(pl.multiple_of(cc * per, 16), per)]

    own_e = [snd.local(we_ref.at[core, m], mats(m, c)) for m in range(3)]
    for m in range(3):
        here = mats(m, c)
        sem = re.at[m * nctx + c]
        for k in range(1, nch):
            q = (chip + k) % nch
            for half in range(2):
                snd.start(we_ref.at[half, m], here, sem, (q * 2 + half, z))
        snd.start(we_ref.at[1 - core, m], here, sem, (pc.sib, z))
    for k in range(1, nch):
        other = pl.ds(pl.multiple_of(((chip + nch - k) % nch) * t2, t2), t2)
        arrived(kv.at[other], rkv.at[k])

    keys = nch * t2
    scale = HEAD ** -0.5
    ok = lax.broadcasted_iota(jnp.int32, (t2, keys), 1) <= (
        chip * t2 + lax.broadcasted_iota(jnp.int32, (t2, keys), 0)
    )

    lane = lax.broadcasted_iota(jnp.int32, (t2, 128), 1)
    lses[...] = jnp.zeros((t2, 128), F32)

    def one_head(hd, carry):
        cols = pl.ds(pl.multiple_of(hd * HEAD, HEAD), HEAD)
        s = dot_t(qs[:, cols], kv[:, 0:HEAD]) * scale
        s = jnp.where(ok, s, -1e30)
        m = jnp.max(s, axis=-1, keepdims=True)
        e = jnp.exp(s - m)
        total = jnp.sum(e, axis=-1, keepdims=True)
        lses[...] = jnp.where(lane == hd, m + jnp.log(total), lses[...])
        p = (e * (1.0 / total)).astype(BF16)
        obs[:, cols] = dot(p, kv[:, HEAD:]).astype(BF16)
        return carry

    lax.fori_loop(0, heads, one_head, 0)
    settle(wb, rb)
    acc = dot_t(obs[...], wb[...])
    for k in range(2):
        part[k] = acc[k * t0:(k + 1) * t0]
    snd.start(part.at[1 - core], pget, rmisc.at[1], (pc.sib, z))
    arrived(pget, rmisc.at[1])
    h1 = h_ref[...].astype(F32) + part[core] + pget[...]
    h1_out[...] = h1
    xm = (h1 * rms(h1, width) * gm).astype(BF16)
    xms[...] = xm
    logits = jnp.where(mask_ref[...] > 0.0, dot(xm, extra), -1e30)
    top = jnp.max(logits, axis=-1, keepdims=True)
    e = jnp.where(mask_ref[...] > 0.0, jnp.exp(logits - top), 0.0)
    gts[...] = e / jnp.sum(e, axis=-1, keepdims=True)
    for dz in range(1, nz):
        to = (c, pc.zto(dz))
        snd.start(xms, xmall.at[z, core], rxm.at[nz + dz], to)
        snd.start(gts, gtall.at[z, core], rxm.at[2 * nz + dz], to)
    snd.start(xms, xmall.at[z, core], rxf.at[nz], (pc.sib, z))
    snd.start(gts, gtall.at[z, core], rxf.at[2 * nz], (pc.sib, z))
    xmall[z, core] = xm
    gtall[z, core] = gts[...]
    outs = [
        snd.local(wa, wa_out), snd.local(wb, wb_out), snd.local(kv, kv_out), snd.local(qs, q_out),
        snd.local(lses, lse_out), snd.local(obs, ob_out), snd.local(xa, xa_out),
    ]
    for dz in range(1, nz):
        s = pc.zfrom(dz)
        for i, buf in enumerate((gall, xmall, gtall)):
            here = buf.at[s, core]
            arrived(here, rxm.at[i * nz + dz])
            snd.start(here, here, rxf.at[i * nz + dz], (pc.sib, z))
    for dz in range(nz):
        s = pc.zfrom(dz)
        for i, buf in enumerate((gall, xmall, gtall)):
            arrived(buf.at[s, 1 - core], rxf.at[i * nz + dz])
    outs += [snd.local(xmall, xm_out), snd.local(gall, g_out), snd.local(gtall, gt_out)]
    for m in range(3):
        for k in range(1, nctx):
            cc = (c + k) % nctx
            arrived(mats(m, cc), re.at[m * nctx + cc])
    for cp in outs + own_e:
        cp.wait()
    snd.drain()


def attend_call(cfg, h, g, mask, cos, sin, pa, pb, we):
    nctx, nz, width, rp, t0, heads, fc = cfg
    nch, t2, dp = nctx // 2, 2 * t0, nctx * nz * rp
    ca, cb = pa.shape[2], pb.shape[2]
    keys = nch * t2
    vm = pl.BlockSpec(memory_space=pltpu.VMEM)
    hb = pl.BlockSpec(memory_space=pltpu.HBM)
    sds = jax.ShapeDtypeStruct
    nsend = 4 * nz + 2 * nz * (2 * nctx) + 3 * nctx + 8 * nz + 40 + nch
    dma = pltpu.SemaphoreType.DMA
    return pl.pallas_call(
        functools.partial(attend_kernel, cfg),
        out_shape=(
            sds((dp, ca), BF16), sds((dp, cb), BF16), sds((3, dp, fc), BF16),
            sds((t2, heads * HEAD), BF16), sds((keys, 2 * HEAD), BF16), sds((t2, 128), F32),
            sds((t2, heads * HEAD), BF16), sds((t2, dp), BF16), sds((t0, dp), F32),
            sds((nz, 2, t0, dp), BF16), sds((nz, 2, t0, dp), BF16), sds((nz, 2, t0, 128), F32),
        ),
        in_specs=[vm, vm, vm, vm, vm, vm, vm, hb],
        out_specs=(hb, hb, hb, hb, hb, hb, hb, hb, vm, hb, hb, hb),
        scratch_shapes=[
            pltpu.VMEM((dp, ca), BF16), pltpu.VMEM((dp, cb), BF16),
            pltpu.VMEM((nz, 2, rp, ca), BF16), pltpu.VMEM((nz, 2, rp, cb), BF16),
            pltpu.VMEM((2, t0, dp), BF16), pltpu.VMEM((t2, dp), BF16),
            pltpu.VMEM((t2, heads * HEAD), BF16), pltpu.VMEM((keys, 2 * HEAD), BF16),
            pltpu.VMEM((t2, heads * HEAD), BF16),
            pltpu.VMEM((2, t0, dp), F32), pltpu.VMEM((t0, dp), F32),
            pltpu.VMEM((t2, 128), F32), pltpu.VMEM((t0, dp), BF16), pltpu.VMEM((t0, 128), F32),
            pltpu.VMEM((nz, 2, t0, dp), BF16), pltpu.VMEM((nz, 2, t0, dp), BF16),
            pltpu.VMEM((nz, 2, t0, 128), F32),
            dma((nsend,)), dma((nctx * nz,)), dma((nctx * nz,)), dma((3 * nctx,)),
            dma((nz,)), dma((nz,)), dma((2,)), dma((nch,)), dma((3 * nz,)), dma((3 * nz,)),
        ],
        compiler_params=pltpu.CompilerParams(
            collective_id=0, has_side_effects=True, vmem_limit_bytes=60 * 2**20
        ),
        name="attend",
    )(h, g, mask, cos, sin, pa, pb, we)


def prepare(hidden, routes, cot, na, wq, wk, wv, wo, nm, wr, wg, wu, wd):
    nctx, nz = lax.axis_size("ctx"), lax.axis_size("wsh")
    t0, width = hidden.shape[1], hidden.shape[2]
    r = wq.shape[1]
    rp = -(-r // 16) * 16
    ndev = nctx * nz
    eloc, ff = wg.shape[2], wg.shape[3]
    half = wq.shape[2] // 2
    heads = half // HEAD
    fc = eloc * ff // 2

    def pad_features(x):
        if rp == r:
            return x
        x = x.reshape(x.shape[0], ndev, r)
        return jnp.pad(x, ((0, 0), (0, 0), (0, rp - r))).reshape(x.shape[0], ndev * rp)

    def pad_rows(x):
        return jnp.pad(x, ((0, rp - r), (0, 0))) if rp != r else x

    def expert(w):
        w = w.reshape(nz * r, eloc * ff)
        if rp != r:
            w = jnp.pad(w.reshape(nz, r, -1), ((0, 0), (0, rp - r), (0, 0))).reshape(nz * rp, -1)
        return jnp.stack([w[:, :fc], w[:, fc:]])

    h = pad_features(hidden[0])
    g = pad_features(cot[0].astype(BF16))
    experts = wr.shape[2]
    extra = jnp.concatenate(
        [wr[0], na[0][:, None], nm[0][:, None], jnp.zeros((r, 128 - experts - 2), BF16)], axis=1
    )
    pa = jnp.stack([
        pad_rows(jnp.concatenate([
            wq[0][:, k * half:(k + 1) * half], wk[0][:, k * HEAD:(k + 1) * HEAD],
            wv[0][:, k * HEAD:(k + 1) * HEAD], extra], axis=1))
        for k in range(2)])
    pb = jnp.stack([pad_rows(wo[0][:, :half]), pad_rows(wo[0][:, half:])])
    we = jnp.stack([expert(wg[0]), expert(wu[0]), expert(wd[0])], axis=1)
    lanes = jnp.arange(128, dtype=jnp.int32)
    mask = jnp.max((routes[0, 0][:, :, None] == lanes[None, None, :]).astype(F32), axis=1)
    chip = lax.axis_index("ctx") // 2
    pos = chip * 2 * t0 + jnp.arange(2 * t0, dtype=jnp.int32)
    freq = BASE ** (-jnp.arange(HEAD // 2, dtype=F32) * 2.0 / HEAD)
    ang = pos.astype(F32)[:, None] * freq[None, :]
    cos, sin = jnp.cos(ang), jnp.sin(ang)
    cosf = jnp.concatenate([cos, cos], axis=1)
    sinf = jnp.concatenate([-sin, sin], axis=1)
    cfg = (nctx, nz, width, rp, t0, heads, fc)
    return cfg, h, g, mask, cosf, sinf, pa, pb, we

class Reduce:
    def __init__(self, pc, snd, slab, first, fx, fy, sems):
        self.pc, self.snd, self.slab = pc, snd, slab
        self.first, self.fx, self.fy, self.sems = first, fx, fy, sems
        self.x, self.y, self.d = pc.xchip(), pc.ychip(), 3 - pc.chip

    def to(self, chip):
        return (chip * 2 + self.pc.core, self.pc.z)

    def diagonal(self):
        self.snd.start(self.slab(self.d, 0), self.first.at[0], self.sems.at[0], self.to(self.x))
        self.snd.start(self.slab(self.d, 1), self.first.at[1], self.sems.at[1], self.to(self.y))

    def straight_x(self):
        self.snd.start(self.slab(self.x, 0), self.fx.at[0], self.sems.at[2], self.to(self.x))

    def straight_y(self):
        self.snd.start(self.slab(self.y, 1), self.fy.at[1], self.sems.at[5], self.to(self.y))

    def merge(self, add):
        arrived(self.first.at[0], self.sems.at[0])
        add(self.slab(self.y, 0), self.first.at[0])
        self.snd.start(self.slab(self.y, 0), self.fy.at[0], self.sems.at[4], self.to(self.y))
        arrived(self.first.at[1], self.sems.at[1])
        add(self.slab(self.x, 1), self.first.at[1])
        self.snd.start(self.slab(self.x, 1), self.fx.at[1], self.sems.at[3], self.to(self.x))

    def wait(self):
        for w in range(2):
            arrived(self.fx.at[w], self.sems.at[2 + w])
            arrived(self.fy.at[w], self.sems.at[4 + w])


def add_into(dst, src):
    dst[...] = (dst[...].astype(F32) + src[...].astype(F32)).astype(BF16)


def back_kernel(
    cfg,
    wa_in, wb_in, we_in, q_in, kv_in, lse_in, ob_in, xa_in, h1_in, xm_in, g_in, gt_in,
    h_ref, cot_ref, cos_ref, sin_ref,
    out_ref, ig_ref, eg_out, da_out, db_out, efirst, efx, efy,
    wa, wb, we, qs, kv, lses, obs, xa, h1s, xm, gr, gts,
    ggu, ap, keep, sibs, sibr, zr, okeep, ozr, kgg, sgg, rgg, zgg,
    gat, gkv, gkvb, gkvr, graw, part, pget, exts,
    esibr,
    afirst, afx, afy, bfirst, bfx, bfy, zra, zrb, fa, fb, fra, frb, rowp,
    ssem, lsem, sib_s, sib_r, z_s, z_r, osib_s, osib_r, oz_s, oz_r, rmisc, esem, asem, bsem,
    rkv, rza, rzb,
):
    nctx, nz, width, rp, t0, heads, fc = cfg
    pc = Place(nctx, nz)
    nch = pc.nch
    t2 = 2 * t0
    qw = heads * HEAD
    kw = qw + 2 * HEAD
    dp = wa.shape[0]
    core, z, c, chip = pc.core, pc.z, pc.c, pc.chip
    per = nz * rp
    snd = Sends(ssem, ssem.shape[0])
    loads = Sends(lsem, lsem.shape[0])
    sib = (pc.sib, z)

    def slab_rows(q, w):
        return pl.ds(pl.multiple_of((q * 2 + w) * per, 16), per)

    l_we = [loads.local(we_in.at[m], we.at[m]) for m in range(3)]
    l_xm = loads.local(xm_in, xm)
    l_gr = loads.local(g_in, gr)
    l_gt = loads.local(gt_in, gts)
    later = [
        loads.local(a, b)
        for a, b in (
            (wb_in, wb), (h1_in, h1s), (wa_in, wa), (ob_in, obs), (q_in, qs), (kv_in, kv),
            (lse_in, lses), (xa_in, xa),
        )
    ]
    greet(pc)
    for cp in l_we + [l_xm, l_gr, l_gt]:
        cp.wait()

    eloc = cfg_eloc(cfg)
    mine_e = z * eloc + (core * eloc) // 2
    lane = lax.broadcasted_iota(jnp.int32, (t2, 128), 1)
    mine0 = pl.ds(pl.multiple_of(core * t0, t0), t0)
    sib0 = pl.ds(pl.multiple_of((1 - core) * t0, t0), t0)

    def zof(i):
        return (z + 1 + i) % nz

    def blk(i):
        return pl.ds(pl.multiple_of(zof(i) * t2, t2), t2)

    def copy_to_sib(src, dst, ss, rs):
        return pltpu.make_async_remote_copy(
            src_ref=src, dst_ref=dst, send_sem=ss, recv_sem=rs, device_id=sib, device_id_type=MESH
        )

    def copy_to_z(i, src, dst, ss, rs):
        return pltpu.make_async_remote_copy(
            src_ref=src, dst_ref=dst, send_sem=ss, recv_sem=rs, device_id=(c, zof(i)),
            device_id_type=MESH,
        )

    def g_copies(i):
        return (
            copy_to_sib(sibs.at[i], sibr.at[i], sib_s.at[i], sib_r.at[i]),
            copy_to_sib(sgg.at[i], rgg.at[i], sib_s.at[nz + i], sib_r.at[nz + i]),
        )

    def gz_copies(i):
        return (
            copy_to_z(i, keep.at[i], zr.at[i], z_s.at[i], z_r.at[i]),
            copy_to_z(i, kgg.at[i], zgg.at[i], z_s.at[nz + i], z_r.at[nz + i]),
        )

    def g_settle(i):
        for cp in g_copies(i):
            cp.wait()
        keep[i] = (keep[i].astype(F32) + sibr[i].astype(F32)).astype(BF16)
        kgg[i] = kgg[i] + rgg[i]

    def rows_back(i, carry):
        x = xm[blk(i)]
        g = gr[blk(i)]
        gate = jnp.sum(jnp.where(lane == mine_e, gts[blk(i)], 0.0), axis=1, keepdims=True)
        pre = dot(x, we[0])
        up = dot(x, we[1])
        ga0 = dot(g, we[2])
        sg = 1.0 / (1.0 + jnp.exp(-pre))
        silu = pre * sg
        act = silu * up
        ggc = jnp.sum(act * ga0, axis=1, keepdims=True)
        ggl = jnp.where(lane == mine_e, ggc, 0.0)
        gact = gate * ga0
        gg = (gact * up * sg * (1.0 + pre * (1.0 - sg))).astype(BF16)
        gu = (gact * silu).astype(BF16)
        ap[blk(i)] = (gate * act).astype(BF16)
        ggu[blk(i), 0:fc] = gg
        ggu[blk(i), fc:] = gu
        gb = (dot_t(gg, we[0]) + dot_t(gu, we[1])).astype(BF16)
        part[0:t0] = gb[:t0].astype(F32)
        part[t0:] = gb[t0:].astype(F32)
        keep[i] = part[mine0].astype(BF16)
        sibs[i] = part[sib0].astype(BF16)
        rowp[...] = ggl
        kgg[i] = rowp[mine0]
        sgg[i] = rowp[sib0]
        for cp in g_copies(i):
            cp.start()

        @pl.when(i > 0)
        def _():
            g_settle(i - 1)
            for cp in gz_copies(i - 1):
                cp.start()

        return carry

    lax.fori_loop(0, nz, rows_back, 0)
    g_settle(nz - 1)

    def o_copy(i):
        return copy_to_sib(sibs.at[i], sibr.at[i], osib_s.at[i], osib_r.at[i])

    def oz_copy(i):
        return copy_to_z(i, okeep.at[i], ozr.at[i], oz_s.at[i], oz_r.at[i])

    def o_settle(i):
        o_copy(i).wait()
        okeep[i] = (okeep[i].astype(F32) + sibr[i].astype(F32)).astype(BF16)

    def rows_out(i, carry):
        part[...] = dot_t(ap[blk(i)], we[2])
        okeep[i] = part[mine0].astype(BF16)
        sibs[i] = part[sib0].astype(BF16)
        o_copy(i).start()

        @pl.when(i > 0)
        def _():
            o_settle(i - 1)
            oz_copy(i - 1).start()

        return carry

    lax.fori_loop(0, nz, rows_out, 0)
    o_settle(nz - 1)

    ers = Reduce(pc, snd, lambda q, w: we.at[:, slab_rows(q, w)], efirst, efx, efy, esem)

    for n, q in enumerate((ers.d, ers.x, ers.y, chip)):
        cols = pl.ds(pl.multiple_of(q * 2 * per, 128), 2 * per)
        gw = t_dot(xm[:, cols], ggu[...])
        we[0, cols] = gw[:, :fc].astype(BF16)
        we[1, cols] = gw[:, fc:].astype(BF16)
        we[2, cols] = t_dot(gr[:, cols], ap[...]).astype(BF16)
        if n == 0:
            ers.diagonal()
        elif n == 1:
            ers.straight_x()
        elif n == 2:
            ers.straight_y()

    for cp in later:
        cp.wait()
    gsum = keep[nz - 1].astype(F32)
    ggs = kgg[nz - 1]
    for i in range(nz - 1):
        arrived(zr.at[i], z_r.at[i])
        arrived(zgg.at[i], z_r.at[nz + i])
        gsum = gsum + zr[i].astype(F32)
        ggs = ggs + zgg[i]
    own = pl.ds(pl.multiple_of(z * t2 + core * t0, t0), t0)
    gate = gts[own]
    glog = (gate * (ggs - jnp.sum(gate * ggs, axis=1, keepdims=True))).astype(BF16)
    extra = wa[:, kw:]
    gain_a = gain_row(extra, 8)
    gain_m = gain_row(extra, 9)
    gxm = gsum + dot_t(glog, extra)
    h1 = h1s[...]
    r = rms(h1, width)
    n = h1 * r
    gy = gxm * gain_m
    g1 = cot_ref[...] + r * (gy - n * (jnp.sum(gy * n, axis=1, keepdims=True) * (1.0 / width)))
    lane0 = lax.broadcasted_iota(jnp.int32, (t0, 128), 1)
    ext = t_dot(xm[own], glog) + t_dot((gxm * n).astype(BF16), (lane0 == 9).astype(BF16))
    exts[...] = ext
    ig_ref[...] = g1
    gat[mine0] = g1.astype(BF16)
    snd.start(gat.at[mine0], gat.at[mine0], rmisc.at[0], sib)
    arrived(gat.at[sib0], rmisc.at[0])
    gav = gat[...]
    go = dot(gav, wb[...]).astype(BF16)
    brs = Reduce(pc, snd, lambda q, w: wb.at[slab_rows(q, w)], bfirst, bfx, bfy, bsem)

    def out_grads(k, carry):
        cols = pl.ds(pl.multiple_of(k * 2 * per, 128), 2 * per)
        wb[cols] = t_dot(gat[:, cols], obs[...]).astype(BF16)
        return carry

    lax.fori_loop(0, nch, out_grads, 0)
    obs[...] = go

    keys = nch * t2
    scale = HEAD ** -0.5
    ok = lax.broadcasted_iota(jnp.int32, (t2, keys), 1) <= (
        chip * t2 + lax.broadcasted_iota(jnp.int32, (t2, keys), 0)
    )
    cos, sin = cos_ref[...], sin_ref[...]
    gkv[...] = jnp.zeros(gkv.shape, F32)

    def one_head(hd, carry):
        cols = pl.ds(pl.multiple_of(hd * HEAD, HEAD), HEAD)
        s = dot_t(qs[:, cols], kv[:, 0:HEAD]) * scale
        pe = jnp.where(ok, jnp.exp(s - jnp.sum(jnp.where(lane == hd, lses[...], 0.0), axis=1, keepdims=True)), 0.0)
        gp = dot_t(obs[:, cols], kv[:, HEAD:])
        delta = jnp.sum(pe * gp, axis=-1, keepdims=True)
        gs = (pe * (gp - delta)).astype(BF16)
        gq = dot(gs, kv[:, 0:HEAD]) * scale
        graw[:, cols] = rope(gq, cos, -sin).astype(BF16)
        gkv[:, 0:HEAD] += t_dot(gs, qs[:, cols])
        gkv[:, HEAD:] += t_dot(pe.astype(BF16), obs[:, cols])
        return carry

    lax.fori_loop(0, heads, one_head, 0)
    def fetch(src, room, col):
        spot = [
            room.at[pl.ds(m * per, per), pl.ds(col * fc, fc)] for m in range(3)
        ]
        cps = [loads.local(src.at[m], spot[m]) for m in range(3)]
        return spot, cps

    def add_mats(dst, src):
        spot, cps = fetch(src, gr, 0)
        for cp in cps:
            cp.wait()
        for m in range(3):
            dst[m] = (dst[m].astype(F32) + spot[m][...].astype(F32)).astype(BF16)

    ers.merge(add_mats)
    mine = pl.ds(pl.multiple_of(chip * t2, t2), t2)
    gkvb[...] = gkv[...].astype(BF16)
    for k in range(1, nch):
        q = (chip + k) % nch
        snd.start(
            gkvb.at[pl.ds(pl.multiple_of(q * t2, t2), t2)], gkvr.at[k - 1], rkv.at[k],
            (q * 2 + core, z),
        )
    brs.diagonal()
    brs.straight_x()
    brs.straight_y()
    gk = gkv[mine]
    for k in range(1, nch):
        arrived(gkvr.at[k - 1], rkv.at[k])
        gk = gk + gkvr[k - 1].astype(F32)
    graw[:, qw:qw + HEAD] = rope(gk[:, :HEAD] * scale, cos, -sin).astype(BF16)
    graw[:, qw + HEAD:] = gk[:, HEAD:].astype(BF16)
    part[...] = dot_t(graw[...], wa[:, :kw])
    pget_src = part.at[sib0]
    snd.start(pget_src, pget, rmisc.at[1], sib)
    ars = Reduce(pc, snd, lambda q, w: wa.at[slab_rows(q, w)], afirst, afx, afy, asem)

    def in_grads(k, carry):
        cols = pl.ds(pl.multiple_of(k * 2 * per, 128), 2 * per)
        wa[cols, 0:kw] = t_dot(xa[:, cols], graw[...]).astype(BF16)
        return carry

    lax.fori_loop(0, nch, in_grads, 0)
    arrived(pget, rmisc.at[1])
    gxa = part[mine0] + pget[...]
    h = h_ref[...].astype(F32)
    r = rms(h, width)
    n = h * r
    gy = gxa * gain_a
    ig_ref[...] += r * (gy - n * (jnp.sum(gy * n, axis=1, keepdims=True) * (1.0 / width)))
    wa[:, kw:] = (
        exts[...] + t_dot((gxa * n).astype(BF16), (lane0 == 8).astype(BF16))
    ).astype(BF16)
    ars.diagonal()
    ars.straight_x()
    ars.straight_y()
    brs.merge(add_into)

    osum = okeep[nz - 1].astype(F32) + h1s[...]
    for i in range(nz - 1):
        arrived(ozr.at[i], oz_r.at[i])
        osum = osum + ozr[i].astype(F32)
    out_ref[...] = osum

    ers.wait()
    got = [
        fetch(src.at[w], room, w) for src, room in ((efx, gr), (efy, xm)) for w in range(2)
    ]
    for _, cps in got:
        for cp in cps:
            cp.wait()
    for w in range(2):
        for m in range(3):
            tot = we[m, slab_rows(chip, w)].astype(F32)
            tot = tot + got[w][0][m][...].astype(F32) + got[2 + w][0][m][...].astype(F32)
            we[m, slab_rows(chip, w)] = tot.astype(BF16)
    snd.start(ers.slab(chip, 1 - core), esibr, rmisc.at[2], sib)
    e_own = loads.local(ers.slab(chip, core), eg_out.at[core])

    ars.merge(add_into)
    zs = []
    def own_piece(q, w):
        return pl.ds(pl.multiple_of((c - core + w) * per + q * rp, 16), rp)

    for rs, buf, fx, fy, zrecv, rz in (
        (brs, wb, bfx, bfy, zrb, rzb), (ars, wa, afx, afy, zra, rza)
    ):
        rs.wait()
        for w in range(2):
            buf[slab_rows(chip, w)] = (
                buf[slab_rows(chip, w)].astype(F32) + fx[w].astype(F32) + fy[w].astype(F32)
            ).astype(BF16)
        for dz in range(1, nz):
            q = pc.zto(dz)
            for w in range(2):
                snd.start(
                    buf.at[own_piece(q, w)], zrecv.at[dz - 1, w], rz.at[2 * dz + w], (c, q)
                )
    arrived(esibr, rmisc.at[2])
    e_sib = loads.local(esibr, eg_out.at[1 - core])
    for k, (buf, zrecv, rz, fin, get) in enumerate(
        ((wb, zrb, rzb, fb, frb), (wa, zra, rza, fa, fra))
    ):
        for w in range(2):
            tot = buf[own_piece(z, w)].astype(F32)
            for dz in range(1, nz):
                arrived(zrecv.at[dz - 1, w], rz.at[2 * dz + w])
                tot = tot + zrecv[dz - 1, w].astype(F32)
            fin[w] = tot
        snd.start(fin.at[1 - core], get, rmisc.at[3 + k], sib)
    arrived(frb, rmisc.at[3])
    db_out[core] = fb[core]
    db_out[1 - core] = frb[...]
    arrived(fra, rmisc.at[4])
    da_out[core] = fa[core]
    da_out[1 - core] = fra[...]
    e_own.wait()
    e_sib.wait()
    for i in range(nz - 1):
        for cp in gz_copies(i):
            cp.wait_send()
        oz_copy(i).wait_send()
    snd.drain()


def cfg_eloc(cfg):
    return 2


def back_call(cfg, wa, wb, we, q, kv, lse, ob, xa, h1, xm, g, gt, h, cot, cos, sin):
    nctx, nz, width, rp, t0, heads, fc = cfg
    nch, t2, dp = nctx // 2, 2 * t0, nctx * nz * rp
    ca, cb = wa.shape[1], wb.shape[1]
    keys = nch * t2
    rows = nz * t2
    per = nz * rp
    vm = pl.BlockSpec(memory_space=pltpu.VMEM)
    hb = pl.BlockSpec(memory_space=pltpu.HBM)
    sds = jax.ShapeDtypeStruct
    dma = pltpu.SemaphoreType.DMA
    v = pltpu.VMEM
    return pl.pallas_call(
        functools.partial(back_kernel, cfg),
        out_shape=(
            sds((t0, dp), F32), sds((t0, dp), F32), sds((2, 3, per, fc), BF16),
            sds((2, rp, ca), F32), sds((2, rp, cb), F32),
        ) + (sds((2, 3, per, fc), BF16),) * 3,
        in_specs=[hb] * 12 + [vm] * 4,
        out_specs=(vm, vm, hb, vm, vm, hb, hb, hb),
        scratch_shapes=[
            v((dp, ca), BF16), v((dp, cb), BF16), v((3, dp, fc), BF16),
            v((t2, heads * HEAD), BF16), v((keys, 2 * HEAD), BF16), v((t2, 128), F32),
            v((t2, heads * HEAD), BF16), v((t2, dp), BF16), v((t0, dp), F32),
            v((rows, dp), BF16), v((rows, dp), BF16), v((rows, 128), F32),
            v((rows, 2 * fc), BF16), v((rows, fc), BF16),
            v((nz, t0, dp), BF16), v((nz, t0, dp), BF16), v((nz, t0, dp), BF16),
            v((nz - 1, t0, dp), BF16),
            v((nz, t0, dp), BF16), v((nz - 1, t0, dp), BF16),
            v((nz, t0, 128), F32), v((nz, t0, 128), F32), v((nz, t0, 128), F32),
            v((nz - 1, t0, 128), F32),
            v((t2, dp), BF16), v((keys, 2 * HEAD), F32), v((keys, 2 * HEAD), BF16),
            v((nch - 1, t2, 2 * HEAD), BF16), v((t2, ca - 128), BF16),
            v((t2, dp), F32), v((t0, dp), F32), v((dp, 128), F32),
            v((3, per, fc), BF16),
            v((2, per, ca), BF16), v((2, per, ca), BF16), v((2, per, ca), BF16),
            v((2, per, cb), BF16), v((2, per, cb), BF16), v((2, per, cb), BF16),
            v((nz - 1, 2, rp, ca), BF16), v((nz - 1, 2, rp, cb), BF16),
            v((2, rp, ca), F32), v((2, rp, cb), F32), v((rp, ca), F32), v((rp, cb), F32),
            v((t2, 128), F32),
            dma((60,)), dma((40,)), dma((2 * nz,)), dma((2 * nz,)), dma((2 * nz,)), dma((2 * nz,)),
            dma((nz,)), dma((nz,)), dma((nz,)), dma((nz,)), dma((5,)), dma((6,)), dma((6,)),
            dma((6,)), dma((nch,)), dma((2 * nz,)), dma((2 * nz,)),
        ],
        compiler_params=pltpu.CompilerParams(
            collective_id=1, has_side_effects=True, vmem_limit_bytes=64 * 2**20
        ),
        name="back",
    )(wa, wb, we, q, kv, lse, ob, xa, h1, xm, g, gt, h, cot, cos, sin)


def body(hidden, routes, cot, na, wq, wk, wv, wo, nm, wr, wg, wu, wd):
    cfg, h, g, mask, cos, sin, pa, pb, we = prepare(
        hidden, routes, cot, na, wq, wk, wv, wo, nm, wr, wg, wu, wd
    )
    nctx, nz, width, rp, t0, heads, fc = cfg
    t2, dp = 2 * t0, nctx * nz * rp
    r = attend_call(cfg, h, g, mask, cos, sin, pa, pb, we)
    wa, wb, wf, q, kv, lse, ob, xa, h1, xm, gall, gt = r
    xm = xm.reshape(nz * t2, dp)
    gall = gall.reshape(nz * t2, dp)
    gt = gt.reshape(nz * t2, 128)
    out, ig, eg, da, db, *_ = back_call(
        cfg, wa, wb, wf, q, kv, lse, ob, xa, h1, xm, gall, gt, h, cot[0], cos, sin
    )
    qw = heads * HEAD
    kw = qw + 2 * HEAD
    ext = da[0, :, kw:] + da[1, :, kw:]
    both = lambda x, lo, hi: jnp.concatenate([x[0, :, lo:hi], x[1, :, lo:hi]], axis=1)[None]
    eg = jnp.transpose(eg.astype(F32), (1, 2, 0, 3))
    experts = wr.shape[2]
    return (
        out[None], ig[None], ext[:, 8][None], both(da, 0, qw), both(da, qw, qw + HEAD),
        both(da, qw + HEAD, kw), both(db, 0, qw), ext[:, 9][None], ext[:, :experts][None],
        eg[0][None], eg[1][None], eg[2][None],
    )


def shifted(value, axis, steps):
    count = lax.axis_size(axis)
    pairs = [(source, (source + steps) % count) for source in range(count)]
    return lax.ppermute(value, axis, pairs)


def normalize(hidden_state, gain):
    return (
        hidden_state
        * lax.rsqrt(jnp.mean(hidden_state * hidden_state, axis=-1, keepdims=True) + NORM_EPSILON)
        * gain
    )


def rotary(token_positions, head_size):
    half_size = head_size // 2
    frequency = ROTARY_BASE ** (-jnp.arange(half_size, dtype=jnp.float32) * 2.0 / head_size)
    angles = token_positions.astype(jnp.float32)[:, None] * frequency[None, :]
    return (jnp.cos(angles)[:, None, :], jnp.sin(angles)[:, None, :])


def apply_rotary(values_in, cosine, sine_rows, direction):
    half_size = values_in.shape[-1] // 2
    first_half = values_in[..., :half_size]
    second = values_in[..., half_size:]
    return jnp.concatenate(
        [
            first_half * cosine - direction * second * sine_rows,
            second * cosine + direction * first_half * sine_rows,
        ],
        axis=-1,
    )


def slot_targets(picks_in, matches):
    flat_matches = matches.reshape(-1, matches.shape[-1]).astype(jnp.int32)
    earlier = jnp.cumsum(flat_matches, axis=0) - flat_matches
    return picks_in.reshape(-1) * CAP + jnp.sum(earlier * flat_matches, axis=1)


def score_rows(query_low, key_rows, token_positions):
    total_rows = query_low.shape[0]
    head_size = query_low.shape[2]
    grouped_heads = query_low.reshape(total_rows, key_rows.shape[1], -1, head_size)
    scores = jnp.einsum(
        "qhgd,khd->hgqk", grouped_heads, key_rows, preferred_element_type=jnp.float32
    ) * head_size ** (-0.5)
    allowed = jnp.arange(key_rows.shape[0], dtype=jnp.int32)[None, :] <= token_positions[:, None]
    return (grouped_heads, jnp.where(allowed[None, None], scores, -1e30))


def attend(query_low, key_rows, value_rows, token_positions):
    grouped_heads, scores = score_rows(query_low, key_rows, token_positions)
    highest = jnp.max(scores, axis=-1, keepdims=True)
    log_total = highest + jnp.log(jnp.sum(jnp.exp(scores - highest), axis=-1, keepdims=True))
    weights = jnp.exp(scores - log_total).astype(jnp.bfloat16)
    attended = jnp.einsum("hgqk,khd->qhgd", weights, value_rows, preferred_element_type=jnp.float32)
    return (attended.reshape(query_low.shape[0], -1), log_total)


def attend_grad(query_low, key_rows, value_rows, token_positions, log_total, grad_mixed):
    grouped_heads, scores = score_rows(query_low, key_rows, token_positions)
    score_scale = query_low.shape[-1] ** (-0.5)
    softmax_rows = jnp.exp(scores - log_total)
    weights = softmax_rows.astype(jnp.bfloat16)
    grad_grouped = grad_mixed.reshape(grouped_heads.shape)
    grad_weights = jnp.einsum(
        "qhgd,khd->hgqk", grad_grouped, value_rows, preferred_element_type=jnp.float32
    )
    grad_values = jnp.einsum(
        "hgqk,qhgd->khd", weights, grad_grouped, preferred_element_type=jnp.float32
    )
    row_inner = jnp.sum(softmax_rows * grad_weights, axis=-1, keepdims=True)
    grad_scores = (softmax_rows * (grad_weights - row_inner)).astype(jnp.bfloat16)
    grad_query = (
        jnp.einsum("hgqk,khd->qhgd", grad_scores, key_rows, preferred_element_type=jnp.float32)
        * score_scale
    )
    grad_keys = (
        jnp.einsum("hgqk,qhgd->khd", grad_scores, grouped_heads, preferred_element_type=jnp.float32)
        * score_scale
    )
    return (grad_query.reshape(query_low.shape), grad_keys, grad_values)


def collect_key_grads(grad_keys, grad_values, total_rows):
    cycle_size = lax.axis_size("ctx")
    own_index = lax.axis_index("ctx")
    both_grads = jnp.stack([grad_keys, grad_values])

    def block_piece(block_index):
        return lax.dynamic_slice_in_dim(both_grads, block_index * total_rows, total_rows, 1)

    def cycle_step(step_index, carried):
        moved = shifted(carried.astype(jnp.bfloat16), "ctx", -1).astype(carried.dtype)
        block_index = (own_index + step_index) % cycle_size
        weight_now = jnp.where(step_index < cycle_size, 1.0, 0.0).astype(jnp.float32)
        return moved + weight_now * block_piece(block_index)

    collected = lax.fori_loop(1, cycle_size + 1, cycle_step, block_piece(own_index))
    return (collected[0], collected[1])


def forward_layer(hidden_state, picks_in, dense_set, expert_set):
    gain_attn, query_matrix, key_matrix, value_matrix, output_matrix, gain_moe, router_matrix = (
        dense_set
    )
    gate_w, up_w, down_w = expert_set
    total_rows, model_width = hidden_state.shape
    token_positions = lax.axis_index("ctx") * total_rows + jnp.arange(total_rows, dtype=jnp.int32)
    cosine, sine_rows = rotary(token_positions, HEAD_DIM)
    attention_normed = normalize(hidden_state, gain_attn.astype(jnp.float32)).astype(jnp.bfloat16)
    query_unrotated = jnp.dot(
        attention_normed, query_matrix, preferred_element_type=jnp.float32
    ).reshape(total_rows, QUERY_HEADS, HEAD_DIM)
    key_unrotated = jnp.dot(
        attention_normed, key_matrix, preferred_element_type=jnp.float32
    ).reshape(total_rows, KEY_VALUE_HEADS, HEAD_DIM)
    query_low = apply_rotary(query_unrotated, cosine, sine_rows, 1.0).astype(jnp.bfloat16)
    key_low = apply_rotary(key_unrotated, cosine, sine_rows, 1.0).astype(jnp.bfloat16)
    value_low = (
        jnp.dot(attention_normed, value_matrix, preferred_element_type=jnp.float32)
        .astype(jnp.bfloat16)
        .reshape(total_rows, KEY_VALUE_HEADS, HEAD_DIM)
    )
    key_rows, value_rows = (
        lax.all_gather(key_low, "ctx", axis=0, tiled=True),
        lax.all_gather(value_low, "ctx", axis=0, tiled=True),
    )
    attended, log_total = attend(query_low, key_rows, value_rows, token_positions)
    mixed_reduced = attended.astype(jnp.bfloat16)
    post_attention = hidden_state + lax.dot_general(
        mixed_reduced, output_matrix, (((1,), (1,)), ((), ())), preferred_element_type=jnp.float32
    )
    expert_normed = normalize(post_attention, gain_moe.astype(jnp.float32)).astype(jnp.bfloat16)
    router_logits = jnp.dot(expert_normed, router_matrix, preferred_element_type=jnp.float32)
    expert_count = router_logits.shape[1]
    matches = picks_in[:, :, None] == jnp.arange(expert_count, dtype=jnp.int32)[None, None, :]
    gate_weights = jax.nn.softmax(
        jnp.sum(jnp.where(matches, router_logits[:, None, :], 0.0), axis=-1), axis=-1
    )
    targets = slot_targets(picks_in, matches)
    outgoing = (
        jnp.zeros((expert_count * CAP, model_width), jnp.bfloat16)
        .at[targets]
        .set(jnp.repeat(expert_normed, TOP, axis=0))
    )
    group_count = lax.axis_size("wsh")
    local_count = gate_w.shape[1]
    arrived = lax.all_to_all(
        outgoing.reshape(group_count, local_count, CAP, model_width),
        "wsh",
        split_axis=0,
        concat_axis=0,
        tiled=True,
    )
    gate_pre = jnp.einsum("sjcd,djf->sjcf", arrived, gate_w, preferred_element_type=jnp.float32)
    up_pre = jnp.einsum("sjcd,djf->sjcf", arrived, up_w, preferred_element_type=jnp.float32)
    activations = (jax.nn.silu(gate_pre) * up_pre).astype(jnp.bfloat16)
    produced = jnp.einsum(
        "sjcf,djf->sjcd", activations, down_w, preferred_element_type=jnp.float32
    ).astype(jnp.bfloat16)
    returned = lax.all_to_all(produced, "wsh", split_axis=0, concat_axis=0, tiled=True)
    returned, arrived, gate_pre, up_pre = (returned, arrived, gate_pre, up_pre)
    picked = (
        returned.reshape(-1, model_width)[targets]
        .reshape(total_rows, TOP, model_width)
        .astype(jnp.float32)
    )
    after_moe = post_attention + jnp.sum(gate_weights[:, :, None] * picked, axis=1)
    stored = (
        hidden_state,
        attention_normed,
        query_low,
        key_low,
        value_low,
        log_total,
        mixed_reduced,
        post_attention,
        expert_normed,
        matches,
        gate_weights,
        targets,
        picked,
        arrived,
        gate_pre,
        up_pre,
    )
    return (after_moe, stored, (key_rows, value_rows))


def backward_layer(incoming, stored, dense_set, expert_set, key_rows, value_rows):
    (
        hidden_state,
        attention_normed,
        query_low,
        key_low,
        value_low,
        log_total,
        mixed_reduced,
        post_attention,
        expert_normed,
        matches,
        gate_weights,
        targets,
        picked,
        arrived,
        gate_pre,
        up_pre,
    ) = stored
    gain_attn, query_matrix, key_matrix, value_matrix, output_matrix, gain_moe, router_matrix = (
        dense_set
    )
    gate_w, up_w, down_w = expert_set
    total_rows, model_width = hidden_state.shape
    token_positions = lax.axis_index("ctx") * total_rows + jnp.arange(total_rows, dtype=jnp.int32)
    cosine, sine_rows = rotary(token_positions, HEAD_DIM)
    grad_y = (gate_weights[:, :, None] * incoming[:, None, :]).astype(jnp.bfloat16)
    grad_gates = jnp.sum(incoming[:, None, :] * picked, axis=-1)
    grad_chosen = gate_weights * (
        grad_gates - jnp.sum(gate_weights * grad_gates, axis=-1, keepdims=True)
    )
    grad_logits = jnp.sum(jnp.where(matches, grad_chosen[:, :, None], 0.0), axis=1).astype(
        jnp.bfloat16
    )
    slot_total = arrived.shape[0] * arrived.shape[1] * arrived.shape[2]
    outgoing = (
        jnp.zeros((slot_total, model_width), jnp.bfloat16)
        .at[targets]
        .set(grad_y.reshape(-1, model_width))
    )
    grad_arrived = lax.all_to_all(
        outgoing.reshape(arrived.shape), "wsh", split_axis=0, concat_axis=0, tiled=True
    )
    grad_acts = jnp.einsum(
        "sjcd,djf->sjcf", grad_arrived, down_w, preferred_element_type=jnp.float32
    )
    sigmoid_gate = jax.nn.sigmoid(gate_pre)
    silu_gate = jax.nn.silu(gate_pre)
    activations = (silu_gate * up_pre).astype(jnp.bfloat16)
    grad_gate = (
        grad_acts * up_pre * sigmoid_gate * (1.0 + gate_pre * (1.0 - sigmoid_gate))
    ).astype(jnp.bfloat16)
    grad_up = (grad_acts * silu_gate).astype(jnp.bfloat16)
    grad_rows = (
        jnp.einsum("sjcf,djf->sjcd", grad_gate, gate_w, preferred_element_type=jnp.float32)
        + jnp.einsum("sjcf,djf->sjcd", grad_up, up_w, preferred_element_type=jnp.float32)
    ).astype(jnp.bfloat16)
    grad_back = lax.all_to_all(grad_rows, "wsh", split_axis=0, concat_axis=0, tiled=True)
    expert_grads = (
        lax.psum_scatter(
            jnp.einsum(
                "sjcd,sjcf->djf", arrived, grad_gate, preferred_element_type=jnp.float32
            ).astype(jnp.bfloat16),
            "ctx",
            scatter_dimension=0,
            tiled=True,
        ).astype(jnp.float32),
        lax.psum_scatter(
            jnp.einsum(
                "sjcd,sjcf->djf", arrived, grad_up, preferred_element_type=jnp.float32
            ).astype(jnp.bfloat16),
            "ctx",
            scatter_dimension=0,
            tiled=True,
        ).astype(jnp.float32),
        lax.psum_scatter(
            jnp.einsum(
                "sjcd,sjcf->djf", grad_arrived, activations, preferred_element_type=jnp.float32
            ).astype(jnp.bfloat16),
            "ctx",
            scatter_dimension=0,
            tiled=True,
        ).astype(jnp.float32),
    )
    returned_rows = (
        grad_back.reshape(-1, model_width)[targets]
        .reshape(total_rows, TOP, model_width)
        .astype(jnp.float32)
    )
    grad_normed_moe = jnp.sum(returned_rows, axis=1) + lax.dot_general(
        grad_logits, router_matrix, (((1,), (1,)), ((), ())), preferred_element_type=jnp.float32
    )
    router_term = jnp.einsum(
        "td,te->de", expert_normed, grad_logits, preferred_element_type=jnp.float32
    )
    unused_moe, pull_moe = jax.vjp(normalize, post_attention, gain_moe.astype(jnp.float32))
    grad_after_norm, gain_moe_term = pull_moe(grad_normed_moe)
    grad_after_attn = incoming + grad_after_norm
    grad_attn = grad_after_attn.astype(jnp.bfloat16)
    out_term = jnp.einsum("td,tj->dj", grad_attn, mixed_reduced, preferred_element_type=jnp.float32)
    grad_mixed = jnp.dot(grad_attn, output_matrix, preferred_element_type=jnp.float32).astype(
        jnp.bfloat16
    )
    grad_query, grad_keys, grad_values = attend_grad(
        query_low, key_rows, value_rows, token_positions, log_total, grad_mixed
    )
    grad_key, grad_value = collect_key_grads(grad_keys, grad_values, total_rows)
    grad_query_raw = (
        apply_rotary(grad_query, cosine, sine_rows, -1.0)
        .reshape(total_rows, -1)
        .astype(jnp.bfloat16)
    )
    grad_key_raw = (
        apply_rotary(grad_key, cosine, sine_rows, -1.0).reshape(total_rows, -1).astype(jnp.bfloat16)
    )
    grad_value_raw = grad_value.reshape(total_rows, -1).astype(jnp.bfloat16)
    contract_last = (((1,), (1,)), ((), ()))
    grad_normed_attn = lax.dot_general(
        grad_query_raw, query_matrix, contract_last, preferred_element_type=jnp.float32
    )
    grad_normed_attn = grad_normed_attn + lax.dot_general(
        grad_key_raw, key_matrix, contract_last, preferred_element_type=jnp.float32
    )
    grad_normed_attn = grad_normed_attn + lax.dot_general(
        grad_value_raw, value_matrix, contract_last, preferred_element_type=jnp.float32
    )
    query_term = jnp.einsum(
        "td,tf->df", attention_normed, grad_query_raw, preferred_element_type=jnp.float32
    )
    key_term = jnp.einsum(
        "td,tf->df", attention_normed, grad_key_raw, preferred_element_type=jnp.float32
    )
    value_term = jnp.einsum(
        "td,tf->df", attention_normed, grad_value_raw, preferred_element_type=jnp.float32
    )
    unused_attn, pull_attn = jax.vjp(normalize, hidden_state, gain_attn.astype(jnp.float32))
    grad_before, gain_attn_term = pull_attn(grad_normed_attn)
    layer_grads = (
        lax.psum_scatter(gain_attn_term, ("ctx", "wsh"), scatter_dimension=0, tiled=True),
        lax.psum_scatter(query_term, ("ctx", "wsh"), scatter_dimension=0, tiled=True),
        lax.psum_scatter(key_term, ("ctx", "wsh"), scatter_dimension=0, tiled=True),
        lax.psum_scatter(value_term, ("ctx", "wsh"), scatter_dimension=0, tiled=True),
        lax.psum_scatter(out_term, ("ctx", "wsh"), scatter_dimension=0, tiled=True),
        lax.psum_scatter(gain_moe_term, ("ctx", "wsh"), scatter_dimension=0, tiled=True),
        lax.psum_scatter(router_term, ("ctx", "wsh"), scatter_dimension=0, tiled=True),
    )
    return (grad_after_attn + grad_before, layer_grads, expert_grads)


def plain_body(
    hidden_in,
    routes,
    cotangent,
    norm_attn,
    w_query,
    key_projection,
    value_projection,
    w_out,
    norm_moe,
    w_router,
    w_gate,
    w_up,
    w_down,
):
    hidden_state = hidden_in[0].astype(jnp.float32)
    layer_number = 0
    dense_set = (
        lax.all_gather(norm_attn[layer_number], ("ctx", "wsh"), axis=0, tiled=True),
        lax.all_gather(w_query[layer_number], ("ctx", "wsh"), axis=0, tiled=True),
        lax.all_gather(key_projection[layer_number], ("ctx", "wsh"), axis=0, tiled=True),
        lax.all_gather(value_projection[layer_number], ("ctx", "wsh"), axis=0, tiled=True),
        lax.all_gather(w_out[layer_number], ("ctx", "wsh"), axis=0, tiled=True),
        lax.all_gather(norm_moe[layer_number], ("ctx", "wsh"), axis=0, tiled=True),
        lax.all_gather(w_router[layer_number], ("ctx", "wsh"), axis=0, tiled=True),
    )
    expert_set = (
        lax.all_gather(w_gate[layer_number], "ctx", axis=0, tiled=True),
        lax.all_gather(w_up[layer_number], "ctx", axis=0, tiled=True),
        lax.all_gather(w_down[layer_number], "ctx", axis=0, tiled=True),
    )
    hidden_state, stored, gathered = forward_layer(
        hidden_state, routes[layer_number, 0], dense_set, expert_set
    )
    records = [(stored, None, None, None)]
    incoming = cotangent[0]
    dense_grads = []
    expert_grads = []
    layer_number = 0
    stored, dense_set, expert_set, gathered = records[layer_number]
    dense_set = (
        lax.all_gather(norm_attn[layer_number], ("ctx", "wsh"), axis=0, tiled=True),
        lax.all_gather(w_query[layer_number], ("ctx", "wsh"), axis=0, tiled=True),
        lax.all_gather(key_projection[layer_number], ("ctx", "wsh"), axis=0, tiled=True),
        lax.all_gather(value_projection[layer_number], ("ctx", "wsh"), axis=0, tiled=True),
        lax.all_gather(w_out[layer_number], ("ctx", "wsh"), axis=0, tiled=True),
        lax.all_gather(norm_moe[layer_number], ("ctx", "wsh"), axis=0, tiled=True),
        lax.all_gather(w_router[layer_number], ("ctx", "wsh"), axis=0, tiled=True),
    )
    expert_set = (
        lax.all_gather(w_gate[layer_number], "ctx", axis=0, tiled=True),
        lax.all_gather(w_up[layer_number], "ctx", axis=0, tiled=True),
        lax.all_gather(w_down[layer_number], "ctx", axis=0, tiled=True),
    )
    gathered = (
        lax.all_gather(stored[3], "ctx", axis=0, tiled=True),
        lax.all_gather(stored[4], "ctx", axis=0, tiled=True),
    )
    incoming, layer_grads, layer_expert = backward_layer(
        incoming, stored, dense_set, expert_set, gathered[0], gathered[1]
    )
    dense_grads.insert(0, layer_grads)
    expert_grads.insert(0, layer_expert)
    stacked_dense = [
        jnp.stack([grads_item[position] for grads_item in dense_grads]) for position in range(7)
    ]
    stacked_expert = [
        jnp.stack([grads_item[position] for grads_item in expert_grads]) for position in range(3)
    ]
    return (
        hidden_state[None],
        incoming[None],
        stacked_dense[0],
        stacked_dense[1],
        stacked_dense[2],
        stacked_dense[3],
        stacked_dense[4],
        stacked_dense[5],
        stacked_dense[6],
        stacked_expert[0],
        stacked_expert[1],
        stacked_expert[2],
    )


def solution(mesh):
    return jax.shard_map(
        body if mesh.shape["ctx"] == 8 and mesh.shape["wsh"] == 4 else plain_body,
        mesh=mesh,
        in_specs=(
            P("wsh", "ctx", None),
            P(None, "wsh", "ctx", None),
            P("wsh", "ctx", None),
            P(None, ("ctx", "wsh")),
            P(None, ("ctx", "wsh"), None),
            P(None, ("ctx", "wsh"), None),
            P(None, ("ctx", "wsh"), None),
            P(None, ("ctx", "wsh"), None),
            P(None, ("ctx", "wsh")),
            P(None, ("ctx", "wsh"), None),
            P(None, "ctx", "wsh", None),
            P(None, "ctx", "wsh", None),
            P(None, "ctx", "wsh", None),
        ),
        out_specs=(
            P("wsh", "ctx", None),
            P("wsh", "ctx", None),
            P(None, ("ctx", "wsh")),
            P(None, ("ctx", "wsh"), None),
            P(None, ("ctx", "wsh"), None),
            P(None, ("ctx", "wsh"), None),
            P(None, ("ctx", "wsh"), None),
            P(None, ("ctx", "wsh")),
            P(None, ("ctx", "wsh"), None),
            P(None, "ctx", "wsh", None),
            P(None, "ctx", "wsh", None),
            P(None, "ctx", "wsh", None),
        ),
        check_vma=False,
    )
```

```python
import functools
import jax
import jax.numpy as jnp
import numpy as np
from jax import lax
from jax.experimental import pallas as pl
from jax.experimental.pallas import tpu as pltpu
from jax.sharding import PartitionSpec as P

QUERY_HEADS = 12
KEY_VALUE_HEADS = 2
HEAD_DIM = 128
CAP = 128
NORM_EPSILON = 1e-06
ROTARY_BASE = 1000000.0
MESH = pl.DeviceIdType.MESH
HEAD = 128
TOP = 4
EPS = 1e-06
BASE = 1000000.0
F32 = jnp.float32
BF16 = jnp.bfloat16


def dot(a, b):
    return lax.dot_general(a, b, (((1,), (0,)), ((), ())), preferred_element_type=F32)


def dot_t(a, b):
    return lax.dot_general(a, b, (((1,), (1,)), ((), ())), preferred_element_type=F32)


def t_dot(a, b):
    return lax.dot_general(a, b, (((0,), (0,)), ((), ())), preferred_element_type=F32)


class Place:
    def __init__(self, nctx, nz):
        self.nctx, self.nz, self.nch = nctx, nz, nctx // 2
        self.c = lax.axis_index("ctx")
        self.z = lax.axis_index("wsh")
        self.chip = self.c // 2
        self.core = self.c % 2
        self.sib = self.chip * 2 + 1 - self.core
        self.square = self.nch == 4

    def xchip(self):
        return self.chip + 1 - 2 * (self.chip % 2)

    def ychip(self):
        return (self.chip + 2) % 4

    def near(self, k):
        s = 0
        for here in range(self.nz):
            order = sorted(
                (v for v in range(self.nz) if v != here), key=lambda v: (abs(v - here), v)
            )
            s = jnp.where(self.z == here, order[k - 1], s)
        return s

    def onward(self, s):
        to = jnp.where(s < self.z, self.z + 1, self.z - 1)
        return to, jnp.logical_and(to >= 0, to < self.nz)

    def zto(self, dz):
        return (self.z + dz) % self.nz

    def zfrom(self, dz):
        return (self.z + self.nz - dz) % self.nz


class Sends:
    def __init__(self, sems, count):
        self.sems, self.count, self.used, self.live = sems, count, 0, []

    def start(self, src, dst, rsem, dev, when=None):
        assert self.used < self.count
        cp = pltpu.make_async_remote_copy(
            src_ref=src,
            dst_ref=dst,
            send_sem=self.sems.at[self.used],
            recv_sem=rsem,
            device_id=dev,
            device_id_type=MESH,
        )
        if when is None:
            cp.start()
        else:
            pl.when(when)(cp.start)
        self.used += 1
        self.live.append((cp, when))

    def local(self, src, dst):
        assert self.used < self.count
        cp = pltpu.make_async_copy(src, dst, self.sems.at[self.used])
        cp.start()
        self.used += 1
        return cp

    def drain(self):
        for cp, when in self.live:
            if when is None:
                cp.wait_send()
            else:
                pl.when(when)(cp.wait_send)
        self.live = []


def arrived(ref, sem):
    pltpu.make_async_copy(ref, ref, sem).wait()


def greet(pl_, plane=True, column=True):
    bar = pltpu.get_barrier_semaphore()
    n = 0
    if plane:
        for k in range(1, pl_.nctx):
            pl.semaphore_signal(
                bar, inc=1, device_id=((pl_.c + k) % pl_.nctx, pl_.z), device_id_type=MESH
            )
            n += 1
    if column:
        for k in range(1, pl_.nz):
            pl.semaphore_signal(bar, inc=1, device_id=(pl_.c, pl_.zto(k)), device_id_type=MESH)
            n += 1
    pl.semaphore_wait(bar, n)


def rms(x, width):
    return lax.rsqrt(jnp.sum(x * x, axis=-1, keepdims=True) * (1.0 / width) + EPS)


def gain_row(extra, lane):
    pick = (lax.broadcasted_iota(jnp.int32, (16, extra.shape[1]), 1) == lane).astype(BF16)
    return dot_t(pick, extra)[0:1]


def rope(x, cos, sin):
    return x * cos + pltpu.roll(x, HEAD // 2, 1) * sin


class Reduce:
    def __init__(self, pc, snd, slab, first, fx, fy, sems):
        self.pc, self.snd, self.slab = pc, snd, slab
        self.first, self.fx, self.fy, self.sems = first, fx, fy, sems
        self.x, self.y, self.d = pc.xchip(), pc.ychip(), 3 - pc.chip

    def to(self, chip):
        return (chip * 2 + self.pc.core, self.pc.z)

    def diagonal(self):
        self.snd.start(self.slab(self.d, 0), self.first.at[0], self.sems.at[0], self.to(self.x))
        self.snd.start(self.slab(self.d, 1), self.first.at[1], self.sems.at[1], self.to(self.y))

    def straight_x(self):
        self.snd.start(self.slab(self.x, 0), self.fx.at[0], self.sems.at[2], self.to(self.x))

    def straight_y(self):
        self.snd.start(self.slab(self.y, 1), self.fy.at[1], self.sems.at[5], self.to(self.y))

    def merge(self, add):
        arrived(self.first.at[0], self.sems.at[0])
        add(self.slab(self.y, 0), self.first.at[0])
        self.snd.start(self.slab(self.y, 0), self.fy.at[0], self.sems.at[4], self.to(self.y))
        arrived(self.first.at[1], self.sems.at[1])
        add(self.slab(self.x, 1), self.first.at[1])
        self.snd.start(self.slab(self.x, 1), self.fx.at[1], self.sems.at[3], self.to(self.x))

    def wait(self):
        for w in range(2):
            arrived(self.fx.at[w], self.sems.at[2 + w])
            arrived(self.fy.at[w], self.sems.at[4 + w])


def add_into(dst, src):
    dst[...] = (dst[...].astype(F32) + src[...].astype(F32)).astype(BF16)


def layer_kernel(
    cfg,
    h_ref, routes_ref, cot_ref, wq_ref, wk_ref, wv_ref, wo_ref, ex_ref, eg_ref, eu_ref, ed_ref,
    cos_in, sin_in,
    out_ref, ig_ref, eg_out, eu_out, ed_out, gwq_out, gwk_out, gwv_out, gwo_out, ext_out,
    efirst, efx, efy, ozr,
    wa, wb, we, za, zb, hbuf, cosr, sinr,
    qs, kv, lses, obs, xa, h1s, xm, gr, gts,
    ggu, ap, keep, sibs, sibr, zr, okeep, kgg, sgg, rgg, zgg,
    gat, gkv, gkvb, gkvr, graw, part, pget, exts,
    esibr,
    bfirst, bfx, bfy, qfirst, qfx, qfy, kfirst, kfx, kfy,
    zrb, zrq, zrk, fb, fq, fk, frb, frq, frk, rowp,
    ssem, lsem, ra, rb, re, rza, rzb_, rfw, rxm, rxf,
    sib_s, sib_r, z_s, z_r, osib_s, osib_r, oz_s, oz_r, rmisc, esem, bsem,
    qsem, ksem, rkv, rkvf, rzb, rzq, rzk,
):
    nctx, nz, width, rp, t0, heads, fc, _ = cfg
    pc = Place(nctx, nz)
    nch = pc.nch
    t2 = 2 * t0
    qw = heads * HEAD
    kw = qw + 2 * HEAD
    kx = wa.shape[1] - qw
    dp = wa.shape[0]
    core, z, c, chip = pc.core, pc.z, pc.c, pc.chip
    per = nz * rp
    snd = Sends(ssem, ssem.shape[0])
    loads = Sends(lsem, lsem.shape[0])
    sib = (pc.sib, z)
    mine = pl.ds(pl.multiple_of(chip * t2, t2), t2)
    mine0 = pl.ds(pl.multiple_of(core * t0, t0), t0)
    sib0 = pl.ds(pl.multiple_of((1 - core) * t0, t0), t0)
    xs, ys, ds = pc.xchip() * 2, pc.ychip() * 2, (3 - chip) * 2
    nearest = [pc.near(k) for k in range(1, nz)]

    def rows(cc, s):
        return pl.ds(pl.multiple_of((cc * nz + s) * rp, 16), rp)

    def slot(s, k):
        return pl.ds(pl.multiple_of(s * t2 + k * t0, t0), t0)

    def slab_rows(q, w):
        return pl.ds(pl.multiple_of((q * 2 + w) * per, 16), per)

    tables = [loads.local(cos_in.at[mine], cosr), loads.local(sin_in.at[mine], sinr)]
    for k in range(2):
        za[z, k, :, 0:qw] = wq_ref[:, k * qw:(k + 1) * qw]
        za[z, k, :, qw:qw + HEAD] = wk_ref[:, k * HEAD:(k + 1) * HEAD]
        za[z, k, :, qw + HEAD:kw] = wv_ref[:, k * HEAD:(k + 1) * HEAD]
        za[z, k, :, kw:] = ex_ref[...]
        zb[z, k] = wo_ref[:, k * qw:(k + 1) * qw]
    own = slot(z, core)
    gr[own] = cot_ref[...].astype(BF16)
    hbuf[core] = h_ref[...]
    greet(pc)

    def chain_start(ref, rs):
        here = ref.at[z]
        snd.start(here, here, rs.at[z], (c, z + 1), when=z + 1 < nz)
        snd.start(here, here, rs.at[z], (c, z - 1), when=z > 0)

    def chain_step(ref, rs, s):
        here = ref.at[s]
        arrived(here, rs.at[s])
        to, on = pc.onward(s)
        snd.start(here, here, rs.at[s], (c, to), when=on)

    def spread(src, dst, rs, s):
        here = dst.at[rows(c, s)]
        sem = rs.at[c * nz + s]
        for q in (pc.xchip(), pc.ychip()):
            for k in range(2):
                snd.start(src.at[k], here, sem, (q * 2 + k, z))
        snd.start(src.at[1 - core], here, sem, sib)

    def forward(dst, rs, s):
        for source, to in ((ys, pc.xchip()), (xs + 1, pc.ychip())):
            here = dst.at[rows(source, s)]
            sem = rs.at[source * nz + s]
            arrived(here, sem)
            snd.start(here, here, sem, (to * 2 + core, z))

    def settle(dst, rs):
        for cc in (pc.sib, xs, ys + 1, ds, ds + 1):
            for s in range(nz):
                arrived(dst.at[rows(cc, s)], rs.at[cc * nz + s])

    chain_start(za, rza)
    snd.start(hbuf.at[core], hbuf.at[core], rfw.at[0], sib)
    keeps = [loads.local(za.at[z, core], wa.at[rows(c, z)])]
    spread(za.at[z], wa, ra, z)
    chain_start(zb, rzb_)
    last = z
    for s in nearest:
        chain_step(za, rza, s)
        spread(za.at[s], wa, ra, s)
        keeps.append(loads.local(za.at[s, core], wa.at[rows(c, s)]))
        forward(wa, ra, last)
        last = s
    forward(wa, ra, last)
    keeps.append(loads.local(zb.at[z, core], wb.at[rows(c, z)]))
    spread(zb.at[z], wb, rb, z)
    for s in nearest:
        chain_step(zb, rzb_, s)
        spread(zb.at[s], wb, rb, s)
        keeps.append(loads.local(zb.at[s, core], wb.at[rows(c, s)]))
    for dz in range(1, nz):
        snd.start(gr.at[own], gr.at[own], rxm.at[dz], (c, pc.zto(dz)))
    snd.start(gr.at[own], gr.at[own], rxf.at[0], sib)

    arrived(hbuf.at[1 - core], rfw.at[0])
    for cp in keeps + tables:
        cp.wait()
    settle(wa, ra)
    cos, sin = cosr[...], sinr[...]
    extra = wa[:, kw:]
    gain_a = gain_row(extra, 8)
    gain_m = gain_row(extra, 9)
    for k in range(2):
        hk = hbuf[k].astype(F32)
        xa[pl.ds(k * t0, t0)] = (hk * rms(hk, width) * gain_a).astype(BF16)
    xav = xa[...]
    kraw = dot(xav, wa[:, qw:kw])
    kv[mine, 0:HEAD] = rope(kraw[:, :HEAD], cos, sin).astype(BF16)
    kv[mine, HEAD:] = kraw[:, HEAD:].astype(BF16)
    for k in range(1, nch):
        snd.start(kv.at[mine], kv.at[mine], rkvf.at[k], (((chip + k) % nch) * 2 + core, z))
    for hd in range(heads):
        cols = slice(hd * HEAD, (hd + 1) * HEAD)
        qs[:, cols] = rope(dot(xav, wa[:, cols]), cos, sin).astype(BF16)

    def mats(m, cc):
        return we.at[m, pl.ds(pl.multiple_of(cc * per, 16), per)]

    experts_in = (eg_ref, eu_ref, ed_ref)
    own_e = [loads.local(experts_in[m].at[core], mats(m, c)) for m in range(3)]

    def expert_spread(m):
        here = mats(m, c)
        sem = re.at[m * nctx + c]
        for q in (pc.xchip(), pc.ychip()):
            for k in range(2):
                snd.start(experts_in[m].at[k], here, sem, (q * 2 + k, z))
        snd.start(experts_in[m].at[1 - core], here, sem, sib)

    expert_spread(0)
    for s in [z] + nearest:
        forward(wb, rb, s)
    expert_spread(1)
    expert_spread(2)
    for k in range(1, nch):
        other = pl.ds(pl.multiple_of(((chip + nch - k) % nch) * t2, t2), t2)
        arrived(kv.at[other], rkvf.at[k])

    keys = nch * t2
    scale = HEAD ** -0.5
    ok = lax.broadcasted_iota(jnp.int32, (t2, keys), 1) <= (
        chip * t2 + lax.broadcasted_iota(jnp.int32, (t2, keys), 0)
    )
    lane = lax.broadcasted_iota(jnp.int32, (t2, 128), 1)
    lane0 = lax.broadcasted_iota(jnp.int32, (t0, 128), 1)
    lses[...] = jnp.zeros((t2, 128), F32)

    def head_forward(hd, carry):
        cols = pl.ds(pl.multiple_of(hd * HEAD, HEAD), HEAD)
        s = dot_t(qs[:, cols], kv[:, 0:HEAD]) * scale
        s = jnp.where(ok, s, -1e30)
        m = jnp.max(s, axis=-1, keepdims=True)
        e = jnp.exp(s - m)
        total = jnp.sum(e, axis=-1, keepdims=True)
        lses[...] = jnp.where(lane == hd, m + jnp.log(total), lses[...])
        p = (e * (1.0 / total)).astype(BF16)
        obs[:, cols] = dot(p, kv[:, HEAD:]).astype(BF16)
        return carry

    lax.fori_loop(0, heads, head_forward, 0)
    settle(wb, rb)
    part[...] = dot_t(obs[...], wb[...])
    snd.start(part.at[sib0], pget, rfw.at[1], sib)
    arrived(pget, rfw.at[1])
    h1 = h_ref[...].astype(F32) + part[mine0] + pget[...]
    h1s[...] = h1
    xmv = (h1 * rms(h1, width) * gain_m).astype(BF16)
    xm[own] = xmv
    chosen = routes_ref[:, 0:1] == lane0
    for k in range(1, TOP):
        chosen = jnp.logical_or(chosen, routes_ref[:, k:k + 1] == lane0)
    logits = jnp.where(chosen, dot(xmv, extra), -1e30)
    top = jnp.max(logits, axis=-1, keepdims=True)
    e = jnp.where(chosen, jnp.exp(logits - top), 0.0)
    gts[own] = e / jnp.sum(e, axis=-1, keepdims=True)
    for i, buf in enumerate((xm, gts)):
        here = buf.at[own]
        snd.start(here, here, rxm.at[(1 + i) * nz + z], (c, z + 1), when=z + 1 < nz)
        snd.start(here, here, rxm.at[(1 + i) * nz + z], (c, z - 1), when=z > 0)
    for i, buf in enumerate((xm, gts)):
        snd.start(buf.at[own], buf.at[own], rxf.at[(1 + i) * nz + z], sib)
    for m in range(3):
        for source, to in ((ys, pc.xchip()), (xs + 1, pc.ychip())):
            here = mats(m, source)
            sem = re.at[m * nctx + source]
            arrived(here, sem)
            snd.start(here, here, sem, (to * 2 + core, z))
    for dz in range(1, nz):
        here = gr.at[slot(pc.zfrom(dz), core)]
        arrived(here, rxm.at[dz])
        snd.start(here, here, rxf.at[dz], sib)
    for s in nearest:
        to, on = pc.onward(s)
        for i, buf in enumerate((xm, gts)):
            here = buf.at[slot(s, core)]
            sem = rxm.at[(1 + i) * nz + s]
            arrived(here, sem)
            snd.start(here, here, sem, (c, to), when=on)
            snd.start(here, here, rxf.at[(1 + i) * nz + s], sib)
    for dz in range(nz):
        arrived(gr.at[slot(pc.zfrom(dz), 1 - core)], rxf.at[dz])
    for i, buf in enumerate((xm, gts)):
        for s in range(nz):
            arrived(buf.at[slot(s, 1 - core)], rxf.at[(1 + i) * nz + s])
    for m in range(3):
        for cc in (pc.sib, xs, ys + 1, ds, ds + 1):
            arrived(mats(m, cc), re.at[m * nctx + cc])
    for cp in own_e:
        cp.wait()
    snd.drain()

    eloc = cfg_experts(cfg)
    mine_e = z * eloc + (core * eloc) // 2

    def zof(i):
        return (z + 1 + i) % nz

    def blk(i):
        return pl.ds(pl.multiple_of(zof(i) * t2, t2), t2)

    def copy_to_sib(src, dst, ss, rs):
        return pltpu.make_async_remote_copy(
            src_ref=src, dst_ref=dst, send_sem=ss, recv_sem=rs, device_id=sib, device_id_type=MESH
        )

    def copy_to_z(i, src, dst, ss, rs):
        return pltpu.make_async_remote_copy(
            src_ref=src, dst_ref=dst, send_sem=ss, recv_sem=rs, device_id=(c, zof(i)),
            device_id_type=MESH,
        )

    def g_copies(i):
        return (
            copy_to_sib(sibs.at[i], sibr.at[i], sib_s.at[i], sib_r.at[i]),
            copy_to_sib(sgg.at[i], rgg.at[i], sib_s.at[nz + i], sib_r.at[nz + i]),
        )

    def gz_copies(i):
        return (
            copy_to_z(i, keep.at[i], zr.at[i], z_s.at[i], z_r.at[i]),
            copy_to_z(i, kgg.at[i], zgg.at[i], z_s.at[nz + i], z_r.at[nz + i]),
        )

    def g_settle(i):
        for cp in g_copies(i):
            cp.wait()
        keep[i] = (keep[i].astype(F32) + sibr[i].astype(F32)).astype(BF16)
        kgg[i] = kgg[i] + rgg[i]

    def rows_back(i, carry):
        x = xm[blk(i)]
        g = gr[blk(i)]
        gate = jnp.sum(jnp.where(lane == mine_e, gts[blk(i)], 0.0), axis=1, keepdims=True)
        pre = dot(x, we[0])
        up = dot(x, we[1])
        ga0 = dot(g, we[2])
        sg = 1.0 / (1.0 + jnp.exp(-pre))
        silu = pre * sg
        act = silu * up
        ggc = jnp.sum(act * ga0, axis=1, keepdims=True)
        ggl = jnp.where(lane == mine_e, ggc, 0.0)
        gact = gate * ga0
        gg = (gact * up * sg * (1.0 + pre * (1.0 - sg))).astype(BF16)
        gu = (gact * silu).astype(BF16)
        ap[blk(i)] = (gate * act).astype(BF16)
        ggu[blk(i), 0:fc] = gg
        ggu[blk(i), fc:] = gu
        gb = (dot_t(gg, we[0]) + dot_t(gu, we[1])).astype(BF16)
        part[0:t0] = gb[:t0].astype(F32)
        part[t0:] = gb[t0:].astype(F32)
        keep[i] = part[mine0].astype(BF16)
        sibs[i] = part[sib0].astype(BF16)
        rowp[...] = ggl
        kgg[i] = rowp[mine0]
        sgg[i] = rowp[sib0]
        for cp in g_copies(i):
            cp.start()

        @pl.when(i > 0)
        def _():
            g_settle(i - 1)
            for cp in gz_copies(i - 1):
                cp.start()

        return carry

    lax.fori_loop(0, nz, rows_back, 0)
    g_settle(nz - 1)

    ers = [
        Reduce(
            pc, snd, lambda q, w, m=m: we.at[m, slab_rows(q, w)], efirst.at[m], efx.at[m],
            efy.at[m], esem.at[m],
        )
        for m in range(3)
    ]
    order = (ers[0].d, ers[0].x, ers[0].y, chip)

    def expert_step(n, rs):
        for one in rs:
            (one.diagonal, one.straight_x, one.straight_y, lambda: None)[n]()

    for n, q in enumerate(order):
        cols = pl.ds(pl.multiple_of(q * 2 * per, 128), 2 * per)
        gw = t_dot(xm[:, cols], ggu[...])
        we[0, cols] = gw[:, :fc].astype(BF16)
        we[1, cols] = gw[:, fc:].astype(BF16)
        expert_step(n, ers[:2])

    def o_copy(i):
        return copy_to_sib(sibs.at[i], sibr.at[i], osib_s.at[i], osib_r.at[i])

    def oz_copy(i):
        return copy_to_z(i, okeep.at[i], ozr.at[i], oz_s.at[i], oz_r.at[i])

    def o_settle(i):
        o_copy(i).wait()
        okeep[i] = (okeep[i].astype(F32) + sibr[i].astype(F32)).astype(BF16)

    def rows_out(i, carry):
        part[...] = dot_t(ap[blk(i)], we[2])
        okeep[i] = part[mine0].astype(BF16)
        sibs[i] = part[sib0].astype(BF16)
        o_copy(i).start()

        @pl.when(i > 0)
        def _():
            o_settle(i - 1)
            oz_copy(i - 1).start()

        return carry

    lax.fori_loop(0, nz, rows_out, 0)
    o_settle(nz - 1)

    for n, q in enumerate(order):
        cols = pl.ds(pl.multiple_of(q * 2 * per, 128), 2 * per)
        we[2, cols] = t_dot(gr[:, cols], ap[...]).astype(BF16)
        expert_step(n, ers[2:])

    gsum = keep[nz - 1].astype(F32)
    ggs = kgg[nz - 1]
    for i in range(nz - 1):
        arrived(zr.at[i], z_r.at[i])
        arrived(zgg.at[i], z_r.at[nz + i])
        gsum = gsum + zr[i].astype(F32)
        ggs = ggs + zgg[i]
    gate = gts[own]
    glog = (gate * (ggs - jnp.sum(gate * ggs, axis=1, keepdims=True))).astype(BF16)
    extra = wa[:, kw:]
    gxm = gsum + dot_t(glog, extra)
    h1 = h1s[...]
    r = rms(h1, width)
    n = h1 * r
    gy = gxm * gain_m
    g1 = cot_ref[...] + r * (gy - n * (jnp.sum(gy * n, axis=1, keepdims=True) * (1.0 / width)))
    ext = t_dot(xm[own], glog) + t_dot((gxm * n).astype(BF16), (lane0 == 9).astype(BF16))
    exts[...] = ext
    ig_ref[...] = g1
    gat[mine0] = g1.astype(BF16)
    snd.start(gat.at[mine0], gat.at[mine0], rmisc.at[0], sib)
    arrived(gat.at[sib0], rmisc.at[0])
    gav = gat[...]
    go = dot(gav, wb[...]).astype(BF16)
    brs = Reduce(pc, snd, lambda q, w: wb.at[slab_rows(q, w)], bfirst, bfx, bfy, bsem)

    def out_grads(k, carry):
        cols = pl.ds(pl.multiple_of(k * 2 * per, 128), 2 * per)
        wb[cols] = t_dot(gat[:, cols], obs[...]).astype(BF16)
        return carry

    lax.fori_loop(0, nch, out_grads, 0)
    brs.diagonal()
    brs.straight_x()
    brs.straight_y()
    obs[...] = go

    cos, sin = cosr[...], sinr[...]
    gkv[...] = jnp.zeros(gkv.shape, F32)

    def one_head(hd, carry):
        cols = pl.ds(pl.multiple_of(hd * HEAD, HEAD), HEAD)
        s = dot_t(qs[:, cols], kv[:, 0:HEAD]) * scale
        pe = jnp.where(ok, jnp.exp(s - jnp.sum(jnp.where(lane == hd, lses[...], 0.0), axis=1, keepdims=True)), 0.0)
        gp = dot_t(obs[:, cols], kv[:, HEAD:])
        delta = jnp.sum(pe * gp, axis=-1, keepdims=True)
        gs = (pe * (gp - delta)).astype(BF16)
        gq = dot(gs, kv[:, 0:HEAD]) * scale
        graw[:, cols] = rope(gq, cos, -sin).astype(BF16)
        gkv[:, 0:HEAD] += t_dot(gs, qs[:, cols])
        gkv[:, HEAD:] += t_dot(pe.astype(BF16), obs[:, cols])
        return carry

    lax.fori_loop(0, heads, one_head, 0)
    gkvb[...] = gkv[...].astype(BF16)
    for k in range(1, nch):
        q = (chip + k) % nch
        snd.start(
            gkvb.at[pl.ds(pl.multiple_of(q * t2, t2), t2)], gkvr.at[k - 1], rkv.at[k],
            (q * 2 + core, z),
        )

    def fetch(src, room, spot):
        here = room.at[pl.ds(spot // 2 * per, per), pl.ds(spot % 2 * fc, fc)]
        return here, loads.local(src, here)

    def add_far(dst, src):
        here, cp = fetch(src, gr, 0)
        cp.wait()
        add_into(dst, here)

    part[...] = dot_t(graw[:, :qw], wa[:, :qw])

    def query_grads(k, carry):
        cols = pl.ds(pl.multiple_of(k * 2 * per, 128), 2 * per)
        wa[cols, 0:qw] = t_dot(xa[:, cols], graw[:, 0:qw]).astype(BF16)
        return carry

    lax.fori_loop(0, nch, query_grads, 0)
    qrs = Reduce(
        pc, snd, lambda q, w: wa.at[slab_rows(q, w), pl.ds(0, qw)], qfirst, qfx, qfy, qsem
    )
    qrs.diagonal()
    qrs.straight_x()
    qrs.straight_y()
    brs.merge(add_into)
    ers[0].merge(add_far)
    gk = gkv[mine]
    for k in range(1, nch):
        arrived(gkvr.at[k - 1], rkv.at[k])
        gk = gk + gkvr[k - 1].astype(F32)
    graw[:, qw:qw + HEAD] = rope(gk[:, :HEAD] * scale, cos, -sin).astype(BF16)
    graw[:, qw + HEAD:] = gk[:, HEAD:].astype(BF16)
    part[...] += dot_t(graw[:, qw:], wa[:, qw:kw])
    snd.start(part.at[sib0], pget, rmisc.at[1], sib)

    def key_grads(k, carry):
        cols = pl.ds(pl.multiple_of(k * 2 * per, 128), 2 * per)
        wa[cols, qw:kw] = t_dot(xa[:, cols], graw[:, qw:]).astype(BF16)
        return carry

    lax.fori_loop(0, nch, key_grads, 0)
    arrived(pget, rmisc.at[1])
    gxa = part[mine0] + pget[...]
    h = h_ref[...].astype(F32)
    r = rms(h, width)
    n = h * r
    gy = gxa * gain_a
    ig_ref[...] += r * (gy - n * (jnp.sum(gy * n, axis=1, keepdims=True) * (1.0 / width)))
    wa[:, kw:] = (
        exts[...] + t_dot((gxa * n).astype(BF16), (lane0 == 8).astype(BF16))
    ).astype(BF16)
    krs = Reduce(
        pc, snd, lambda q, w: wa.at[slab_rows(q, w), pl.ds(qw, kx)], kfirst, kfx, kfy, ksem
    )
    krs.diagonal()
    krs.straight_x()
    krs.straight_y()
    qrs.merge(add_into)
    ers[1].merge(add_far)
    krs.merge(add_into)
    ers[2].merge(add_far)

    osum = okeep[nz - 1].astype(F32) + h1s[...]
    room = [xm.at[pl.ds(i * t0, t0)] for i in range(nz - 1)]
    got = []
    for i in range(nz - 1):
        arrived(ozr.at[i], oz_r.at[i])
        got.append(loads.local(ozr.at[i], room[i]))
    for i in range(nz - 1):
        got[i].wait()
        osum = osum + room[i][...].astype(F32)
    out_ref[...] = osum

    def piece(q, w):
        return pl.ds(pl.multiple_of((chip * 2 + w) * per + q * rp, 16), rp)

    groups = (
        (brs, lambda rows: wb.at[rows], zrb, rzb, fb, frb),
        (qrs, lambda rows: wa.at[rows, pl.ds(0, qw)], zrq, rzq, fq, frq),
        (krs, lambda rows: wa.at[rows, pl.ds(qw, kx)], zrk, rzk, fk, frk),
    )
    for rs, at, zrecv, rz, _, _ in groups:
        rs.wait()
        for w in range(2):
            dst = rs.slab(chip, w)
            dst[...] = (
                dst[...].astype(F32) + rs.fx[w].astype(F32) + rs.fy[w].astype(F32)
            ).astype(BF16)
        for dz in range(1, nz):
            q = pc.zto(dz)
            for w in range(2):
                snd.start(at(piece(q, w)), zrecv.at[dz - 1, w], rz.at[2 * dz + w], (c, q))

    e_own = []
    for m in range(3):
        ers[m].wait()
        got = [
            fetch(src.at[m, w], room, 2 * m + w)
            for src, room in ((efx, gr), (efy, xm)) for w in range(2)
        ]
        for _, cp in got:
            cp.wait()
        for w in range(2):
            dst = ers[m].slab(chip, w)
            tot = dst[...].astype(F32) + got[w][0][...].astype(F32)
            dst[...] = (tot + got[2 + w][0][...].astype(F32)).astype(BF16)
        snd.start(ers[m].slab(chip, 1 - core), esibr.at[m], rmisc.at[2 + m], sib)
        e_own.append(loads.local(ers[m].slab(chip, core), (eg_out, eu_out, ed_out)[m].at[core]))
    for k, (rs, at, zrecv, rz, fin, get) in enumerate(groups):
        for w in range(2):
            tot = at(piece(z, w))[...].astype(F32)
            for dz in range(1, nz):
                arrived(zrecv.at[dz - 1, w], rz.at[2 * dz + w])
                tot = tot + zrecv[dz - 1, w].astype(F32)
            fin[w] = tot
        snd.start(fin.at[1 - core], get, rmisc.at[5 + k], sib)
    for m in range(3):
        arrived(esibr.at[m], rmisc.at[2 + m])
        e_own.append(loads.local(esibr.at[m], (eg_out, eu_out, ed_out)[m].at[1 - core]))

    def half(k, count):
        return pl.ds(pl.multiple_of(k * count, 128), count)

    for k, (out, count, fin, get, off) in enumerate((
        (gwo_out, qw, fb, frb, 0), (gwq_out, qw, fq, frq, 0),
        (gwk_out, HEAD, fk, frk, 0), (gwv_out, HEAD, fk, frk, HEAD),
    )):
        if k < 3:
            arrived(get, rmisc.at[5 + k])
        out[:, half(core, count)] = fin[core, :, off:off + count]
        out[:, half(1 - core, count)] = get[:, off:off + count]
    ext_out[...] = fk[core, :, 2 * HEAD:] + frk[:, 2 * HEAD:]
    for cp in e_own:
        cp.wait()
    for i in range(nz - 1):
        for cp in gz_copies(i):
            cp.wait_send()
        oz_copy(i).wait_send()
    snd.drain()


def cfg_experts(cfg):
    return cfg[7]


def layer_call(cfg, args):
    nctx, nz, width, rp, t0, heads, fc, eloc = cfg
    nch, t2, dp = nctx // 2, 2 * t0, nctx * nz * rp
    qw = heads * HEAD
    kx = 3 * HEAD
    ca = qw + kx
    keys = nch * t2
    rows = nz * t2
    per = nz * rp
    vm = pl.BlockSpec(memory_space=pltpu.VMEM)
    hb = pl.BlockSpec(memory_space=pltpu.HBM)
    sds = jax.ShapeDtypeStruct
    dma = pltpu.SemaphoreType.DMA
    v = pltpu.VMEM
    return pl.pallas_call(
        functools.partial(layer_kernel, cfg),
        out_shape=(
            sds((t0, dp), F32), sds((t0, dp), F32),
            sds((2, per, fc), BF16), sds((2, per, fc), BF16), sds((2, per, fc), BF16),
            sds((rp, 2 * qw), F32), sds((rp, 2 * HEAD), F32), sds((rp, 2 * HEAD), F32),
            sds((rp, 2 * qw), F32), sds((rp, 128), F32),
        ) + (sds((3, 2, per, fc), BF16),) * 3 + (sds((nz - 1, t0, dp), BF16),),
        in_specs=[vm] * 8 + [hb] * 5,
        out_specs=(vm, vm, hb, hb, hb, vm, vm, vm, vm, vm, hb, hb, hb, hb),
        scratch_shapes=[
            v((dp, ca), BF16), v((dp, qw), BF16), v((3, dp, fc), BF16),
            v((nz, 2, rp, ca), BF16), v((nz, 2, rp, qw), BF16), v((2, t0, dp), BF16),
            v((t2, HEAD), F32), v((t2, HEAD), F32),
            v((t2, qw), BF16), v((keys, 2 * HEAD), BF16), v((t2, 128), F32), v((t2, qw), BF16),
            v((t2, dp), BF16), v((t0, dp), F32),
            v((rows, dp), BF16), v((rows, dp), BF16), v((rows, 128), F32),
            v((rows, 2 * fc), BF16), v((rows, fc), BF16),
            v((nz, t0, dp), BF16), v((nz, t0, dp), BF16), v((nz, t0, dp), BF16),
            v((nz - 1, t0, dp), BF16), v((nz, t0, dp), BF16),
            v((nz, t0, 128), F32), v((nz, t0, 128), F32), v((nz, t0, 128), F32),
            v((nz - 1, t0, 128), F32),
            v((t2, dp), BF16), v((keys, 2 * HEAD), F32), v((keys, 2 * HEAD), BF16),
            v((nch - 1, t2, 2 * HEAD), BF16), v((t2, ca - 128), BF16),
            v((t2, dp), F32), v((t0, dp), F32), v((dp, 128), F32),
            v((3, per, fc), BF16),
            v((2, per, qw), BF16), v((2, per, qw), BF16), v((2, per, qw), BF16),
            v((2, per, qw), BF16), v((2, per, qw), BF16), v((2, per, qw), BF16),
            v((2, per, kx), BF16), v((2, per, kx), BF16), v((2, per, kx), BF16),
            v((nz - 1, 2, rp, qw), BF16), v((nz - 1, 2, rp, qw), BF16),
            v((nz - 1, 2, rp, kx), BF16),
            v((2, rp, qw), F32), v((2, rp, qw), F32), v((2, rp, kx), F32),
            v((rp, qw), F32), v((rp, qw), F32), v((rp, kx), F32),
            v((t2, 128), F32),
            dma((270,)), dma((60,)), dma((nctx * nz,)), dma((nctx * nz,)), dma((3 * nctx,)),
            dma((nz,)), dma((nz,)), dma((2,)), dma((3 * nz,)), dma((3 * nz,)),
            dma((2 * nz,)), dma((2 * nz,)), dma((2 * nz,)), dma((2 * nz,)),
            dma((nz,)), dma((nz,)), dma((nz,)), dma((nz,)), dma((8,)), dma((3, 6)), dma((6,)),
            dma((6,)), dma((6,)), dma((nch,)), dma((nch,)), dma((2 * nz,)), dma((2 * nz,)),
            dma((2 * nz,)),
        ],
        compiler_params=pltpu.CompilerParams(
            collective_id=0, has_side_effects=True, vmem_limit_bytes=64 * 2**20
        ),
        name="layer",
    )(*args)


def body(hidden, routes, cot, na, wq, wk, wv, wo, nm, wr, wg, wu, wd):
    nctx, nz = lax.axis_size("ctx"), lax.axis_size("wsh")
    t0, width = hidden.shape[1], hidden.shape[2]
    rp = wq.shape[1]
    eloc, ff = wg.shape[2], wg.shape[3]
    heads = wq.shape[2] // HEAD // 2
    fc = eloc * ff // 2
    cfg = (nctx, nz, width, rp, t0, heads, fc, eloc)
    experts = wr.shape[2]
    extra = jnp.concatenate(
        [wr[0], na[0][:, None], nm[0][:, None], jnp.zeros((rp, 128 - experts - 2), BF16)], axis=1
    )
    pos = np.arange(nctx * t0, dtype=np.float32)
    freq = np.float32(BASE) ** (-np.arange(HEAD // 2, dtype=np.float32) * 2.0 / HEAD)
    ang = pos[:, None] * freq.astype(np.float32)[None, :]
    cos, sin = np.cos(ang), np.sin(ang)
    cosf = jnp.asarray(np.concatenate([cos, cos], axis=1), F32)
    sinf = jnp.asarray(np.concatenate([-sin, sin], axis=1), F32)
    halves = [jnp.transpose(w[0], (1, 0, 2)) for w in (wg, wu, wd)]
    r = layer_call(
        cfg,
        (hidden[0], routes[0, 0], cot[0], wq[0], wk[0], wv[0], wo[0], extra, *halves, cosf, sinf),
    )
    out, ig, eg, eu, ed, gwq, gwk, gwv, gwo, ext = r[:10]
    back = lambda x: jnp.transpose(x.astype(F32), (1, 0, 2))[None]
    return (
        out[None], ig[None], ext[:, 8][None], gwq[None], gwk[None], gwv[None], gwo[None],
        ext[:, 9][None], ext[:, :experts][None], back(eg), back(eu), back(ed),
    )


def shifted(value, axis, steps):
    count = lax.axis_size(axis)
    pairs = [(source, (source + steps) % count) for source in range(count)]
    return lax.ppermute(value, axis, pairs)


def normalize(hidden_state, gain):
    return (
        hidden_state
        * lax.rsqrt(jnp.mean(hidden_state * hidden_state, axis=-1, keepdims=True) + NORM_EPSILON)
        * gain
    )


def rotary(token_positions, head_size):
    half_size = head_size // 2
    frequency = ROTARY_BASE ** (-jnp.arange(half_size, dtype=jnp.float32) * 2.0 / head_size)
    angles = token_positions.astype(jnp.float32)[:, None] * frequency[None, :]
    return (jnp.cos(angles)[:, None, :], jnp.sin(angles)[:, None, :])


def apply_rotary(values_in, cosine, sine_rows, direction):
    half_size = values_in.shape[-1] // 2
    first_half = values_in[..., :half_size]
    second = values_in[..., half_size:]
    return jnp.concatenate(
        [
            first_half * cosine - direction * second * sine_rows,
            second * cosine + direction * first_half * sine_rows,
        ],
        axis=-1,
    )


def slot_targets(picks_in, matches):
    flat_matches = matches.reshape(-1, matches.shape[-1]).astype(jnp.int32)
    earlier = jnp.cumsum(flat_matches, axis=0) - flat_matches
    return picks_in.reshape(-1) * CAP + jnp.sum(earlier * flat_matches, axis=1)


def score_rows(query_low, key_rows, token_positions):
    total_rows = query_low.shape[0]
    head_size = query_low.shape[2]
    grouped_heads = query_low.reshape(total_rows, key_rows.shape[1], -1, head_size)
    scores = jnp.einsum(
        "qhgd,khd->hgqk", grouped_heads, key_rows, preferred_element_type=jnp.float32
    ) * head_size ** (-0.5)
    allowed = jnp.arange(key_rows.shape[0], dtype=jnp.int32)[None, :] <= token_positions[:, None]
    return (grouped_heads, jnp.where(allowed[None, None], scores, -1e30))


def attend(query_low, key_rows, value_rows, token_positions):
    grouped_heads, scores = score_rows(query_low, key_rows, token_positions)
    highest = jnp.max(scores, axis=-1, keepdims=True)
    log_total = highest + jnp.log(jnp.sum(jnp.exp(scores - highest), axis=-1, keepdims=True))
    weights = jnp.exp(scores - log_total).astype(jnp.bfloat16)
    attended = jnp.einsum("hgqk,khd->qhgd", weights, value_rows, preferred_element_type=jnp.float32)
    return (attended.reshape(query_low.shape[0], -1), log_total)


def attend_grad(query_low, key_rows, value_rows, token_positions, log_total, grad_mixed):
    grouped_heads, scores = score_rows(query_low, key_rows, token_positions)
    score_scale = query_low.shape[-1] ** (-0.5)
    softmax_rows = jnp.exp(scores - log_total)
    weights = softmax_rows.astype(jnp.bfloat16)
    grad_grouped = grad_mixed.reshape(grouped_heads.shape)
    grad_weights = jnp.einsum(
        "qhgd,khd->hgqk", grad_grouped, value_rows, preferred_element_type=jnp.float32
    )
    grad_values = jnp.einsum(
        "hgqk,qhgd->khd", weights, grad_grouped, preferred_element_type=jnp.float32
    )
    row_inner = jnp.sum(softmax_rows * grad_weights, axis=-1, keepdims=True)
    grad_scores = (softmax_rows * (grad_weights - row_inner)).astype(jnp.bfloat16)
    grad_query = (
        jnp.einsum("hgqk,khd->qhgd", grad_scores, key_rows, preferred_element_type=jnp.float32)
        * score_scale
    )
    grad_keys = (
        jnp.einsum("hgqk,qhgd->khd", grad_scores, grouped_heads, preferred_element_type=jnp.float32)
        * score_scale
    )
    return (grad_query.reshape(query_low.shape), grad_keys, grad_values)


def collect_key_grads(grad_keys, grad_values, total_rows):
    cycle_size = lax.axis_size("ctx")
    own_index = lax.axis_index("ctx")
    both_grads = jnp.stack([grad_keys, grad_values])

    def block_piece(block_index):
        return lax.dynamic_slice_in_dim(both_grads, block_index * total_rows, total_rows, 1)

    def cycle_step(step_index, carried):
        moved = shifted(carried.astype(jnp.bfloat16), "ctx", -1).astype(carried.dtype)
        block_index = (own_index + step_index) % cycle_size
        weight_now = jnp.where(step_index < cycle_size, 1.0, 0.0).astype(jnp.float32)
        return moved + weight_now * block_piece(block_index)

    collected = lax.fori_loop(1, cycle_size + 1, cycle_step, block_piece(own_index))
    return (collected[0], collected[1])


def forward_layer(hidden_state, picks_in, dense_set, expert_set):
    gain_attn, query_matrix, key_matrix, value_matrix, output_matrix, gain_moe, router_matrix = (
        dense_set
    )
    gate_w, up_w, down_w = expert_set
    total_rows, model_width = hidden_state.shape
    token_positions = lax.axis_index("ctx") * total_rows + jnp.arange(total_rows, dtype=jnp.int32)
    cosine, sine_rows = rotary(token_positions, HEAD_DIM)
    attention_normed = normalize(hidden_state, gain_attn.astype(jnp.float32)).astype(jnp.bfloat16)
    query_unrotated = jnp.dot(
        attention_normed, query_matrix, preferred_element_type=jnp.float32
    ).reshape(total_rows, QUERY_HEADS, HEAD_DIM)
    key_unrotated = jnp.dot(
        attention_normed, key_matrix, preferred_element_type=jnp.float32
    ).reshape(total_rows, KEY_VALUE_HEADS, HEAD_DIM)
    query_low = apply_rotary(query_unrotated, cosine, sine_rows, 1.0).astype(jnp.bfloat16)
    key_low = apply_rotary(key_unrotated, cosine, sine_rows, 1.0).astype(jnp.bfloat16)
    value_low = (
        jnp.dot(attention_normed, value_matrix, preferred_element_type=jnp.float32)
        .astype(jnp.bfloat16)
        .reshape(total_rows, KEY_VALUE_HEADS, HEAD_DIM)
    )
    key_rows, value_rows = (
        lax.all_gather(key_low, "ctx", axis=0, tiled=True),
        lax.all_gather(value_low, "ctx", axis=0, tiled=True),
    )
    attended, log_total = attend(query_low, key_rows, value_rows, token_positions)
    mixed_reduced = attended.astype(jnp.bfloat16)
    post_attention = hidden_state + lax.dot_general(
        mixed_reduced, output_matrix, (((1,), (1,)), ((), ())), preferred_element_type=jnp.float32
    )
    expert_normed = normalize(post_attention, gain_moe.astype(jnp.float32)).astype(jnp.bfloat16)
    router_logits = jnp.dot(expert_normed, router_matrix, preferred_element_type=jnp.float32)
    expert_count = router_logits.shape[1]
    matches = picks_in[:, :, None] == jnp.arange(expert_count, dtype=jnp.int32)[None, None, :]
    gate_weights = jax.nn.softmax(
        jnp.sum(jnp.where(matches, router_logits[:, None, :], 0.0), axis=-1), axis=-1
    )
    targets = slot_targets(picks_in, matches)
    outgoing = (
        jnp.zeros((expert_count * CAP, model_width), jnp.bfloat16)
        .at[targets]
        .set(jnp.repeat(expert_normed, TOP, axis=0))
    )
    group_count = lax.axis_size("wsh")
    local_count = gate_w.shape[1]
    arrived = lax.all_to_all(
        outgoing.reshape(group_count, local_count, CAP, model_width),
        "wsh",
        split_axis=0,
        concat_axis=0,
        tiled=True,
    )
    gate_pre = jnp.einsum("sjcd,djf->sjcf", arrived, gate_w, preferred_element_type=jnp.float32)
    up_pre = jnp.einsum("sjcd,djf->sjcf", arrived, up_w, preferred_element_type=jnp.float32)
    activations = (jax.nn.silu(gate_pre) * up_pre).astype(jnp.bfloat16)
    produced = jnp.einsum(
        "sjcf,djf->sjcd", activations, down_w, preferred_element_type=jnp.float32
    ).astype(jnp.bfloat16)
    returned = lax.all_to_all(produced, "wsh", split_axis=0, concat_axis=0, tiled=True)
    returned, arrived, gate_pre, up_pre = (returned, arrived, gate_pre, up_pre)
    picked = (
        returned.reshape(-1, model_width)[targets]
        .reshape(total_rows, TOP, model_width)
        .astype(jnp.float32)
    )
    after_moe = post_attention + jnp.sum(gate_weights[:, :, None] * picked, axis=1)
    stored = (
        hidden_state,
        attention_normed,
        query_low,
        key_low,
        value_low,
        log_total,
        mixed_reduced,
        post_attention,
        expert_normed,
        matches,
        gate_weights,
        targets,
        picked,
        arrived,
        gate_pre,
        up_pre,
    )
    return (after_moe, stored, (key_rows, value_rows))


def backward_layer(incoming, stored, dense_set, expert_set, key_rows, value_rows):
    (
        hidden_state,
        attention_normed,
        query_low,
        key_low,
        value_low,
        log_total,
        mixed_reduced,
        post_attention,
        expert_normed,
        matches,
        gate_weights,
        targets,
        picked,
        arrived,
        gate_pre,
        up_pre,
    ) = stored
    gain_attn, query_matrix, key_matrix, value_matrix, output_matrix, gain_moe, router_matrix = (
        dense_set
    )
    gate_w, up_w, down_w = expert_set
    total_rows, model_width = hidden_state.shape
    token_positions = lax.axis_index("ctx") * total_rows + jnp.arange(total_rows, dtype=jnp.int32)
    cosine, sine_rows = rotary(token_positions, HEAD_DIM)
    grad_y = (gate_weights[:, :, None] * incoming[:, None, :]).astype(jnp.bfloat16)
    grad_gates = jnp.sum(incoming[:, None, :] * picked, axis=-1)
    grad_chosen = gate_weights * (
        grad_gates - jnp.sum(gate_weights * grad_gates, axis=-1, keepdims=True)
    )
    grad_logits = jnp.sum(jnp.where(matches, grad_chosen[:, :, None], 0.0), axis=1).astype(
        jnp.bfloat16
    )
    slot_total = arrived.shape[0] * arrived.shape[1] * arrived.shape[2]
    outgoing = (
        jnp.zeros((slot_total, model_width), jnp.bfloat16)
        .at[targets]
        .set(grad_y.reshape(-1, model_width))
    )
    grad_arrived = lax.all_to_all(
        outgoing.reshape(arrived.shape), "wsh", split_axis=0, concat_axis=0, tiled=True
    )
    grad_acts = jnp.einsum(
        "sjcd,djf->sjcf", grad_arrived, down_w, preferred_element_type=jnp.float32
    )
    sigmoid_gate = jax.nn.sigmoid(gate_pre)
    silu_gate = jax.nn.silu(gate_pre)
    activations = (silu_gate * up_pre).astype(jnp.bfloat16)
    grad_gate = (
        grad_acts * up_pre * sigmoid_gate * (1.0 + gate_pre * (1.0 - sigmoid_gate))
    ).astype(jnp.bfloat16)
    grad_up = (grad_acts * silu_gate).astype(jnp.bfloat16)
    grad_rows = (
        jnp.einsum("sjcf,djf->sjcd", grad_gate, gate_w, preferred_element_type=jnp.float32)
        + jnp.einsum("sjcf,djf->sjcd", grad_up, up_w, preferred_element_type=jnp.float32)
    ).astype(jnp.bfloat16)
    grad_back = lax.all_to_all(grad_rows, "wsh", split_axis=0, concat_axis=0, tiled=True)
    expert_grads = (
        lax.psum_scatter(
            jnp.einsum(
                "sjcd,sjcf->djf", arrived, grad_gate, preferred_element_type=jnp.float32
            ).astype(jnp.bfloat16),
            "ctx",
            scatter_dimension=0,
            tiled=True,
        ).astype(jnp.float32),
        lax.psum_scatter(
            jnp.einsum(
                "sjcd,sjcf->djf", arrived, grad_up, preferred_element_type=jnp.float32
            ).astype(jnp.bfloat16),
            "ctx",
            scatter_dimension=0,
            tiled=True,
        ).astype(jnp.float32),
        lax.psum_scatter(
            jnp.einsum(
                "sjcd,sjcf->djf", grad_arrived, activations, preferred_element_type=jnp.float32
            ).astype(jnp.bfloat16),
            "ctx",
            scatter_dimension=0,
            tiled=True,
        ).astype(jnp.float32),
    )
    returned_rows = (
        grad_back.reshape(-1, model_width)[targets]
        .reshape(total_rows, TOP, model_width)
        .astype(jnp.float32)
    )
    grad_normed_moe = jnp.sum(returned_rows, axis=1) + lax.dot_general(
        grad_logits, router_matrix, (((1,), (1,)), ((), ())), preferred_element_type=jnp.float32
    )
    router_term = jnp.einsum(
        "td,te->de", expert_normed, grad_logits, preferred_element_type=jnp.float32
    )
    unused_moe, pull_moe = jax.vjp(normalize, post_attention, gain_moe.astype(jnp.float32))
    grad_after_norm, gain_moe_term = pull_moe(grad_normed_moe)
    grad_after_attn = incoming + grad_after_norm
    grad_attn = grad_after_attn.astype(jnp.bfloat16)
    out_term = jnp.einsum("td,tj->dj", grad_attn, mixed_reduced, preferred_element_type=jnp.float32)
    grad_mixed = jnp.dot(grad_attn, output_matrix, preferred_element_type=jnp.float32).astype(
        jnp.bfloat16
    )
    grad_query, grad_keys, grad_values = attend_grad(
        query_low, key_rows, value_rows, token_positions, log_total, grad_mixed
    )
    grad_key, grad_value = collect_key_grads(grad_keys, grad_values, total_rows)
    grad_query_raw = (
        apply_rotary(grad_query, cosine, sine_rows, -1.0)
        .reshape(total_rows, -1)
        .astype(jnp.bfloat16)
    )
    grad_key_raw = (
        apply_rotary(grad_key, cosine, sine_rows, -1.0).reshape(total_rows, -1).astype(jnp.bfloat16)
    )
    grad_value_raw = grad_value.reshape(total_rows, -1).astype(jnp.bfloat16)
    contract_last = (((1,), (1,)), ((), ()))
    grad_normed_attn = lax.dot_general(
        grad_query_raw, query_matrix, contract_last, preferred_element_type=jnp.float32
    )
    grad_normed_attn = grad_normed_attn + lax.dot_general(
        grad_key_raw, key_matrix, contract_last, preferred_element_type=jnp.float32
    )
    grad_normed_attn = grad_normed_attn + lax.dot_general(
        grad_value_raw, value_matrix, contract_last, preferred_element_type=jnp.float32
    )
    query_term = jnp.einsum(
        "td,tf->df", attention_normed, grad_query_raw, preferred_element_type=jnp.float32
    )
    key_term = jnp.einsum(
        "td,tf->df", attention_normed, grad_key_raw, preferred_element_type=jnp.float32
    )
    value_term = jnp.einsum(
        "td,tf->df", attention_normed, grad_value_raw, preferred_element_type=jnp.float32
    )
    unused_attn, pull_attn = jax.vjp(normalize, hidden_state, gain_attn.astype(jnp.float32))
    grad_before, gain_attn_term = pull_attn(grad_normed_attn)
    layer_grads = (
        lax.psum_scatter(gain_attn_term, ("ctx", "wsh"), scatter_dimension=0, tiled=True),
        lax.psum_scatter(query_term, ("ctx", "wsh"), scatter_dimension=0, tiled=True),
        lax.psum_scatter(key_term, ("ctx", "wsh"), scatter_dimension=0, tiled=True),
        lax.psum_scatter(value_term, ("ctx", "wsh"), scatter_dimension=0, tiled=True),
        lax.psum_scatter(out_term, ("ctx", "wsh"), scatter_dimension=0, tiled=True),
        lax.psum_scatter(gain_moe_term, ("ctx", "wsh"), scatter_dimension=0, tiled=True),
        lax.psum_scatter(router_term, ("ctx", "wsh"), scatter_dimension=0, tiled=True),
    )
    return (grad_after_attn + grad_before, layer_grads, expert_grads)


def plain_body(
    hidden_in,
    routes,
    cotangent,
    norm_attn,
    w_query,
    key_projection,
    value_projection,
    w_out,
    norm_moe,
    w_router,
    w_gate,
    w_up,
    w_down,
):
    hidden_state = hidden_in[0].astype(jnp.float32)
    layer_number = 0
    dense_set = (
        lax.all_gather(norm_attn[layer_number], ("ctx", "wsh"), axis=0, tiled=True),
        lax.all_gather(w_query[layer_number], ("ctx", "wsh"), axis=0, tiled=True),
        lax.all_gather(key_projection[layer_number], ("ctx", "wsh"), axis=0, tiled=True),
        lax.all_gather(value_projection[layer_number], ("ctx", "wsh"), axis=0, tiled=True),
        lax.all_gather(w_out[layer_number], ("ctx", "wsh"), axis=0, tiled=True),
        lax.all_gather(norm_moe[layer_number], ("ctx", "wsh"), axis=0, tiled=True),
        lax.all_gather(w_router[layer_number], ("ctx", "wsh"), axis=0, tiled=True),
    )
    expert_set = (
        lax.all_gather(w_gate[layer_number], "ctx", axis=0, tiled=True),
        lax.all_gather(w_up[layer_number], "ctx", axis=0, tiled=True),
        lax.all_gather(w_down[layer_number], "ctx", axis=0, tiled=True),
    )
    hidden_state, stored, gathered = forward_layer(
        hidden_state, routes[layer_number, 0], dense_set, expert_set
    )
    records = [(stored, None, None, None)]
    incoming = cotangent[0]
    dense_grads = []
    expert_grads = []
    layer_number = 0
    stored, dense_set, expert_set, gathered = records[layer_number]
    dense_set = (
        lax.all_gather(norm_attn[layer_number], ("ctx", "wsh"), axis=0, tiled=True),
        lax.all_gather(w_query[layer_number], ("ctx", "wsh"), axis=0, tiled=True),
        lax.all_gather(key_projection[layer_number], ("ctx", "wsh"), axis=0, tiled=True),
        lax.all_gather(value_projection[layer_number], ("ctx", "wsh"), axis=0, tiled=True),
        lax.all_gather(w_out[layer_number], ("ctx", "wsh"), axis=0, tiled=True),
        lax.all_gather(norm_moe[layer_number], ("ctx", "wsh"), axis=0, tiled=True),
        lax.all_gather(w_router[layer_number], ("ctx", "wsh"), axis=0, tiled=True),
    )
    expert_set = (
        lax.all_gather(w_gate[layer_number], "ctx", axis=0, tiled=True),
        lax.all_gather(w_up[layer_number], "ctx", axis=0, tiled=True),
        lax.all_gather(w_down[layer_number], "ctx", axis=0, tiled=True),
    )
    gathered = (
        lax.all_gather(stored[3], "ctx", axis=0, tiled=True),
        lax.all_gather(stored[4], "ctx", axis=0, tiled=True),
    )
    incoming, layer_grads, layer_expert = backward_layer(
        incoming, stored, dense_set, expert_set, gathered[0], gathered[1]
    )
    dense_grads.insert(0, layer_grads)
    expert_grads.insert(0, layer_expert)
    stacked_dense = [
        jnp.stack([grads_item[position] for grads_item in dense_grads]) for position in range(7)
    ]
    stacked_expert = [
        jnp.stack([grads_item[position] for grads_item in expert_grads]) for position in range(3)
    ]
    return (
        hidden_state[None],
        incoming[None],
        stacked_dense[0],
        stacked_dense[1],
        stacked_dense[2],
        stacked_dense[3],
        stacked_dense[4],
        stacked_dense[5],
        stacked_dense[6],
        stacked_expert[0],
        stacked_expert[1],
        stacked_expert[2],
    )


def solution(mesh):
    return jax.shard_map(
        body if mesh.shape["ctx"] == 8 and mesh.shape["wsh"] == 4 else plain_body,
        mesh=mesh,
        in_specs=(
            P("wsh", "ctx", None),
            P(None, "wsh", "ctx", None),
            P("wsh", "ctx", None),
            P(None, ("ctx", "wsh")),
            P(None, ("ctx", "wsh"), None),
            P(None, ("ctx", "wsh"), None),
            P(None, ("ctx", "wsh"), None),
            P(None, ("ctx", "wsh"), None),
            P(None, ("ctx", "wsh")),
            P(None, ("ctx", "wsh"), None),
            P(None, "ctx", "wsh", None),
            P(None, "ctx", "wsh", None),
            P(None, "ctx", "wsh", None),
        ),
        out_specs=(
            P("wsh", "ctx", None),
            P("wsh", "ctx", None),
            P(None, ("ctx", "wsh")),
            P(None, ("ctx", "wsh"), None),
            P(None, ("ctx", "wsh"), None),
            P(None, ("ctx", "wsh"), None),
            P(None, ("ctx", "wsh"), None),
            P(None, ("ctx", "wsh")),
            P(None, ("ctx", "wsh"), None),
            P(None, "ctx", "wsh", None),
            P(None, "ctx", "wsh", None),
            P(None, "ctx", "wsh", None),
        ),
        check_vma=False,
    )
```

```python
import functools
import jax
import jax.numpy as jnp
import numpy as np
from jax import lax
from jax.experimental import pallas as pl
from jax.experimental.pallas import tpu as pltpu
from jax.sharding import PartitionSpec as P

QUERY_HEADS = 12
KEY_VALUE_HEADS = 2
HEAD_DIM = 128
CAP = 128
NORM_EPSILON = 1e-06
ROTARY_BASE = 1000000.0
MESH = pl.DeviceIdType.MESH
HEAD = 128
TOP = 4
EPS = 1e-06
BASE = 1000000.0
F32 = jnp.float32
BF16 = jnp.bfloat16


def dot(a, b):
    return lax.dot_general(a, b, (((1,), (0,)), ((), ())), preferred_element_type=F32)


def dot_t(a, b):
    return lax.dot_general(a, b, (((1,), (1,)), ((), ())), preferred_element_type=F32)


def t_dot(a, b):
    return lax.dot_general(a, b, (((0,), (0,)), ((), ())), preferred_element_type=F32)


class Place:
    def __init__(self, nctx, nz):
        self.nctx, self.nz, self.nch = nctx, nz, nctx // 2
        self.c = lax.axis_index("ctx")
        self.z = lax.axis_index("wsh")
        self.chip = self.c // 2
        self.core = self.c % 2
        self.sib = self.chip * 2 + 1 - self.core
        self.square = self.nch == 4

    def xchip(self):
        return self.chip + 1 - 2 * (self.chip % 2)

    def ychip(self):
        return (self.chip + 2) % 4

    def near(self, k):
        s = 0
        for here in range(self.nz):
            order = sorted(
                (v for v in range(self.nz) if v != here),
                key=lambda v: (abs(v - here), 2 * v // self.nz != 2 * here // self.nz),
            )
            s = jnp.where(self.z == here, order[k - 1], s)
        return s

    def zto(self, dz):
        return (self.z + dz) % self.nz

    def zfrom(self, dz):
        return (self.z + self.nz - dz) % self.nz


class Sends:
    def __init__(self, sems, count):
        self.sems, self.count, self.used, self.live = sems, count, 0, []

    def start(self, src, dst, rsem, dev, when=None):
        assert self.used < self.count
        cp = pltpu.make_async_remote_copy(
            src_ref=src,
            dst_ref=dst,
            send_sem=self.sems.at[self.used],
            recv_sem=rsem,
            device_id=dev,
            device_id_type=MESH,
        )
        if when is None:
            cp.start()
        else:
            pl.when(when)(cp.start)
        self.used += 1
        self.live.append((cp, when))

    def local(self, src, dst):
        assert self.used < self.count
        cp = pltpu.make_async_copy(src, dst, self.sems.at[self.used])
        cp.start()
        self.used += 1
        return cp

    def drain(self):
        for cp, when in self.live:
            if when is None:
                cp.wait_send()
            else:
                pl.when(when)(cp.wait_send)
        self.live = []


def arrived(ref, sem):
    pltpu.make_async_copy(ref, ref, sem).wait()


def greet(pc):
    bar = pltpu.get_barrier_semaphore()
    for k in range(1, pc.nctx):
        to = ((pc.c + k) % pc.nctx, pc.z)
        pl.semaphore_signal(bar, inc=1, device_id=to, device_id_type=MESH)
    for k in range(1, pc.nz):
        pl.semaphore_signal(bar, inc=1, device_id=(pc.c, pc.zto(k)), device_id_type=MESH)
    return lambda: pl.semaphore_wait(bar, pc.nctx + pc.nz - 2)


def rms(x, width):
    return lax.rsqrt(jnp.sum(x * x, axis=-1, keepdims=True) * (1.0 / width) + EPS)


def gain_row(extra, lane):
    pick = (lax.broadcasted_iota(jnp.int32, (16, extra.shape[1]), 1) == lane).astype(BF16)
    return dot_t(pick, extra)[0:1]


def rope(x, cos, sin):
    return x * cos + pltpu.roll(x, HEAD // 2, 1) * sin


class Reduce:
    def __init__(self, pc, snd, slab, first, fx, fy, sems, far=None):
        self.pc, self.snd, self.slab = pc, snd, slab
        self.first, self.fx, self.fy, self.sems = first, fx, fy, sems
        self.x, self.y, self.d = pc.xchip(), pc.ychip(), 3 - pc.chip
        self.far = far or (lambda w: slab(self.d, w))

    def to(self, chip):
        return (chip * 2 + self.pc.core, self.pc.z)

    def diagonal(self):
        self.snd.start(self.far(0), self.first.at[0], self.sems.at[0], self.to(self.x))
        self.snd.start(self.far(1), self.first.at[1], self.sems.at[1], self.to(self.y))

    def straight_x(self):
        self.snd.start(self.slab(self.x, 0), self.fx.at[0], self.sems.at[2], self.to(self.x))

    def straight_y(self):
        self.snd.start(self.slab(self.y, 1), self.fy.at[1], self.sems.at[5], self.to(self.y))

    def merge(self, add):
        arrived(self.first.at[0], self.sems.at[0])
        add(self.slab(self.y, 0), self.first.at[0])
        self.snd.start(self.slab(self.y, 0), self.fy.at[0], self.sems.at[4], self.to(self.y))
        arrived(self.first.at[1], self.sems.at[1])
        add(self.slab(self.x, 1), self.first.at[1])
        self.snd.start(self.slab(self.x, 1), self.fx.at[1], self.sems.at[3], self.to(self.x))

    def wait(self):
        for w in range(2):
            arrived(self.fx.at[w], self.sems.at[2 + w])
            arrived(self.fy.at[w], self.sems.at[4 + w])


def add_into(dst, src):
    dst[...] = (dst[...].astype(F32) + src[...].astype(F32)).astype(BF16)


def layer_kernel(
    cfg,
    h_ref, routes_ref, cot_ref, wq_ref, wk_ref, wv_ref, wo_ref, ga_ref, gm_ref, wr_ref,
    eg_ref, eu_ref, ed_ref,
    cos_in, sin_in,
    out_ref, ig_ref, eg_out, eu_out, ed_out, gwq_out, gwk_out, gwv_out, gwo_out, ext_out,
    efirst, efx, efy, ozr,
    wk, wq, wb, we, zk, zq, zb, hbuf, cosr, sinr, square,
    qs, kv, lses, obs, xa, h1s, xm, gr, gts,
    ggu, ap, keep, sibs, sibr, zr, okeep, kgg, sgg, rgg, zgg,
    gat, gkv, gkvb, gkvr, graw, part, pget, exts,
    esibr,
    bfirst, bfx, bfy, qfirst, qfx, qfy, kfirst, kfx, kfy,
    zrb, zrq, zrk, fb, fq, fk, frb, frq, frk, rowp,
    ssem, lsem, rwk, rwq, rwb, re, rzk_, rzq_, rzb_, rfw, rxm, rxf,
    sib_s, sib_r, z_s, z_r, osib_s, osib_r, oz_s, oz_r, rmisc, esem, bsem,
    qsem, ksem, rkv, rkvf, rzb, rzq, rzk,
):
    nctx, nz, width, rp, t0, heads, fc, _ = cfg
    pc = Place(nctx, nz)
    nch = pc.nch
    t2 = 2 * t0
    qw = heads * HEAD
    kw = qw + 2 * HEAD
    kx = wk.shape[1]
    dp = wk.shape[0]
    core, z, c, chip = pc.core, pc.z, pc.c, pc.chip
    per = nz * rp
    met = greet(pc)
    snd = Sends(ssem, ssem.shape[0])
    loads = Sends(lsem, lsem.shape[0])
    sib = (pc.sib, z)
    mine = pl.ds(pl.multiple_of(chip * t2, t2), t2)
    mine0 = pl.ds(pl.multiple_of(core * t0, t0), t0)
    sib0 = pl.ds(pl.multiple_of((1 - core) * t0, t0), t0)
    xs, ys, ds = pc.xchip() * 2, pc.ychip() * 2, (3 - chip) * 2
    nearest = [pc.near(k) for k in range(1, nz)]

    def rows(cc, s):
        return pl.ds(pl.multiple_of((cc * nz + s) * rp, 16), rp)

    def slot(s, k):
        return pl.ds(pl.multiple_of(s * t2 + k * t0, t0), t0)

    def both_parts(s):
        return pl.ds(pl.multiple_of(s * 2 * rp, 16), 2 * rp)

    def part_of(s, k):
        return pl.ds(pl.multiple_of((s * 2 + k) * rp, 16), rp)

    def slab_rows(q, w):
        return pl.ds(pl.multiple_of((q * 2 + w) * per, 16), per)

    tables = [loads.local(cos_in.at[mine], cosr), loads.local(sin_in.at[mine], sinr)]
    square[...] = jnp.zeros(square.shape, F32)
    experts = wr_ref.shape[0]
    square[0:experts, 0:rp] = wr_ref[...].astype(F32)
    square[8:9, 0:rp] = ga_ref[...].astype(F32)
    square[9:10, 0:rp] = gm_ref[...].astype(F32)
    ex = square[...].T[0:rp].astype(BF16)
    for k in range(2):
        at = part_of(z, k)
        zk[at, 0:HEAD] = wk_ref[:, k * HEAD:(k + 1) * HEAD]
        zk[at, HEAD:2 * HEAD] = wv_ref[:, k * HEAD:(k + 1) * HEAD]
        zk[at, 2 * HEAD:] = ex
        zq[at] = wq_ref[:, k * qw:(k + 1) * qw]
        zb[at] = wo_ref[:, k * qw:(k + 1) * qw]
    own = slot(z, core)
    gr[own] = cot_ref[...].astype(BF16)
    hbuf[core] = h_ref[...]
    met()

    def spread(src, dst, rs, s):
        here = dst.at[rows(c, s)]
        sem = rs.at[c * nz + s]
        for q in (pc.xchip(), pc.ychip()):
            for k in range(2):
                snd.start(src.at[part_of(s, k)], here, sem, (q * 2 + k, z))
        snd.start(src.at[part_of(s, 1 - core)], here, sem, sib)

    def forward(dst, rs, s):
        for source, to in ((ys, pc.xchip()), (xs + 1, pc.ychip())):
            here = dst.at[rows(source, s)]
            sem = rs.at[source * nz + s]
            arrived(here, sem)
            snd.start(here, here, sem, (to * 2 + core, z))

    def settle(dst, rs):
        for cc in (pc.sib, xs, ys + 1, ds, ds + 1):
            for s in range(nz):
                arrived(dst.at[rows(cc, s)], rs.at[cc * nz + s])

    packs = ((zk, rzk_, wk, rwk), (zq, rzq_, wq, rwq), (zb, rzb_, wb, rwb))
    for ref, rs, _, _ in packs:
        for s in nearest:
            here = ref.at[both_parts(z)]
            snd.start(here, here, rs.at[z], (c, s))
    for s in nearest:
        snd.start(gr.at[own], gr.at[own], rxm.at[z], (c, s))
    keeps = ([], [], [])
    snd.start(hbuf.at[core], hbuf.at[core], rfw.at[0], sib)
    for (ref, _, dst, rs), kept in zip(packs, keeps):
        spread(ref, dst, rs, z)
        kept.append(loads.local(ref.at[part_of(z, core)], dst.at[rows(c, z)]))
    snd.start(gr.at[own], gr.at[own], rxf.at[z], sib)

    def column(which):
        ref, zs, dst, rs = packs[which]
        for s in nearest:
            arrived(ref.at[both_parts(s)], zs.at[s])
            spread(ref, dst, rs, s)
            keeps[which].append(loads.local(ref.at[part_of(s, core)], dst.at[rows(c, s)]))

    def onward(which):
        _, _, dst, rs = packs[which]
        for s in [z] + nearest:
            forward(dst, rs, s)

    def have(which):
        _, _, dst, rs = packs[which]
        for cp in keeps[which]:
            cp.wait()
        settle(dst, rs)

    column(0)
    onward(0)
    column(1)
    arrived(hbuf.at[1 - core], rfw.at[0])
    for cp in tables:
        cp.wait()
    have(0)
    cos, sin = cosr[...], sinr[...]
    extra = wk[:, 2 * HEAD:]
    gain_a = gain_row(extra, 8)
    gain_m = gain_row(extra, 9)
    for k in range(2):
        hk = hbuf[k].astype(F32)
        xa[pl.ds(k * t0, t0)] = (hk * rms(hk, width) * gain_a).astype(BF16)
    xav = xa[...]
    kraw = dot(xav, wk[:, :2 * HEAD])
    kv[mine, 0:HEAD] = rope(kraw[:, :HEAD], cos, sin).astype(BF16)
    kv[mine, HEAD:] = kraw[:, HEAD:].astype(BF16)
    for k in range(1, nch):
        snd.start(kv.at[mine], kv.at[mine], rkvf.at[k], (((chip + k) % nch) * 2 + core, z))
    onward(1)
    column(2)

    def mats(m, cc):
        return we.at[m, pl.ds(pl.multiple_of(cc * per, 16), per)]

    experts_in = (eg_ref, eu_ref, ed_ref)
    own_e = [loads.local(experts_in[m].at[core], mats(m, c)) for m in range(3)]

    def expert_spread(m):
        here = mats(m, c)
        sem = re.at[m * nctx + c]
        for q in (pc.xchip(), pc.ychip()):
            for k in range(2):
                snd.start(experts_in[m].at[k], here, sem, (q * 2 + k, z))
        snd.start(experts_in[m].at[1 - core], here, sem, sib)

    def expert_onward(m):
        for source, to in ((ys, pc.xchip()), (xs + 1, pc.ychip())):
            here = mats(m, source)
            sem = re.at[m * nctx + source]
            arrived(here, sem)
            snd.start(here, here, sem, (to * 2 + core, z))

    def expert_have(m):
        for cc in (pc.sib, xs, ys + 1, ds, ds + 1):
            arrived(mats(m, cc), re.at[m * nctx + cc])
        own_e[m].wait()

    expert_spread(2)
    have(1)
    for hd in range(heads):
        cols = slice(hd * HEAD, (hd + 1) * HEAD)
        qs[:, cols] = rope(dot(xav, wq[:, cols]), cos, sin).astype(BF16)
    onward(2)
    expert_spread(0)
    expert_spread(1)
    for k in range(1, nch):
        other = pl.ds(pl.multiple_of(((chip + nch - k) % nch) * t2, t2), t2)
        arrived(kv.at[other], rkvf.at[k])

    keys = nch * t2
    scale = HEAD ** -0.5
    ok = lax.broadcasted_iota(jnp.int32, (t2, keys), 1) <= (
        chip * t2 + lax.broadcasted_iota(jnp.int32, (t2, keys), 0)
    )
    lane = lax.broadcasted_iota(jnp.int32, (t2, 128), 1)
    lane0 = lax.broadcasted_iota(jnp.int32, (t0, 128), 1)
    lses[...] = jnp.zeros((t2, 128), F32)

    def head_forward(hd, carry):
        cols = pl.ds(pl.multiple_of(hd * HEAD, HEAD), HEAD)
        s = dot_t(qs[:, cols], kv[:, 0:HEAD]) * scale
        s = jnp.where(ok, s, -1e30)
        m = jnp.max(s, axis=-1, keepdims=True)
        e = jnp.exp(s - m)
        total = jnp.sum(e, axis=-1, keepdims=True)
        lses[...] = jnp.where(lane == hd, m + jnp.log(total), lses[...])
        p = (e * (1.0 / total)).astype(BF16)
        obs[:, cols] = dot(p, kv[:, HEAD:]).astype(BF16)
        return carry

    lax.fori_loop(0, heads, head_forward, 0)
    expert_onward(2)
    have(2)
    part[...] = dot_t(obs[...], wb[...])
    snd.start(part.at[sib0], pget, rfw.at[1], sib)
    arrived(pget, rfw.at[1])
    h1 = h_ref[...].astype(F32) + part[mine0] + pget[...]
    h1s[...] = h1
    xmv = (h1 * rms(h1, width) * gain_m).astype(BF16)
    xm[own] = xmv
    picks = jnp.zeros((128, t0), F32)
    for k in range(TOP):
        row = lax.broadcasted_iota(jnp.int32, (128, t0), 0)
        picks = picks + (routes_ref[k:k + 1, :] == row).astype(F32)
    chosen = picks.T > 0.0
    logits = jnp.where(chosen, dot(xmv, extra), -1e30)
    top = jnp.max(logits, axis=-1, keepdims=True)
    e = jnp.where(chosen, jnp.exp(logits - top), 0.0)
    gts[own] = e / jnp.sum(e, axis=-1, keepdims=True)
    for s in nearest:
        for i, buf in enumerate((xm, gts)):
            snd.start(buf.at[own], buf.at[own], rxm.at[(1 + i) * nz + z], (c, s))
    for i, buf in enumerate((xm, gts)):
        snd.start(buf.at[own], buf.at[own], rxf.at[(1 + i) * nz + z], sib)
    expert_onward(0)
    expert_onward(1)
    for s in nearest:
        here = gr.at[slot(s, core)]
        arrived(here, rxm.at[s])
        snd.start(here, here, rxf.at[s], sib)
    for s in nearest:
        for i, buf in enumerate((xm, gts)):
            here = buf.at[slot(s, core)]
            arrived(here, rxm.at[(1 + i) * nz + s])
            snd.start(here, here, rxf.at[(1 + i) * nz + s], sib)
    for s in range(nz):
        arrived(gr.at[slot(s, 1 - core)], rxf.at[s])
    expert_have(2)

    def rows_first(i, carry):
        at = pl.ds(pl.multiple_of(i * t2, t2), t2)
        ggu[at, 0:fc] = dot(gr[at], we[2]).astype(BF16)
        return carry

    lax.fori_loop(0, nz, rows_first, 0)
    for i, buf in ((1, xm), (2, gts)):
        for s in range(nz):
            arrived(buf.at[slot(s, 1 - core)], rxf.at[i * nz + s])
    expert_have(0)

    def rows_pre(i, carry):
        at = pl.ds(pl.multiple_of(i * t2, t2), t2)
        pre = dot(xm[at], we[0])
        high = pre.astype(BF16)
        ap[at] = high
        ggu[at, fc:] = (pre - high.astype(F32)).astype(BF16)
        return carry

    lax.fori_loop(0, nz, rows_pre, 0)
    expert_have(1)
    snd.drain()

    eloc = cfg_experts(cfg)
    mine_e = z * eloc + (core * eloc) // 2

    def seat(source, at):
        return jnp.where(source > at, source - 1, source)

    def zof(i):
        s = z
        for k in range(nz - 1):
            s = jnp.where(i == k, nearest[nz - 2 - k], s)
        return s

    def blk(i):
        return pl.ds(pl.multiple_of(zof(i) * t2, t2), t2)

    def copy_to_sib(src, dst, ss, rs):
        return pltpu.make_async_remote_copy(
            src_ref=src, dst_ref=dst, send_sem=ss, recv_sem=rs, device_id=sib, device_id_type=MESH
        )

    def copy_to_z(i, src, dst, ss, rs):
        return pltpu.make_async_remote_copy(
            src_ref=src, dst_ref=dst, send_sem=ss, recv_sem=rs, device_id=(c, zof(i)),
            device_id_type=MESH,
        )

    def g_copies(i):
        return (
            copy_to_sib(sibs.at[i], sibr.at[i], sib_s.at[i], sib_r.at[i]),
            copy_to_sib(sgg.at[i], rgg.at[i], sib_s.at[nz + i], sib_r.at[nz + i]),
        )

    def gz_copies(i):
        to = seat(z, zof(i))
        return (
            copy_to_z(i, keep.at[i], zr.at[to], z_s.at[i], z_r.at[to]),
            copy_to_z(i, kgg.at[i], zgg.at[to], z_s.at[nz + i], z_r.at[nz + to]),
        )

    def g_settle(i):
        for cp in g_copies(i):
            cp.wait()
        keep[i] = (keep[i].astype(F32) + sibr[i].astype(F32)).astype(BF16)
        kgg[i] = kgg[i] + rgg[i]

    def rows_mid(i, carry):
        x = xm[blk(i)]
        gate = jnp.sum(jnp.where(lane == mine_e, gts[blk(i)], 0.0), axis=1, keepdims=True)
        pre = ap[blk(i)].astype(F32) + ggu[blk(i), fc:].astype(F32)
        up = dot(x, we[1])
        ga0 = ggu[blk(i), 0:fc].astype(F32)
        sg = 1.0 / (1.0 + jnp.exp(-pre))
        silu = pre * sg
        act = silu * up
        ggc = jnp.sum(act * ga0, axis=1, keepdims=True)
        rowp[...] = jnp.where(lane == mine_e, ggc, 0.0)
        kgg[i] = rowp[mine0]
        sgg[i] = rowp[sib0]
        gact = gate * ga0
        ap[blk(i)] = (gate * act).astype(BF16)
        ggu[blk(i), 0:fc] = (gact * up * sg * (1.0 + pre * (1.0 - sg))).astype(BF16)
        ggu[blk(i), fc:] = (gact * silu).astype(BF16)
        return carry

    def rows_back(i, carry):
        part[...] = dot_t(ggu[blk(i), 0:fc], we[0]) + dot_t(ggu[blk(i), fc:], we[1])
        keep[i] = part[mine0].astype(BF16)
        sibs[i] = part[sib0].astype(BF16)
        for cp in g_copies(i):
            cp.start()

        @pl.when(i > 0)
        def _():
            g_settle(i - 1)
            for cp in gz_copies(i - 1):
                cp.start()

        return carry

    lax.fori_loop(0, nz, rows_mid, 0)

    far = (zq, zb)
    ers = [
        Reduce(
            pc, snd, lambda q, w, m=m: we.at[m, slab_rows(q, w)], efirst.at[m], efx.at[m],
            efy.at[m], esem.at[m], (lambda w, m=m: far[m].at[pl.ds(w * per, per)])
            if m < 2 else None,
        )
        for m in range(3)
    ]
    order = (ers[0].d, ers[0].x, ers[0].y, chip)

    def expert_step(n, rs):
        for one in rs:
            (one.diagonal, one.straight_x, one.straight_y, lambda: None)[n]()

    for n, q in enumerate(order):
        cols = pl.ds(pl.multiple_of(q * 2 * per, 128), 2 * per)
        gw = t_dot(xm[:, cols], ggu[...])
        if n == 0:
            zq[...] = gw[:, :fc].astype(BF16)
            zb[...] = gw[:, fc:].astype(BF16)
        else:
            we[0, cols] = gw[:, :fc].astype(BF16)
            we[1, cols] = gw[:, fc:].astype(BF16)
        expert_step(n, ers[:2])
        if n == 0:
            lax.fori_loop(0, nz, rows_back, 0)
            g_settle(nz - 1)

    def o_copy(i):
        return copy_to_sib(sibs.at[i], sibr.at[i], osib_s.at[i], osib_r.at[i])

    def oz_copy(i):
        to = seat(z, zof(i))
        return copy_to_z(i, okeep.at[i], ozr.at[to], oz_s.at[i], oz_r.at[to])

    def o_settle(i):
        o_copy(i).wait()
        okeep[i] = (okeep[i].astype(F32) + sibr[i].astype(F32)).astype(BF16)

    def rows_out(i, carry):
        part[...] = dot_t(ap[blk(i)], we[2])
        okeep[i] = part[mine0].astype(BF16)
        sibs[i] = part[sib0].astype(BF16)
        o_copy(i).start()

        @pl.when(i > 0)
        def _():
            o_settle(i - 1)
            oz_copy(i - 1).start()

        return carry

    lax.fori_loop(0, nz, rows_out, 0)
    o_settle(nz - 1)

    for n, q in enumerate(order):
        cols = pl.ds(pl.multiple_of(q * 2 * per, 128), 2 * per)
        we[2, cols] = t_dot(gr[:, cols], ap[...]).astype(BF16)
        expert_step(n, ers[2:])

    def fetch(src, room, spot):
        here = room.at[pl.ds(spot // 2 * per, per), pl.ds(spot % 2 * fc, fc)]
        return here, loads.local(src, here)

    def add_far(dst, src):
        here, cp = fetch(src, gr, 0)
        cp.wait()
        add_into(dst, here)

    ers[0].merge(add_far)
    ers[1].merge(add_far)

    gsum = keep[nz - 1].astype(F32)
    ggs = kgg[nz - 1]
    for i in range(nz - 1):
        arrived(zr.at[i], z_r.at[i])
        arrived(zgg.at[i], z_r.at[nz + i])
        gsum = gsum + zr[i].astype(F32)
        ggs = ggs + zgg[i]
    gate = gts[own]
    glog = (gate * (ggs - jnp.sum(gate * ggs, axis=1, keepdims=True))).astype(BF16)
    extra = wk[:, 2 * HEAD:]
    gxm = gsum + dot_t(glog, extra)
    h1 = h1s[...]
    r = rms(h1, width)
    n = h1 * r
    gy = gxm * gain_m
    g1 = cot_ref[...] + r * (gy - n * (jnp.sum(gy * n, axis=1, keepdims=True) * (1.0 / width)))
    ext = t_dot(xm[own], glog) + t_dot((gxm * n).astype(BF16), (lane0 == 9).astype(BF16))
    exts[...] = ext
    ig_ref[...] = g1
    gat[mine0] = g1.astype(BF16)
    snd.start(gat.at[mine0], gat.at[mine0], rmisc.at[0], sib)
    arrived(gat.at[sib0], rmisc.at[0])
    gav = gat[...]
    go = dot(gav, wb[...]).astype(BF16)
    brs = Reduce(pc, snd, lambda q, w: wb.at[slab_rows(q, w)], bfirst, bfx, bfy, bsem)

    def out_grads(k, carry):
        cols = pl.ds(pl.multiple_of(k * 2 * per, 128), 2 * per)
        wb[cols] = t_dot(gat[:, cols], obs[...]).astype(BF16)
        return carry

    lax.fori_loop(0, nch, out_grads, 0)
    brs.diagonal()
    brs.straight_x()
    brs.straight_y()
    obs[...] = go

    cos, sin = cosr[...], sinr[...]
    gkv[...] = jnp.zeros(gkv.shape, F32)

    def one_head(hd, carry):
        cols = pl.ds(pl.multiple_of(hd * HEAD, HEAD), HEAD)
        s = dot_t(qs[:, cols], kv[:, 0:HEAD]) * scale
        pe = jnp.where(ok, jnp.exp(s - jnp.sum(jnp.where(lane == hd, lses[...], 0.0), axis=1, keepdims=True)), 0.0)
        gp = dot_t(obs[:, cols], kv[:, HEAD:])
        delta = jnp.sum(pe * gp, axis=-1, keepdims=True)
        gs = (pe * (gp - delta)).astype(BF16)
        gq = dot(gs, kv[:, 0:HEAD]) * scale
        graw[:, cols] = rope(gq, cos, -sin).astype(BF16)
        gkv[:, 0:HEAD] += t_dot(gs, qs[:, cols])
        gkv[:, HEAD:] += t_dot(pe.astype(BF16), obs[:, cols])
        return carry

    lax.fori_loop(0, heads, one_head, 0)
    gkvb[...] = gkv[...].astype(BF16)
    for k in range(1, nch):
        q = (chip + k) % nch
        snd.start(
            gkvb.at[pl.ds(pl.multiple_of(q * t2, t2), t2)], gkvr.at[k - 1], rkv.at[k],
            (q * 2 + core, z),
        )

    part[...] = dot_t(graw[:, :qw], wq[...])

    def query_grads(k, carry):
        cols = pl.ds(pl.multiple_of(k * 2 * per, 128), 2 * per)
        wq[cols] = t_dot(xa[:, cols], graw[:, 0:qw]).astype(BF16)
        return carry

    lax.fori_loop(0, nch, query_grads, 0)
    qrs = Reduce(
        pc, snd, lambda q, w: wq.at[slab_rows(q, w)], qfirst, qfx, qfy, qsem
    )
    qrs.diagonal()
    qrs.straight_x()
    qrs.straight_y()
    brs.merge(add_into)
    gk = gkv[mine]
    for k in range(1, nch):
        arrived(gkvr.at[k - 1], rkv.at[k])
        gk = gk + gkvr[k - 1].astype(F32)
    graw[:, qw:qw + HEAD] = rope(gk[:, :HEAD] * scale, cos, -sin).astype(BF16)
    graw[:, qw + HEAD:] = gk[:, HEAD:].astype(BF16)
    part[...] += dot_t(graw[:, qw:], wk[:, :2 * HEAD])
    snd.start(part.at[sib0], pget, rmisc.at[1], sib)

    def key_grads(k, carry):
        cols = pl.ds(pl.multiple_of(k * 2 * per, 128), 2 * per)
        wk[cols, 0:2 * HEAD] = t_dot(xa[:, cols], graw[:, qw:]).astype(BF16)
        return carry

    lax.fori_loop(0, nch, key_grads, 0)
    arrived(pget, rmisc.at[1])
    gxa = part[mine0] + pget[...]
    h = h_ref[...].astype(F32)
    r = rms(h, width)
    n = h * r
    gy = gxa * gain_a
    ig_ref[...] += r * (gy - n * (jnp.sum(gy * n, axis=1, keepdims=True) * (1.0 / width)))
    wk[:, 2 * HEAD:] = (
        exts[...] + t_dot((gxa * n).astype(BF16), (lane0 == 8).astype(BF16))
    ).astype(BF16)
    krs = Reduce(
        pc, snd, lambda q, w: wk.at[slab_rows(q, w)], kfirst, kfx, kfy, ksem
    )
    krs.diagonal()
    krs.straight_x()
    krs.straight_y()
    qrs.merge(add_into)
    krs.merge(add_into)
    ers[2].merge(add_far)

    osum = okeep[nz - 1].astype(F32) + h1s[...]
    room = [xm.at[pl.ds(i * t0, t0)] for i in range(nz - 1)]
    got = []
    for i in range(nz - 1):
        arrived(ozr.at[i], oz_r.at[i])
        got.append(loads.local(ozr.at[i], room[i]))
    for i in range(nz - 1):
        got[i].wait()
        osum = osum + room[i][...].astype(F32)
    out_ref[...] = osum

    def piece(q, w):
        return pl.ds(pl.multiple_of((chip * 2 + w) * per + q * rp, 16), rp)

    groups = (
        (brs, lambda rows: wb.at[rows], zrb, rzb, fb, frb),
        (qrs, lambda rows: wq.at[rows], zrq, rzq, fq, frq),
        (krs, lambda rows: wk.at[rows], zrk, rzk, fk, frk),
    )
    for rs, at, zrecv, rz, _, _ in groups:
        rs.wait()
        for w in range(2):
            dst = rs.slab(chip, w)
            dst[...] = (
                dst[...].astype(F32) + rs.fx[w].astype(F32) + rs.fy[w].astype(F32)
            ).astype(BF16)
        for q in nearest[::-1]:
            to = seat(z, q)
            for w in range(2):
                snd.start(at(piece(q, w)), zrecv.at[to, w], rz.at[2 * to + w], (c, q))

    e_own = []
    for m in range(3):
        ers[m].wait()
        got = [
            fetch(src.at[m, w], room, 2 * m + w)
            for src, room in ((efx, gr), (efy, xm)) for w in range(2)
        ]
        for _, cp in got:
            cp.wait()
        for w in range(2):
            dst = ers[m].slab(chip, w)
            tot = dst[...].astype(F32) + got[w][0][...].astype(F32)
            dst[...] = (tot + got[2 + w][0][...].astype(F32)).astype(BF16)
        snd.start(ers[m].slab(chip, 1 - core), esibr.at[m], rmisc.at[2 + m], sib)
        e_own.append(loads.local(ers[m].slab(chip, core), (eg_out, eu_out, ed_out)[m].at[core]))
    for k, (rs, at, zrecv, rz, fin, get) in enumerate(groups):
        for w in range(2):
            tot = at(piece(z, w))[...].astype(F32)
            for dz in range(1, nz):
                arrived(zrecv.at[dz - 1, w], rz.at[2 * dz - 2 + w])
                tot = tot + zrecv[dz - 1, w].astype(F32)
            fin[w] = tot
        snd.start(fin.at[1 - core], get, rmisc.at[5 + k], sib)
    for m in range(3):
        arrived(esibr.at[m], rmisc.at[2 + m])
        e_own.append(loads.local(esibr.at[m], (eg_out, eu_out, ed_out)[m].at[1 - core]))

    def half(k, count):
        return pl.ds(pl.multiple_of(k * count, 128), count)

    for k, (out, count, fin, get, off) in enumerate((
        (gwo_out, qw, fb, frb, 0), (gwq_out, qw, fq, frq, 0),
        (gwk_out, HEAD, fk, frk, 0), (gwv_out, HEAD, fk, frk, HEAD),
    )):
        if k < 3:
            arrived(get, rmisc.at[5 + k])
        out[:, half(core, count)] = fin[core, :, off:off + count]
        out[:, half(1 - core, count)] = get[:, off:off + count]
    ext_out[...] = fk[core, :, 2 * HEAD:] + frk[:, 2 * HEAD:]
    for cp in e_own:
        cp.wait()
    for i in range(nz - 1):
        for cp in gz_copies(i):
            cp.wait_send()
        oz_copy(i).wait_send()
    snd.drain()


def cfg_experts(cfg):
    return cfg[7]


def layer_call(cfg, args):
    nctx, nz, width, rp, t0, heads, fc, eloc = cfg
    nch, t2, dp = nctx // 2, 2 * t0, nctx * nz * rp
    qw = heads * HEAD
    kx = 3 * HEAD
    ca = qw + kx
    keys = nch * t2
    rows = nz * t2
    per = nz * rp
    vm = pl.BlockSpec(memory_space=pltpu.VMEM)
    hb = pl.BlockSpec(memory_space=pltpu.HBM)
    sds = jax.ShapeDtypeStruct
    dma = pltpu.SemaphoreType.DMA
    v = pltpu.VMEM
    return pl.pallas_call(
        functools.partial(layer_kernel, cfg),
        out_shape=(
            sds((t0, dp), F32), sds((t0, dp), F32),
            sds((2, per, fc), BF16), sds((2, per, fc), BF16), sds((2, per, fc), BF16),
            sds((rp, 2 * qw), F32), sds((rp, 2 * HEAD), F32), sds((rp, 2 * HEAD), F32),
            sds((rp, 2 * qw), F32), sds((rp, 128), F32),
        ) + (sds((3, 2, per, fc), BF16),) * 3 + (sds((nz - 1, t0, dp), BF16),),
        in_specs=[vm] * 10 + [hb] * 5,
        out_specs=(vm, vm, hb, hb, hb, vm, vm, vm, vm, vm, hb, hb, hb, hb),
        scratch_shapes=[
            v((dp, kx), BF16), v((dp, qw), BF16), v((dp, qw), BF16), v((3, dp, fc), BF16),
            v((nz * 2 * rp, kx), BF16), v((nz * 2 * rp, qw), BF16), v((nz * 2 * rp, qw), BF16),
            v((2, t0, dp), BF16), v((t2, HEAD), F32), v((t2, HEAD), F32), v((128, 128), F32),
            v((t2, qw), BF16), v((keys, 2 * HEAD), BF16), v((t2, 128), F32), v((t2, qw), BF16),
            v((t2, dp), BF16), v((t0, dp), F32),
            v((rows, dp), BF16), v((rows, dp), BF16), v((rows, 128), F32),
            v((rows, 2 * fc), BF16), v((rows, fc), BF16),
            v((nz, t0, dp), BF16), v((nz, t0, dp), BF16), v((nz, t0, dp), BF16),
            v((nz - 1, t0, dp), BF16), v((nz, t0, dp), BF16),
            v((nz, t0, 128), F32), v((nz, t0, 128), F32), v((nz, t0, 128), F32),
            v((nz - 1, t0, 128), F32),
            v((t2, dp), BF16), v((keys, 2 * HEAD), F32), v((keys, 2 * HEAD), BF16),
            v((nch - 1, t2, 2 * HEAD), BF16), v((t2, ca - 128), BF16),
            v((t2, dp), F32), v((t0, dp), F32), v((dp, 128), F32),
            v((3, per, fc), BF16),
            v((2, per, qw), BF16), v((2, per, qw), BF16), v((2, per, qw), BF16),
            v((2, per, qw), BF16), v((2, per, qw), BF16), v((2, per, qw), BF16),
            v((2, per, kx), BF16), v((2, per, kx), BF16), v((2, per, kx), BF16),
            v((nz - 1, 2, rp, qw), BF16), v((nz - 1, 2, rp, qw), BF16),
            v((nz - 1, 2, rp, kx), BF16),
            v((2, rp, qw), F32), v((2, rp, qw), F32), v((2, rp, kx), F32),
            v((rp, qw), F32), v((rp, qw), F32), v((rp, kx), F32),
            v((t2, 128), F32),
            dma((270,)), dma((60,)), dma((nctx * nz,)), dma((nctx * nz,)), dma((nctx * nz,)),
            dma((3 * nctx,)), dma((nz,)), dma((nz,)), dma((nz,)), dma((2,)), dma((3 * nz,)), dma((3 * nz,)),
            dma((2 * nz,)), dma((2 * nz,)), dma((2 * nz,)), dma((2 * nz,)),
            dma((nz,)), dma((nz,)), dma((nz,)), dma((nz,)), dma((8,)), dma((3, 6)), dma((6,)),
            dma((6,)), dma((6,)), dma((nch,)), dma((nch,)), dma((2 * nz,)), dma((2 * nz,)),
            dma((2 * nz,)),
        ],
        compiler_params=pltpu.CompilerParams(
            collective_id=0, has_side_effects=True, vmem_limit_bytes=64 * 2**20
        ),
        name="layer",
    )(*args)


def body(hidden, routes, cot, na, wq, wk, wv, wo, nm, wr, wg, wu, wd):
    nctx, nz = lax.axis_size("ctx"), lax.axis_size("wsh")
    t0, width = hidden.shape[1], hidden.shape[2]
    rp = wq.shape[1]
    eloc, ff = wg.shape[2], wg.shape[3]
    heads = wq.shape[2] // HEAD // 2
    fc = eloc * ff // 2
    cfg = (nctx, nz, width, rp, t0, heads, fc, eloc)
    experts = wr.shape[2]
    pos = np.arange(nctx * t0, dtype=np.float32)
    freq = np.float32(BASE) ** (-np.arange(HEAD // 2, dtype=np.float32) * 2.0 / HEAD)
    ang = pos[:, None] * freq.astype(np.float32)[None, :]
    cos, sin = np.cos(ang), np.sin(ang)
    cosf = jnp.asarray(np.concatenate([cos, cos], axis=1), F32)
    sinf = jnp.asarray(np.concatenate([-sin, sin], axis=1), F32)
    halves = [jnp.transpose(w[0], (1, 0, 2)) for w in (wg, wu, wd)]
    r = layer_call(
        cfg,
        (hidden[0], routes[0, 0].T, cot[0], wq[0], wk[0], wv[0], wo[0], na, nm, wr[0].T, *halves,
         cosf, sinf),
    )
    out, ig, eg, eu, ed, gwq, gwk, gwv, gwo, ext = r[:10]
    back = lambda x: jnp.transpose(x.astype(F32), (1, 0, 2))[None]
    return (
        out[None], ig[None], ext[:, 8][None], gwq[None], gwk[None], gwv[None], gwo[None],
        ext[:, 9][None], ext[:, :experts][None], back(eg), back(eu), back(ed),
    )


def shifted(value, axis, steps):
    count = lax.axis_size(axis)
    pairs = [(source, (source + steps) % count) for source in range(count)]
    return lax.ppermute(value, axis, pairs)


def normalize(hidden_state, gain):
    return (
        hidden_state
        * lax.rsqrt(jnp.mean(hidden_state * hidden_state, axis=-1, keepdims=True) + NORM_EPSILON)
        * gain
    )


def rotary(token_positions, head_size):
    half_size = head_size // 2
    frequency = ROTARY_BASE ** (-jnp.arange(half_size, dtype=jnp.float32) * 2.0 / head_size)
    angles = token_positions.astype(jnp.float32)[:, None] * frequency[None, :]
    return (jnp.cos(angles)[:, None, :], jnp.sin(angles)[:, None, :])


def apply_rotary(values_in, cosine, sine_rows, direction):
    half_size = values_in.shape[-1] // 2
    first_half = values_in[..., :half_size]
    second = values_in[..., half_size:]
    return jnp.concatenate(
        [
            first_half * cosine - direction * second * sine_rows,
            second * cosine + direction * first_half * sine_rows,
        ],
        axis=-1,
    )


def slot_targets(picks_in, matches):
    flat_matches = matches.reshape(-1, matches.shape[-1]).astype(jnp.int32)
    earlier = jnp.cumsum(flat_matches, axis=0) - flat_matches
    return picks_in.reshape(-1) * CAP + jnp.sum(earlier * flat_matches, axis=1)


def score_rows(query_low, key_rows, token_positions):
    total_rows = query_low.shape[0]
    head_size = query_low.shape[2]
    grouped_heads = query_low.reshape(total_rows, key_rows.shape[1], -1, head_size)
    scores = jnp.einsum(
        "qhgd,khd->hgqk", grouped_heads, key_rows, preferred_element_type=jnp.float32
    ) * head_size ** (-0.5)
    allowed = jnp.arange(key_rows.shape[0], dtype=jnp.int32)[None, :] <= token_positions[:, None]
    return (grouped_heads, jnp.where(allowed[None, None], scores, -1e30))


def attend(query_low, key_rows, value_rows, token_positions):
    grouped_heads, scores = score_rows(query_low, key_rows, token_positions)
    highest = jnp.max(scores, axis=-1, keepdims=True)
    log_total = highest + jnp.log(jnp.sum(jnp.exp(scores - highest), axis=-1, keepdims=True))
    weights = jnp.exp(scores - log_total).astype(jnp.bfloat16)
    attended = jnp.einsum("hgqk,khd->qhgd", weights, value_rows, preferred_element_type=jnp.float32)
    return (attended.reshape(query_low.shape[0], -1), log_total)


def attend_grad(query_low, key_rows, value_rows, token_positions, log_total, grad_mixed):
    grouped_heads, scores = score_rows(query_low, key_rows, token_positions)
    score_scale = query_low.shape[-1] ** (-0.5)
    softmax_rows = jnp.exp(scores - log_total)
    weights = softmax_rows.astype(jnp.bfloat16)
    grad_grouped = grad_mixed.reshape(grouped_heads.shape)
    grad_weights = jnp.einsum(
        "qhgd,khd->hgqk", grad_grouped, value_rows, preferred_element_type=jnp.float32
    )
    grad_values = jnp.einsum(
        "hgqk,qhgd->khd", weights, grad_grouped, preferred_element_type=jnp.float32
    )
    row_inner = jnp.sum(softmax_rows * grad_weights, axis=-1, keepdims=True)
    grad_scores = (softmax_rows * (grad_weights - row_inner)).astype(jnp.bfloat16)
    grad_query = (
        jnp.einsum("hgqk,khd->qhgd", grad_scores, key_rows, preferred_element_type=jnp.float32)
        * score_scale
    )
    grad_keys = (
        jnp.einsum("hgqk,qhgd->khd", grad_scores, grouped_heads, preferred_element_type=jnp.float32)
        * score_scale
    )
    return (grad_query.reshape(query_low.shape), grad_keys, grad_values)


def collect_key_grads(grad_keys, grad_values, total_rows):
    cycle_size = lax.axis_size("ctx")
    own_index = lax.axis_index("ctx")
    both_grads = jnp.stack([grad_keys, grad_values])

    def block_piece(block_index):
        return lax.dynamic_slice_in_dim(both_grads, block_index * total_rows, total_rows, 1)

    def cycle_step(step_index, carried):
        moved = shifted(carried.astype(jnp.bfloat16), "ctx", -1).astype(carried.dtype)
        block_index = (own_index + step_index) % cycle_size
        weight_now = jnp.where(step_index < cycle_size, 1.0, 0.0).astype(jnp.float32)
        return moved + weight_now * block_piece(block_index)

    collected = lax.fori_loop(1, cycle_size + 1, cycle_step, block_piece(own_index))
    return (collected[0], collected[1])


def forward_layer(hidden_state, picks_in, dense_set, expert_set):
    gain_attn, query_matrix, key_matrix, value_matrix, output_matrix, gain_moe, router_matrix = (
        dense_set
    )
    gate_w, up_w, down_w = expert_set
    total_rows, model_width = hidden_state.shape
    token_positions = lax.axis_index("ctx") * total_rows + jnp.arange(total_rows, dtype=jnp.int32)
    cosine, sine_rows = rotary(token_positions, HEAD_DIM)
    attention_normed = normalize(hidden_state, gain_attn.astype(jnp.float32)).astype(jnp.bfloat16)
    query_unrotated = jnp.dot(
        attention_normed, query_matrix, preferred_element_type=jnp.float32
    ).reshape(total_rows, QUERY_HEADS, HEAD_DIM)
    key_unrotated = jnp.dot(
        attention_normed, key_matrix, preferred_element_type=jnp.float32
    ).reshape(total_rows, KEY_VALUE_HEADS, HEAD_DIM)
    query_low = apply_rotary(query_unrotated, cosine, sine_rows, 1.0).astype(jnp.bfloat16)
    key_low = apply_rotary(key_unrotated, cosine, sine_rows, 1.0).astype(jnp.bfloat16)
    value_low = (
        jnp.dot(attention_normed, value_matrix, preferred_element_type=jnp.float32)
        .astype(jnp.bfloat16)
        .reshape(total_rows, KEY_VALUE_HEADS, HEAD_DIM)
    )
    key_rows, value_rows = (
        lax.all_gather(key_low, "ctx", axis=0, tiled=True),
        lax.all_gather(value_low, "ctx", axis=0, tiled=True),
    )
    attended, log_total = attend(query_low, key_rows, value_rows, token_positions)
    mixed_reduced = attended.astype(jnp.bfloat16)
    post_attention = hidden_state + lax.dot_general(
        mixed_reduced, output_matrix, (((1,), (1,)), ((), ())), preferred_element_type=jnp.float32
    )
    expert_normed = normalize(post_attention, gain_moe.astype(jnp.float32)).astype(jnp.bfloat16)
    router_logits = jnp.dot(expert_normed, router_matrix, preferred_element_type=jnp.float32)
    expert_count = router_logits.shape[1]
    matches = picks_in[:, :, None] == jnp.arange(expert_count, dtype=jnp.int32)[None, None, :]
    gate_weights = jax.nn.softmax(
        jnp.sum(jnp.where(matches, router_logits[:, None, :], 0.0), axis=-1), axis=-1
    )
    targets = slot_targets(picks_in, matches)
    outgoing = (
        jnp.zeros((expert_count * CAP, model_width), jnp.bfloat16)
        .at[targets]
        .set(jnp.repeat(expert_normed, TOP, axis=0))
    )
    group_count = lax.axis_size("wsh")
    local_count = gate_w.shape[1]
    arrived = lax.all_to_all(
        outgoing.reshape(group_count, local_count, CAP, model_width),
        "wsh",
        split_axis=0,
        concat_axis=0,
        tiled=True,
    )
    gate_pre = jnp.einsum("sjcd,djf->sjcf", arrived, gate_w, preferred_element_type=jnp.float32)
    up_pre = jnp.einsum("sjcd,djf->sjcf", arrived, up_w, preferred_element_type=jnp.float32)
    activations = (jax.nn.silu(gate_pre) * up_pre).astype(jnp.bfloat16)
    produced = jnp.einsum(
        "sjcf,djf->sjcd", activations, down_w, preferred_element_type=jnp.float32
    ).astype(jnp.bfloat16)
    returned = lax.all_to_all(produced, "wsh", split_axis=0, concat_axis=0, tiled=True)
    returned, arrived, gate_pre, up_pre = (returned, arrived, gate_pre, up_pre)
    picked = (
        returned.reshape(-1, model_width)[targets]
        .reshape(total_rows, TOP, model_width)
        .astype(jnp.float32)
    )
    after_moe = post_attention + jnp.sum(gate_weights[:, :, None] * picked, axis=1)
    stored = (
        hidden_state,
        attention_normed,
        query_low,
        key_low,
        value_low,
        log_total,
        mixed_reduced,
        post_attention,
        expert_normed,
        matches,
        gate_weights,
        targets,
        picked,
        arrived,
        gate_pre,
        up_pre,
    )
    return (after_moe, stored, (key_rows, value_rows))


def backward_layer(incoming, stored, dense_set, expert_set, key_rows, value_rows):
    (
        hidden_state,
        attention_normed,
        query_low,
        key_low,
        value_low,
        log_total,
        mixed_reduced,
        post_attention,
        expert_normed,
        matches,
        gate_weights,
        targets,
        picked,
        arrived,
        gate_pre,
        up_pre,
    ) = stored
    gain_attn, query_matrix, key_matrix, value_matrix, output_matrix, gain_moe, router_matrix = (
        dense_set
    )
    gate_w, up_w, down_w = expert_set
    total_rows, model_width = hidden_state.shape
    token_positions = lax.axis_index("ctx") * total_rows + jnp.arange(total_rows, dtype=jnp.int32)
    cosine, sine_rows = rotary(token_positions, HEAD_DIM)
    grad_y = (gate_weights[:, :, None] * incoming[:, None, :]).astype(jnp.bfloat16)
    grad_gates = jnp.sum(incoming[:, None, :] * picked, axis=-1)
    grad_chosen = gate_weights * (
        grad_gates - jnp.sum(gate_weights * grad_gates, axis=-1, keepdims=True)
    )
    grad_logits = jnp.sum(jnp.where(matches, grad_chosen[:, :, None], 0.0), axis=1).astype(
        jnp.bfloat16
    )
    slot_total = arrived.shape[0] * arrived.shape[1] * arrived.shape[2]
    outgoing = (
        jnp.zeros((slot_total, model_width), jnp.bfloat16)
        .at[targets]
        .set(grad_y.reshape(-1, model_width))
    )
    grad_arrived = lax.all_to_all(
        outgoing.reshape(arrived.shape), "wsh", split_axis=0, concat_axis=0, tiled=True
    )
    grad_acts = jnp.einsum(
        "sjcd,djf->sjcf", grad_arrived, down_w, preferred_element_type=jnp.float32
    )
    sigmoid_gate = jax.nn.sigmoid(gate_pre)
    silu_gate = jax.nn.silu(gate_pre)
    activations = (silu_gate * up_pre).astype(jnp.bfloat16)
    grad_gate = (
        grad_acts * up_pre * sigmoid_gate * (1.0 + gate_pre * (1.0 - sigmoid_gate))
    ).astype(jnp.bfloat16)
    grad_up = (grad_acts * silu_gate).astype(jnp.bfloat16)
    grad_rows = (
        jnp.einsum("sjcf,djf->sjcd", grad_gate, gate_w, preferred_element_type=jnp.float32)
        + jnp.einsum("sjcf,djf->sjcd", grad_up, up_w, preferred_element_type=jnp.float32)
    ).astype(jnp.bfloat16)
    grad_back = lax.all_to_all(grad_rows, "wsh", split_axis=0, concat_axis=0, tiled=True)
    expert_grads = (
        lax.psum_scatter(
            jnp.einsum(
                "sjcd,sjcf->djf", arrived, grad_gate, preferred_element_type=jnp.float32
            ).astype(jnp.bfloat16),
            "ctx",
            scatter_dimension=0,
            tiled=True,
        ).astype(jnp.float32),
        lax.psum_scatter(
            jnp.einsum(
                "sjcd,sjcf->djf", arrived, grad_up, preferred_element_type=jnp.float32
            ).astype(jnp.bfloat16),
            "ctx",
            scatter_dimension=0,
            tiled=True,
        ).astype(jnp.float32),
        lax.psum_scatter(
            jnp.einsum(
                "sjcd,sjcf->djf", grad_arrived, activations, preferred_element_type=jnp.float32
            ).astype(jnp.bfloat16),
            "ctx",
            scatter_dimension=0,
            tiled=True,
        ).astype(jnp.float32),
    )
    returned_rows = (
        grad_back.reshape(-1, model_width)[targets]
        .reshape(total_rows, TOP, model_width)
        .astype(jnp.float32)
    )
    grad_normed_moe = jnp.sum(returned_rows, axis=1) + lax.dot_general(
        grad_logits, router_matrix, (((1,), (1,)), ((), ())), preferred_element_type=jnp.float32
    )
    router_term = jnp.einsum(
        "td,te->de", expert_normed, grad_logits, preferred_element_type=jnp.float32
    )
    unused_moe, pull_moe = jax.vjp(normalize, post_attention, gain_moe.astype(jnp.float32))
    grad_after_norm, gain_moe_term = pull_moe(grad_normed_moe)
    grad_after_attn = incoming + grad_after_norm
    grad_attn = grad_after_attn.astype(jnp.bfloat16)
    out_term = jnp.einsum("td,tj->dj", grad_attn, mixed_reduced, preferred_element_type=jnp.float32)
    grad_mixed = jnp.dot(grad_attn, output_matrix, preferred_element_type=jnp.float32).astype(
        jnp.bfloat16
    )
    grad_query, grad_keys, grad_values = attend_grad(
        query_low, key_rows, value_rows, token_positions, log_total, grad_mixed
    )
    grad_key, grad_value = collect_key_grads(grad_keys, grad_values, total_rows)
    grad_query_raw = (
        apply_rotary(grad_query, cosine, sine_rows, -1.0)
        .reshape(total_rows, -1)
        .astype(jnp.bfloat16)
    )
    grad_key_raw = (
        apply_rotary(grad_key, cosine, sine_rows, -1.0).reshape(total_rows, -1).astype(jnp.bfloat16)
    )
    grad_value_raw = grad_value.reshape(total_rows, -1).astype(jnp.bfloat16)
    contract_last = (((1,), (1,)), ((), ()))
    grad_normed_attn = lax.dot_general(
        grad_query_raw, query_matrix, contract_last, preferred_element_type=jnp.float32
    )
    grad_normed_attn = grad_normed_attn + lax.dot_general(
        grad_key_raw, key_matrix, contract_last, preferred_element_type=jnp.float32
    )
    grad_normed_attn = grad_normed_attn + lax.dot_general(
        grad_value_raw, value_matrix, contract_last, preferred_element_type=jnp.float32
    )
    query_term = jnp.einsum(
        "td,tf->df", attention_normed, grad_query_raw, preferred_element_type=jnp.float32
    )
    key_term = jnp.einsum(
        "td,tf->df", attention_normed, grad_key_raw, preferred_element_type=jnp.float32
    )
    value_term = jnp.einsum(
        "td,tf->df", attention_normed, grad_value_raw, preferred_element_type=jnp.float32
    )
    unused_attn, pull_attn = jax.vjp(normalize, hidden_state, gain_attn.astype(jnp.float32))
    grad_before, gain_attn_term = pull_attn(grad_normed_attn)
    layer_grads = (
        lax.psum_scatter(gain_attn_term, ("ctx", "wsh"), scatter_dimension=0, tiled=True),
        lax.psum_scatter(query_term, ("ctx", "wsh"), scatter_dimension=0, tiled=True),
        lax.psum_scatter(key_term, ("ctx", "wsh"), scatter_dimension=0, tiled=True),
        lax.psum_scatter(value_term, ("ctx", "wsh"), scatter_dimension=0, tiled=True),
        lax.psum_scatter(out_term, ("ctx", "wsh"), scatter_dimension=0, tiled=True),
        lax.psum_scatter(gain_moe_term, ("ctx", "wsh"), scatter_dimension=0, tiled=True),
        lax.psum_scatter(router_term, ("ctx", "wsh"), scatter_dimension=0, tiled=True),
    )
    return (grad_after_attn + grad_before, layer_grads, expert_grads)


def plain_body(
    hidden_in,
    routes,
    cotangent,
    norm_attn,
    w_query,
    key_projection,
    value_projection,
    w_out,
    norm_moe,
    w_router,
    w_gate,
    w_up,
    w_down,
):
    hidden_state = hidden_in[0].astype(jnp.float32)
    layer_number = 0
    dense_set = (
        lax.all_gather(norm_attn[layer_number], ("ctx", "wsh"), axis=0, tiled=True),
        lax.all_gather(w_query[layer_number], ("ctx", "wsh"), axis=0, tiled=True),
        lax.all_gather(key_projection[layer_number], ("ctx", "wsh"), axis=0, tiled=True),
        lax.all_gather(value_projection[layer_number], ("ctx", "wsh"), axis=0, tiled=True),
        lax.all_gather(w_out[layer_number], ("ctx", "wsh"), axis=0, tiled=True),
        lax.all_gather(norm_moe[layer_number], ("ctx", "wsh"), axis=0, tiled=True),
        lax.all_gather(w_router[layer_number], ("ctx", "wsh"), axis=0, tiled=True),
    )
    expert_set = (
        lax.all_gather(w_gate[layer_number], "ctx", axis=0, tiled=True),
        lax.all_gather(w_up[layer_number], "ctx", axis=0, tiled=True),
        lax.all_gather(w_down[layer_number], "ctx", axis=0, tiled=True),
    )
    hidden_state, stored, gathered = forward_layer(
        hidden_state, routes[layer_number, 0], dense_set, expert_set
    )
    records = [(stored, None, None, None)]
    incoming = cotangent[0]
    dense_grads = []
    expert_grads = []
    layer_number = 0
    stored, dense_set, expert_set, gathered = records[layer_number]
    dense_set = (
        lax.all_gather(norm_attn[layer_number], ("ctx", "wsh"), axis=0, tiled=True),
        lax.all_gather(w_query[layer_number], ("ctx", "wsh"), axis=0, tiled=True),
        lax.all_gather(key_projection[layer_number], ("ctx", "wsh"), axis=0, tiled=True),
        lax.all_gather(value_projection[layer_number], ("ctx", "wsh"), axis=0, tiled=True),
        lax.all_gather(w_out[layer_number], ("ctx", "wsh"), axis=0, tiled=True),
        lax.all_gather(norm_moe[layer_number], ("ctx", "wsh"), axis=0, tiled=True),
        lax.all_gather(w_router[layer_number], ("ctx", "wsh"), axis=0, tiled=True),
    )
    expert_set = (
        lax.all_gather(w_gate[layer_number], "ctx", axis=0, tiled=True),
        lax.all_gather(w_up[layer_number], "ctx", axis=0, tiled=True),
        lax.all_gather(w_down[layer_number], "ctx", axis=0, tiled=True),
    )
    gathered = (
        lax.all_gather(stored[3], "ctx", axis=0, tiled=True),
        lax.all_gather(stored[4], "ctx", axis=0, tiled=True),
    )
    incoming, layer_grads, layer_expert = backward_layer(
        incoming, stored, dense_set, expert_set, gathered[0], gathered[1]
    )
    dense_grads.insert(0, layer_grads)
    expert_grads.insert(0, layer_expert)
    stacked_dense = [
        jnp.stack([grads_item[position] for grads_item in dense_grads]) for position in range(7)
    ]
    stacked_expert = [
        jnp.stack([grads_item[position] for grads_item in expert_grads]) for position in range(3)
    ]
    return (
        hidden_state[None],
        incoming[None],
        stacked_dense[0],
        stacked_dense[1],
        stacked_dense[2],
        stacked_dense[3],
        stacked_dense[4],
        stacked_dense[5],
        stacked_dense[6],
        stacked_expert[0],
        stacked_expert[1],
        stacked_expert[2],
    )


def solution(mesh):
    return jax.shard_map(
        body if mesh.shape["ctx"] == 8 and mesh.shape["wsh"] == 4 else plain_body,
        mesh=mesh,
        in_specs=(
            P("wsh", "ctx", None),
            P(None, "wsh", "ctx", None),
            P("wsh", "ctx", None),
            P(None, ("ctx", "wsh")),
            P(None, ("ctx", "wsh"), None),
            P(None, ("ctx", "wsh"), None),
            P(None, ("ctx", "wsh"), None),
            P(None, ("ctx", "wsh"), None),
            P(None, ("ctx", "wsh")),
            P(None, ("ctx", "wsh"), None),
            P(None, "ctx", "wsh", None),
            P(None, "ctx", "wsh", None),
            P(None, "ctx", "wsh", None),
        ),
        out_specs=(
            P("wsh", "ctx", None),
            P("wsh", "ctx", None),
            P(None, ("ctx", "wsh")),
            P(None, ("ctx", "wsh"), None),
            P(None, ("ctx", "wsh"), None),
            P(None, ("ctx", "wsh"), None),
            P(None, ("ctx", "wsh"), None),
            P(None, ("ctx", "wsh")),
            P(None, ("ctx", "wsh"), None),
            P(None, "ctx", "wsh", None),
            P(None, "ctx", "wsh", None),
            P(None, "ctx", "wsh", None),
        ),
        check_vma=False,
    )
```

```python
import functools
import jax
import jax.numpy as jnp
import numpy as np
from jax import lax
from jax.experimental import pallas as pl
from jax.experimental.pallas import tpu as pltpu
from jax.sharding import PartitionSpec as P

QUERY_HEADS = 12
KEY_VALUE_HEADS = 2
HEAD_DIM = 128
CAP = 128
NORM_EPSILON = 1e-06
ROTARY_BASE = 1000000.0
MESH = pl.DeviceIdType.MESH
HEAD = 128
TOP = 4
EPS = 1e-06
BASE = 1000000.0
F32 = jnp.float32
BF16 = jnp.bfloat16


def dot(a, b):
    return lax.dot_general(a, b, (((1,), (0,)), ((), ())), preferred_element_type=F32)


def dot_t(a, b):
    return lax.dot_general(a, b, (((1,), (1,)), ((), ())), preferred_element_type=F32)


def t_dot(a, b):
    return lax.dot_general(a, b, (((0,), (0,)), ((), ())), preferred_element_type=F32)


class Place:
    def __init__(self, nctx, nz):
        self.nctx, self.nz, self.nch = nctx, nz, nctx // 2
        self.c = lax.axis_index("ctx")
        self.z = lax.axis_index("wsh")
        self.chip = self.c // 2
        self.core = self.c % 2
        self.sib = self.chip * 2 + 1 - self.core
        self.square = self.nch == 4

    def xchip(self):
        return self.chip + 1 - 2 * (self.chip % 2)

    def ychip(self):
        return (self.chip + 2) % 4

    def near(self, k):
        s = 0
        for here in range(self.nz):
            order = sorted(
                (v for v in range(self.nz) if v != here),
                key=lambda v: (abs(v - here), 2 * v // self.nz != 2 * here // self.nz),
            )
            s = jnp.where(self.z == here, order[k - 1], s)
        return s

    def zto(self, dz):
        return (self.z + dz) % self.nz

    def zfrom(self, dz):
        return (self.z + self.nz - dz) % self.nz


class Sends:
    def __init__(self, sems, count):
        self.sems, self.count, self.used, self.live = sems, count, 0, []

    def start(self, src, dst, rsem, dev, when=None):
        assert self.used < self.count
        cp = pltpu.make_async_remote_copy(
            src_ref=src,
            dst_ref=dst,
            send_sem=self.sems.at[self.used],
            recv_sem=rsem,
            device_id=dev,
            device_id_type=MESH,
        )
        if when is None:
            cp.start()
        else:
            pl.when(when)(cp.start)
        self.used += 1
        self.live.append((cp, when))

    def local(self, src, dst):
        assert self.used < self.count
        cp = pltpu.make_async_copy(src, dst, self.sems.at[self.used])
        cp.start()
        self.used += 1
        return cp

    def take(self):
        live, self.live = self.live, []
        return live

    def drain(self, live=None):
        for cp, when in self.take() if live is None else live:
            if when is None:
                cp.wait_send()
            else:
                pl.when(when)(cp.wait_send)


def arrived(ref, sem):
    pltpu.make_async_copy(ref, ref, sem).wait()


def greet(pc):
    bar = pltpu.get_barrier_semaphore()
    for k in range(1, pc.nctx):
        to = ((pc.c + k) % pc.nctx, pc.z)
        pl.semaphore_signal(bar, inc=1, device_id=to, device_id_type=MESH)
    for k in range(1, pc.nz):
        pl.semaphore_signal(bar, inc=1, device_id=(pc.c, pc.zto(k)), device_id_type=MESH)
    return lambda: pl.semaphore_wait(bar, pc.nctx + pc.nz - 2)


def rms(x, width):
    return lax.rsqrt(jnp.sum(x * x, axis=-1, keepdims=True) * (1.0 / width) + EPS)


def gain_row(extra, lane):
    pick = (lax.broadcasted_iota(jnp.int32, (16, extra.shape[1]), 1) == lane).astype(BF16)
    return dot_t(pick, extra)[0:1]


def rope(x, cos, sin):
    return x * cos + pltpu.roll(x, HEAD // 2, 1) * sin


class Reduce:
    def __init__(self, pc, snd, slab, first, fx, fy, sems):
        self.pc, self.snd, self.slab = pc, snd, slab
        self.first, self.fx, self.fy, self.sems = first, fx, fy, sems
        self.x, self.y, self.d = pc.xchip(), pc.ychip(), 3 - pc.chip

    def to(self, chip):
        return (chip * 2 + self.pc.core, self.pc.z)

    def diagonal(self):
        self.snd.start(self.slab(self.d, 0), self.first.at[0], self.sems.at[0], self.to(self.x))
        self.snd.start(self.slab(self.d, 1), self.first.at[1], self.sems.at[1], self.to(self.y))

    def straight_x(self):
        self.snd.start(self.slab(self.x, 0), self.fx.at[0], self.sems.at[2], self.to(self.x))

    def straight_y(self):
        self.snd.start(self.slab(self.y, 1), self.fy.at[1], self.sems.at[5], self.to(self.y))

    def merge(self, add):
        arrived(self.first.at[0], self.sems.at[0])
        add(self.slab(self.y, 0), self.first.at[0])
        self.snd.start(self.slab(self.y, 0), self.fy.at[0], self.sems.at[4], self.to(self.y))
        arrived(self.first.at[1], self.sems.at[1])
        add(self.slab(self.x, 1), self.first.at[1])
        self.snd.start(self.slab(self.x, 1), self.fx.at[1], self.sems.at[3], self.to(self.x))

    def wait(self):
        for w in range(2):
            arrived(self.fx.at[w], self.sems.at[2 + w])
            arrived(self.fy.at[w], self.sems.at[4 + w])


def add_into(dst, src):
    dst[...] = (dst[...].astype(F32) + src[...].astype(F32)).astype(BF16)


def layer_kernel(
    cfg,
    h_ref, routes_ref, cot_ref, wq_ref, wk_ref, wv_ref, wo_ref, ga_ref, gm_ref, wr_ref,
    eg_ref, eu_ref, ed_ref,
    cos_in, sin_in,
    out_ref, ig_ref, eg_out, eu_out, ed_out, gwq_out, gwk_out, gwv_out, gwo_out, gna_out, gnm_out, gwr_out,
    efirst, efx, efy, ozr,
    wk, wq, wb, we, zk, zq, zb, hbuf, cosr, sinr, square,
    qs, kv, lses, obs, xa, h1s, xm, gr, gts,
    ggu, ap, keep, sibs, sibr, zr, okeep, kgg, sgg, rgg, zgg, gtt,
    gat, gkv, gkvb, gkvr, graw, part, pget, exts,
    esibr,
    bfirst, bfx, bfy, qfirst, qfx, qfy, kfirst, kfx, kfy,
    zrb, zrq, zrk, fb, fq, fk, frb, frq, frk, rowp,
    ssem, lsem, rwk, rwq, rwb, re, rzk_, rzq_, rzb_, rfw, rxm, rxf,
    sib_s, sib_r, z_s, z_r, osib_s, osib_r, oz_s, oz_r, rmisc, esem, bsem,
    qsem, ksem, rkv, rkvf, rzb, rzq, rzk,
):
    nctx, nz, width, rp, t0, heads, fc, _ = cfg
    pc = Place(nctx, nz)
    nch = pc.nch
    t2 = 2 * t0
    qw = heads * HEAD
    kw = qw + 2 * HEAD
    kx = wk.shape[1]
    dp = wk.shape[0]
    core, z, c, chip = pc.core, pc.z, pc.c, pc.chip
    per = nz * rp
    met = greet(pc)
    snd = Sends(ssem, ssem.shape[0])
    loads = Sends(lsem, lsem.shape[0])
    sib = (pc.sib, z)
    mine = pl.ds(pl.multiple_of(chip * t2, t2), t2)
    mine0 = pl.ds(pl.multiple_of(core * t0, t0), t0)
    sib0 = pl.ds(pl.multiple_of((1 - core) * t0, t0), t0)
    xs, ys, ds = pc.xchip() * 2, pc.ychip() * 2, (3 - chip) * 2
    nearest = [pc.near(k) for k in range(1, nz)]

    def line_send(src, sem, order):
        for s in order:
            snd.start(src, src, sem, (c, s))

    def rows(cc, s):
        return pl.ds(pl.multiple_of((cc * nz + s) * rp, 16), rp)

    def slot(s, k):
        return pl.ds(pl.multiple_of(s * t2 + k * t0, t0), t0)

    def slot8(s, k):
        return pl.ds(pl.multiple_of((s * 2 + k) * 8, 8), 8)

    def both_parts(s):
        return pl.ds(pl.multiple_of(s * 2 * rp, 16), 2 * rp)

    def part_of(s, k):
        return pl.ds(pl.multiple_of((s * 2 + k) * rp, 16), rp)

    def slab_rows(q, w):
        return pl.ds(pl.multiple_of((q * 2 + w) * per, 16), per)

    tables = [loads.local(cos_in.at[mine], cosr), loads.local(sin_in.at[mine], sinr)]
    square[...] = jnp.zeros(square.shape, F32)
    experts = wr_ref.shape[0]
    square[0:experts, 0:rp] = wr_ref[...].astype(F32)
    square[8:9, 0:rp] = ga_ref[...].astype(F32)
    square[9:10, 0:rp] = gm_ref[...].astype(F32)
    ex = square[...].T[0:rp].astype(BF16)
    for k in range(2):
        at = part_of(z, k)
        zk[at, 0:HEAD] = wk_ref[:, k * HEAD:(k + 1) * HEAD]
        zk[at, HEAD:2 * HEAD] = wv_ref[:, k * HEAD:(k + 1) * HEAD]
        zk[at, 2 * HEAD:] = ex
        zq[at] = wq_ref[:, k * qw:(k + 1) * qw]
        zb[at] = wo_ref[:, k * qw:(k + 1) * qw]
    own = slot(z, core)
    gr[own] = cot_ref[...].astype(BF16)
    hbuf[core] = h_ref[...]
    met()

    def spread(src, dst, rs, s):
        here = dst.at[rows(c, s)]
        sem = rs.at[c * nz + s]
        for q in (pc.xchip(), pc.ychip()):
            for k in range(2):
                snd.start(src.at[part_of(s, k)], here, sem, (q * 2 + k, z))
        snd.start(src.at[part_of(s, 1 - core)], here, sem, sib)

    def forward(dst, rs, s):
        for source, to in ((ys, pc.xchip()), (xs + 1, pc.ychip())):
            here = dst.at[rows(source, s)]
            sem = rs.at[source * nz + s]
            arrived(here, sem)
            snd.start(here, here, sem, (to * 2 + core, z))

    def settle(dst, rs):
        for cc in (pc.sib, xs, ys + 1, ds, ds + 1):
            for s in range(nz):
                arrived(dst.at[rows(cc, s)], rs.at[cc * nz + s])

    packs = ((zk, rzk_, wk, rwk), (zq, rzq_, wq, rwq), (zb, rzb_, wb, rwb))
    for ref, rs, _, _ in packs:
        line_send(ref.at[both_parts(z)], rs.at[z], nearest)
    line_send(gr.at[own], rxm.at[z], nearest)
    keeps = ([], [], [])
    snd.start(hbuf.at[core], hbuf.at[core], rfw.at[0], sib)
    for (ref, _, dst, rs), kept in zip(packs, keeps):
        spread(ref, dst, rs, z)
        kept.append(loads.local(ref.at[part_of(z, core)], dst.at[rows(c, z)]))
    snd.start(gr.at[own], gr.at[own], rxf.at[z], sib)

    def column(which):
        ref, zs, dst, rs = packs[which]
        for s in nearest:
            arrived(ref.at[both_parts(s)], zs.at[s])
            spread(ref, dst, rs, s)
            keeps[which].append(loads.local(ref.at[part_of(s, core)], dst.at[rows(c, s)]))

    def onward(which):
        _, _, dst, rs = packs[which]
        for s in [z] + nearest:
            forward(dst, rs, s)

    def have(which):
        _, _, dst, rs = packs[which]
        for cp in keeps[which]:
            cp.wait()
        settle(dst, rs)

    column(0)
    onward(0)
    column(1)
    arrived(hbuf.at[1 - core], rfw.at[0])
    for cp in tables:
        cp.wait()
    have(0)
    cos, sin = cosr[...], sinr[...]
    extra = wk[:, 2 * HEAD:]
    gain_a = gain_row(extra, 8)
    gain_m = gain_row(extra, 9)
    for k in range(2):
        hk = hbuf[k].astype(F32)
        xa[pl.ds(k * t0, t0)] = (hk * rms(hk, width) * gain_a).astype(BF16)
    xav = xa[...]
    kraw = dot(xav, wk[:, :2 * HEAD])
    kv[mine, 0:HEAD] = rope(kraw[:, :HEAD], cos, sin).astype(BF16)
    kv[mine, HEAD:] = kraw[:, HEAD:].astype(BF16)
    for k in range(1, nch):
        snd.start(kv.at[mine], kv.at[mine], rkvf.at[k], (((chip + k) % nch) * 2 + core, z))
    onward(1)
    column(2)

    fh = fc // 2

    def mats(m, j, cc):
        at = pl.ds(pl.multiple_of(cc * per, 16), per)
        return we.at[m, at, pl.ds(j * fh, fh)]

    experts_in = (eg_ref, eu_ref, ed_ref)
    own_e = [
        loads.local(experts_in[m].at[core], we.at[m, pl.ds(pl.multiple_of(c * per, 16), per)])
        for m in range(3)
    ]

    def expert_spread(m, j):
        here = mats(m, j, c)
        sem = re.at[(2 * m + j) * nctx + c]
        half = pl.ds(j * fh, fh)
        for q in (pc.xchip(), pc.ychip()):
            for k in range(2):
                snd.start(experts_in[m].at[k, :, half], here, sem, (q * 2 + k, z))
        snd.start(experts_in[m].at[1 - core, :, half], here, sem, sib)

    def expert_onward(m, j):
        for source, to in ((ys, pc.xchip()), (xs + 1, pc.ychip())):
            here = mats(m, j, source)
            sem = re.at[(2 * m + j) * nctx + source]
            arrived(here, sem)
            snd.start(here, here, sem, (to * 2 + core, z))

    def expert_have(m, j):
        for cc in (pc.sib, xs, ys + 1, ds, ds + 1):
            arrived(mats(m, j, cc), re.at[(2 * m + j) * nctx + cc])
        if j == 0:
            own_e[m].wait()

    units = [(m, j) for j in range(2) for m in (2, 0, 1)]
    dense_sends = snd.take()
    expert_spread(*units[0])
    have(1)
    for hd in range(heads):
        cols = slice(hd * HEAD, (hd + 1) * HEAD)
        qs[:, cols] = rope(dot(xav, wq[:, cols]), cos, sin).astype(BF16)
    onward(2)
    for unit in units[1:]:
        expert_spread(*unit)
    for k in range(1, nch):
        other = pl.ds(pl.multiple_of(((chip + nch - k) % nch) * t2, t2), t2)
        arrived(kv.at[other], rkvf.at[k])

    keys = nch * t2
    scale = HEAD ** -0.5
    ok = lax.broadcasted_iota(jnp.int32, (t2, keys), 1) <= (
        chip * t2 + lax.broadcasted_iota(jnp.int32, (t2, keys), 0)
    )
    lane = lax.broadcasted_iota(jnp.int32, (t2, 128), 1)
    lane0 = lax.broadcasted_iota(jnp.int32, (t0, 128), 1)
    lses[...] = jnp.zeros((t2, 128), F32)

    def head_forward(hd, carry):
        cols = pl.ds(pl.multiple_of(hd * HEAD, HEAD), HEAD)
        s = dot_t(qs[:, cols], kv[:, 0:HEAD]) * scale
        s = jnp.where(ok, s, -1e30)
        m = jnp.max(s, axis=-1, keepdims=True)
        e = jnp.exp(s - m)
        total = jnp.sum(e, axis=-1, keepdims=True)
        lses[...] = jnp.where(lane == hd, m + jnp.log(total), lses[...])
        p = (e * (1.0 / total)).astype(BF16)
        obs[:, cols] = dot(p, kv[:, HEAD:]).astype(BF16)
        return carry

    def tokens_in(i, s):
        buf, at = tokens[i]
        here = buf.at[at(s, core)]
        arrived(here, rxm.at[i * nz + s])
        snd.start(here, here, rxf.at[i * nz + s], sib)

    tokens = ((gr, slot), (xm, slot), (gtt, slot8))
    lax.fori_loop(0, heads, head_forward, 0)
    expert_onward(*units[0])
    have(2)
    part[...] = dot_t(obs[...], wb[...])
    snd.start(part.at[sib0], pget, rfw.at[1], sib)
    arrived(pget, rfw.at[1])
    h1 = h_ref[...].astype(F32) + part[mine0] + pget[...]
    h1s[...] = h1
    xmv = (h1 * rms(h1, width) * gain_m).astype(BF16)
    xm[own] = xmv
    picks = jnp.zeros((128, t0), F32)
    for k in range(TOP):
        row = lax.broadcasted_iota(jnp.int32, (128, t0), 0)
        picks = picks + (routes_ref[k:k + 1, :] == row).astype(F32)
    chosen = picks.T > 0.0
    logits = jnp.where(chosen, dot(xmv, extra), -1e30)
    top = jnp.max(logits, axis=-1, keepdims=True)
    e = jnp.where(chosen, jnp.exp(logits - top), 0.0)
    gts[own] = e / jnp.sum(e, axis=-1, keepdims=True)
    gtt[slot8(z, core)] = gts[own].T[0:8]
    for i in (2, 1):
        buf, at = tokens[i]
        line_send(buf.at[at(z, core)], rxm.at[i * nz + z], nearest[::-1])
        snd.start(buf.at[at(z, core)], buf.at[at(z, core)], rxf.at[i * nz + z], sib)
    for unit in units[1:]:
        expert_onward(*unit)
    for s in nearest:
        tokens_in(0, s)
    for s in nearest:
        for i in (1, 2):
            tokens_in(i, s)
    for s in range(nz):
        arrived(gr.at[slot(s, 1 - core)], rxf.at[s])
    def rows_first(i, carry, j):
        at = pl.ds(pl.multiple_of(i * t2, t2), t2)
        ggu[at, 2 * j * fh:(2 * j + 1) * fh] = dot(
            gr[at], we[2, :, j * fh:(j + 1) * fh]
        ).astype(BF16)
        return carry

    for j in range(2):
        expert_have(2, j)
        lax.fori_loop(0, nz, functools.partial(rows_first, j=j), 0)
    for buf, at, i in ((xm, slot, 1), (gtt, slot8, 2)):
        for s in range(nz):
            arrived(buf.at[at(s, 1 - core)], rxf.at[i * nz + s])
    square[...] = jnp.zeros(square.shape, F32)
    for s in range(nz):
        for k in range(2):
            square[0:8] = gtt[slot8(s, k)]
            gts[slot(s, k)] = square[...].T

    mine128 = pl.ds(pl.multiple_of(core * 128, 128), 128)
    sib128 = pl.ds(pl.multiple_of((1 - core) * 128, 128), 128)
    eloc = cfg_experts(cfg)
    mine_e = z * eloc + (core * eloc) // 2

    def seat(source, at):
        return jnp.where(source > at, source - 1, source)

    def zof(i):
        s = z
        for k in range(nz - 1):
            s = jnp.where(i == k, nearest[nz - 2 - k], s)
        return s

    def blk(i):
        return pl.ds(pl.multiple_of(zof(i) * t2, t2), t2)

    def copy_to_sib(src, dst, ss, rs):
        return pltpu.make_async_remote_copy(
            src_ref=src, dst_ref=dst, send_sem=ss, recv_sem=rs, device_id=sib, device_id_type=MESH
        )

    def copy_to_z(i, src, dst, ss, rs):
        return pltpu.make_async_remote_copy(
            src_ref=src, dst_ref=dst, send_sem=ss, recv_sem=rs, device_id=(c, zof(i)),
            device_id_type=MESH,
        )

    def g_copies(i):
        return (
            copy_to_sib(sibs.at[i], sibr.at[i], sib_s.at[i], sib_r.at[i]),
            copy_to_sib(sgg.at[i], rgg.at[i], sib_s.at[nz + i], sib_r.at[nz + i]),
        )

    def gz_copies(i):
        to = seat(z, zof(i))
        return (
            copy_to_z(i, keep.at[i], zr.at[to], z_s.at[i], z_r.at[to]),
            copy_to_z(i, kgg.at[i], zgg.at[to], z_s.at[nz + i], z_r.at[nz + to]),
        )

    def g_settle(i):
        for cp in g_copies(i):
            cp.wait()
        keep[i] = (keep[i].astype(F32) + sibr[i].astype(F32)).astype(BF16)
        kgg[i] = kgg[i] + rgg[i]

    def rows_mid(i, carry, j):
        x = xm[blk(i)]
        cols = slice(j * fh, (j + 1) * fh)
        first = slice(2 * j * fh, (2 * j + 1) * fh)
        gate = jnp.sum(jnp.where(lane == mine_e, gts[blk(i)], 0.0), axis=1, keepdims=True)
        pre = dot(x, we[0, :, cols])
        up = dot(x, we[1, :, cols])
        ga0 = ggu[blk(i), first].astype(F32)
        sg = 1.0 / (1.0 + jnp.exp(-pre))
        silu = pre * sg
        act = silu * up
        ggc = jnp.sum(act * ga0, axis=1, keepdims=True)
        rowp[...] = jnp.where(lane == mine_e, ggc, 0.0).T[0:8]
        if j == 0:
            kgg[i] = rowp[:, mine128]
            sgg[i] = rowp[:, sib128]
        else:
            kgg[i] += rowp[:, mine128]
            sgg[i] += rowp[:, sib128]
        gact = gate * ga0
        ap[blk(i), cols] = (gate * act).astype(BF16)
        ggu[blk(i), first] = (gact * up * sg * (1.0 + pre * (1.0 - sg))).astype(BF16)
        ggu[blk(i), (2 * j + 1) * fh:(2 * j + 2) * fh] = (gact * silu).astype(BF16)
        return carry

    def rows_back(i, carry):
        total = None
        for k in range(4):
            term = dot_t(
                ggu[blk(i), k * fh:(k + 1) * fh], we[k % 2, :, k // 2 * fh:(k // 2 + 1) * fh]
            )
            total = term if total is None else total + term
        part[...] = total
        keep[i] = part[mine0].astype(BF16)
        sibs[i] = part[sib0].astype(BF16)
        for cp in g_copies(i):
            cp.start()

        @pl.when(i > 0)
        def _():
            g_settle(i - 1)
            for cp in gz_copies(i - 1):
                cp.start()

        return carry

    far = (zq, zb)
    ers = [
        Reduce(
            pc, snd, lambda q, w, m=m: we.at[m, slab_rows(q, w)], efirst.at[m], efx.at[m],
            efy.at[m], esem.at[m],
        )
        for m in range(3)
    ]
    order = (ers[0].d, ers[0].x, ers[0].y, chip)

    def chip_cols(q):
        return pl.ds(pl.multiple_of(q * 2 * per, 128), 2 * per)

    row_sends = snd.take()
    for j in range(2):
        expert_have(0, j)
        expert_have(1, j)
        lax.fori_loop(0, nz, functools.partial(rows_mid, j=j), 0)
        if j == 0:
            snd.drain(dense_sends)
        half = pl.ds(j * fh, fh)
        gw = t_dot(xm[:, chip_cols(order[0])], ggu[:, 2 * j * fh:2 * (j + 1) * fh])
        for m in range(2):
            far[m][:, j * fh:(j + 1) * fh] = gw[:, m * fh:(m + 1) * fh].astype(BF16)
            for w, q in ((0, ers[m].x), (1, ers[m].y)):
                snd.start(
                    far[m].at[pl.ds(w * per, per), half], efirst.at[m, w, :, half],
                    esem.at[m, w], ers[m].to(q),
                )
    snd.drain(row_sends)
    lax.fori_loop(0, nz, rows_back, 0)
    g_settle(nz - 1)

    def expert_step(n, rs):
        for one in rs:
            (one.diagonal, one.straight_x, one.straight_y, lambda: None)[n]()

    for n, q in enumerate(order):
        if n == 0:
            continue
        cols = chip_cols(q)
        gw = t_dot(xm[:, cols], ggu[...])
        for k in range(4):
            we[k % 2, cols, k // 2 * fh:(k // 2 + 1) * fh] = gw[:, k * fh:(k + 1) * fh].astype(BF16)
        expert_step(n, ers[:2])

    def o_copy(i):
        return copy_to_sib(sibs.at[i], sibr.at[i], osib_s.at[i], osib_r.at[i])

    def oz_copy(i):
        to = seat(z, zof(i))
        return copy_to_z(i, okeep.at[i], ozr.at[to], oz_s.at[i], oz_r.at[to])

    def o_settle(i):
        o_copy(i).wait()
        okeep[i] = (okeep[i].astype(F32) + sibr[i].astype(F32)).astype(BF16)

    def rows_out(i, carry):
        part[...] = dot_t(ap[blk(i)], we[2])
        okeep[i] = part[mine0].astype(BF16)
        sibs[i] = part[sib0].astype(BF16)
        o_copy(i).start()

        @pl.when(i > 0)
        def _():
            o_settle(i - 1)
            oz_copy(i - 1).start()

        return carry

    lax.fori_loop(0, nz, rows_out, 0)
    o_settle(nz - 1)

    for n, q in enumerate(order):
        cols = pl.ds(pl.multiple_of(q * 2 * per, 128), 2 * per)
        we[2, cols] = t_dot(gr[:, cols], ap[...]).astype(BF16)
        expert_step(n, ers[2:])

    def fetch(src, room, spot):
        here = room.at[pl.ds(spot // 2 * per, per), pl.ds(spot % 2 * fc, fc)]
        return here, loads.local(src, here)

    def add_far(dst, src):
        here, cp = fetch(src, gr, 0)
        cp.wait()
        add_into(dst, here)

    ers[0].merge(add_far)
    ers[1].merge(add_far)

    gsum = keep[nz - 1].astype(F32)
    ggs = kgg[nz - 1]
    for i in range(nz - 1):
        arrived(zr.at[i], z_r.at[i])
        arrived(zgg.at[i], z_r.at[nz + i])
        gsum = gsum + zr[i].astype(F32)
        ggs = ggs + zgg[i]
    square[...] = jnp.zeros(square.shape, F32)
    square[0:8] = ggs
    ggs = square[...].T
    gate = gts[own]
    glog = (gate * (ggs - jnp.sum(gate * ggs, axis=1, keepdims=True))).astype(BF16)
    extra = wk[:, 2 * HEAD:]
    gxm = gsum + dot_t(glog, extra)
    h1 = h1s[...]
    r = rms(h1, width)
    n = h1 * r
    gy = gxm * gain_m
    g1 = cot_ref[...] + r * (gy - n * (jnp.sum(gy * n, axis=1, keepdims=True) * (1.0 / width)))
    ext = t_dot(xm[own], glog) + t_dot((gxm * n).astype(BF16), (lane0 == 9).astype(BF16))
    exts[...] = ext
    ig_ref[...] = g1
    gat[mine0] = g1.astype(BF16)
    snd.start(gat.at[mine0], gat.at[mine0], rmisc.at[0], sib)
    arrived(gat.at[sib0], rmisc.at[0])
    gav = gat[...]
    go = dot(gav, wb[...]).astype(BF16)
    brs = Reduce(pc, snd, lambda q, w: wb.at[slab_rows(q, w)], bfirst, bfx, bfy, bsem)

    def out_grads(k, carry):
        cols = pl.ds(pl.multiple_of(k * 2 * per, 128), 2 * per)
        wb[cols] = t_dot(gat[:, cols], obs[...]).astype(BF16)
        return carry

    lax.fori_loop(0, nch, out_grads, 0)
    brs.diagonal()
    brs.straight_x()
    brs.straight_y()
    obs[...] = go

    cos, sin = cosr[...], sinr[...]
    gkv[...] = jnp.zeros(gkv.shape, F32)

    def one_head(hd, carry):
        cols = pl.ds(pl.multiple_of(hd * HEAD, HEAD), HEAD)
        s = dot_t(qs[:, cols], kv[:, 0:HEAD]) * scale
        pe = jnp.where(ok, jnp.exp(s - jnp.sum(jnp.where(lane == hd, lses[...], 0.0), axis=1, keepdims=True)), 0.0)
        gp = dot_t(obs[:, cols], kv[:, HEAD:])
        delta = jnp.sum(pe * gp, axis=-1, keepdims=True)
        gs = (pe * (gp - delta)).astype(BF16)
        gq = dot(gs, kv[:, 0:HEAD]) * scale
        graw[:, cols] = rope(gq, cos, -sin).astype(BF16)
        gkv[:, 0:HEAD] += t_dot(gs, qs[:, cols])
        gkv[:, HEAD:] += t_dot(pe.astype(BF16), obs[:, cols])
        return carry

    lax.fori_loop(0, heads, one_head, 0)
    gkvb[...] = gkv[...].astype(BF16)
    for k in range(1, nch):
        q = (chip + k) % nch
        snd.start(
            gkvb.at[pl.ds(pl.multiple_of(q * t2, t2), t2)], gkvr.at[k - 1], rkv.at[k],
            (q * 2 + core, z),
        )

    part[...] = dot_t(graw[:, :qw], wq[...])

    def query_grads(k, carry):
        cols = pl.ds(pl.multiple_of(k * 2 * per, 128), 2 * per)
        wq[cols] = t_dot(xa[:, cols], graw[:, 0:qw]).astype(BF16)
        return carry

    lax.fori_loop(0, nch, query_grads, 0)
    qrs = Reduce(
        pc, snd, lambda q, w: wq.at[slab_rows(q, w)], qfirst, qfx, qfy, qsem
    )
    qrs.diagonal()
    qrs.straight_x()
    qrs.straight_y()
    brs.merge(add_into)
    gk = gkv[mine]
    for k in range(1, nch):
        arrived(gkvr.at[k - 1], rkv.at[k])
        gk = gk + gkvr[k - 1].astype(F32)
    graw[:, qw:qw + HEAD] = rope(gk[:, :HEAD] * scale, cos, -sin).astype(BF16)
    graw[:, qw + HEAD:] = gk[:, HEAD:].astype(BF16)
    part[...] += dot_t(graw[:, qw:], wk[:, :2 * HEAD])
    snd.start(part.at[sib0], pget, rmisc.at[1], sib)

    def key_grads(k, carry):
        cols = pl.ds(pl.multiple_of(k * 2 * per, 128), 2 * per)
        wk[cols, 0:2 * HEAD] = t_dot(xa[:, cols], graw[:, qw:]).astype(BF16)
        return carry

    lax.fori_loop(0, nch, key_grads, 0)
    arrived(pget, rmisc.at[1])
    gxa = part[mine0] + pget[...]
    h = h_ref[...].astype(F32)
    r = rms(h, width)
    n = h * r
    gy = gxa * gain_a
    ig_ref[...] += r * (gy - n * (jnp.sum(gy * n, axis=1, keepdims=True) * (1.0 / width)))
    wk[:, 2 * HEAD:] = (
        exts[...] + t_dot((gxa * n).astype(BF16), (lane0 == 8).astype(BF16))
    ).astype(BF16)
    krs = Reduce(
        pc, snd, lambda q, w: wk.at[slab_rows(q, w)], kfirst, kfx, kfy, ksem
    )
    krs.diagonal()
    krs.straight_x()
    krs.straight_y()
    qrs.merge(add_into)
    krs.merge(add_into)
    ers[2].merge(add_far)

    def piece(q, w):
        return pl.ds(pl.multiple_of((chip * 2 + w) * per + q * rp, 16), rp)

    groups = (
        (brs, lambda rows: wb.at[rows], zrb, rzb, fb, frb),
        (qrs, lambda rows: wq.at[rows], zrq, rzq, fq, frq),
        (krs, lambda rows: wk.at[rows], zrk, rzk, fk, frk),
    )

    def column_out(which):
        rs, at, zrecv, rz, _, _ = groups[which]
        rs.wait()
        for w in range(2):
            dst = rs.slab(chip, w)
            dst[...] = (
                dst[...].astype(F32) + rs.fx[w].astype(F32) + rs.fy[w].astype(F32)
            ).astype(BF16)
        for q in nearest[::-1]:
            to = seat(z, q)
            for w in range(2):
                snd.start(at(piece(q, w)), zrecv.at[to, w], rz.at[2 * to + w], (c, q))

    def column_in(which):
        _, at, zrecv, rz, fin, get = groups[which]
        for w in range(2):
            tot = at(piece(z, w))[...].astype(F32)
            for i in range(nz - 1):
                arrived(zrecv.at[i, w], rz.at[2 * i + w])
                tot = tot + zrecv[i, w].astype(F32)
            fin[w] = tot
        snd.start(fin.at[1 - core], get, rmisc.at[5 + which], sib)

    e_own = []
    e_outs = (eg_out, eu_out, ed_out)

    def expert_final(m):
        ers[m].wait()
        got = [
            fetch(src.at[m, w], room, 2 * m + w)
            for src, room in ((efx, gr), (efy, xm)) for w in range(2)
        ]
        for _, cp in got:
            cp.wait()
        for w in range(2):
            dst = ers[m].slab(chip, w)
            tot = dst[...].astype(F32) + got[w][0][...].astype(F32)
            dst[...] = (tot + got[2 + w][0][...].astype(F32)).astype(BF16)
        snd.start(ers[m].slab(chip, 1 - core), esibr.at[m], rmisc.at[2 + m], sib)
        e_own.append(loads.local(ers[m].slab(chip, core), e_outs[m].at[core]))

    column_out(0)
    expert_final(0)
    expert_final(1)
    osum = okeep[nz - 1].astype(F32) + h1s[...]
    base = nz * t2 - (nz - 1) * t0
    room = [xm.at[pl.ds(base + i * t0, t0)] for i in range(nz - 1)]
    got = []
    for i in range(nz - 1):
        arrived(ozr.at[i], oz_r.at[i])
        got.append(loads.local(ozr.at[i], room[i]))
    for i in range(nz - 1):
        got[i].wait()
        osum = osum + room[i][...].astype(F32)
    out_ref[...] = osum
    column_out(1)
    column_in(0)
    column_out(2)
    for m in range(2):
        arrived(esibr.at[m], rmisc.at[2 + m])
        e_own.append(loads.local(esibr.at[m], e_outs[m].at[1 - core]))
    column_in(1)
    expert_final(2)
    column_in(2)
    arrived(esibr.at[2], rmisc.at[4])
    e_own.append(loads.local(esibr.at[2], e_outs[2].at[1 - core]))

    def half(k, count):
        return pl.ds(pl.multiple_of(k * count, 128), count)

    for k, (out, count, fin, get, off) in enumerate((
        (gwo_out, qw, fb, frb, 0), (gwq_out, qw, fq, frq, 0),
        (gwk_out, HEAD, fk, frk, 0), (gwv_out, HEAD, fk, frk, HEAD),
    )):
        if k < 3:
            arrived(get, rmisc.at[5 + k])
        out[:, half(core, count)] = fin[core, :, off:off + count]
        out[:, half(1 - core, count)] = get[:, off:off + count]
    square[...] = jnp.zeros(square.shape, F32)
    square[0:rp] = fk[core, :, 2 * HEAD:] + frk[:, 2 * HEAD:]
    turned = square[...].T
    gwr_out[...] = turned[0:gwr_out.shape[0], 0:rp]
    gna_out[...] = turned[8:9, 0:rp]
    gnm_out[...] = turned[9:10, 0:rp]
    for cp in e_own:
        cp.wait()
    for i in range(nz - 1):
        for cp in gz_copies(i):
            cp.wait_send()
        oz_copy(i).wait_send()
    snd.drain()


def cfg_experts(cfg):
    return cfg[7]


def layer_call(cfg, args):
    nctx, nz, width, rp, t0, heads, fc, eloc = cfg
    nch, t2, dp = nctx // 2, 2 * t0, nctx * nz * rp
    qw = heads * HEAD
    kx = 3 * HEAD
    ca = qw + kx
    keys = nch * t2
    rows = nz * t2
    per = nz * rp
    experts = args[9].shape[0]
    vm = pl.BlockSpec(memory_space=pltpu.VMEM)
    hb = pl.BlockSpec(memory_space=pltpu.HBM)
    sds = jax.ShapeDtypeStruct
    dma = pltpu.SemaphoreType.DMA
    v = pltpu.VMEM
    return pl.pallas_call(
        functools.partial(layer_kernel, cfg),
        out_shape=(
            sds((t0, dp), F32), sds((t0, dp), F32),
            sds((2, per, fc), BF16), sds((2, per, fc), BF16), sds((2, per, fc), BF16),
            sds((rp, 2 * qw), F32), sds((rp, 2 * HEAD), F32), sds((rp, 2 * HEAD), F32),
            sds((rp, 2 * qw), F32), sds((1, rp), F32), sds((1, rp), F32), sds((experts, rp), F32),
        ) + (sds((3, 2, per, fc), BF16),) * 3 + (sds((nz - 1, t0, dp), BF16),),
        in_specs=[vm] * 10 + [hb] * 5,
        out_specs=(vm, vm, hb, hb, hb) + (vm,) * 7 + (hb,) * 4,
        scratch_shapes=[
            v((dp, kx), BF16), v((dp, qw), BF16), v((dp, qw), BF16), v((3, dp, fc), BF16),
            v((nz * 2 * rp, kx), BF16), v((nz * 2 * rp, qw), BF16), v((nz * 2 * rp, qw), BF16),
            v((2, t0, dp), BF16), v((t2, HEAD), F32), v((t2, HEAD), F32), v((128, 128), F32),
            v((t2, qw), BF16), v((keys, 2 * HEAD), BF16), v((t2, 128), F32), v((t2, qw), BF16),
            v((t2, dp), BF16), v((t0, dp), F32),
            v((rows, dp), BF16), v((rows, dp), BF16), v((rows, 128), F32),
            v((rows, 2 * fc), BF16), v((rows, fc), BF16),
            v((nz, t0, dp), BF16), v((nz, t0, dp), BF16), v((nz, t0, dp), BF16),
            v((nz - 1, t0, dp), BF16), v((nz, t0, dp), BF16),
            v((nz, 8, t0), F32), v((nz, 8, t0), F32), v((nz, 8, t0), F32),
            v((nz - 1, 8, t0), F32),
            v((nz * 2 * 8, t0), F32),
            v((t2, dp), BF16), v((keys, 2 * HEAD), F32), v((keys, 2 * HEAD), BF16),
            v((nch - 1, t2, 2 * HEAD), BF16), v((t2, ca - 128), BF16),
            v((t2, dp), F32), v((t0, dp), F32), v((dp, 128), F32),
            v((3, per, fc), BF16),
            v((2, per, qw), BF16), v((2, per, qw), BF16), v((2, per, qw), BF16),
            v((2, per, qw), BF16), v((2, per, qw), BF16), v((2, per, qw), BF16),
            v((2, per, kx), BF16), v((2, per, kx), BF16), v((2, per, kx), BF16),
            v((nz - 1, 2, rp, qw), BF16), v((nz - 1, 2, rp, qw), BF16),
            v((nz - 1, 2, rp, kx), BF16),
            v((2, rp, qw), F32), v((2, rp, qw), F32), v((2, rp, kx), F32),
            v((rp, qw), F32), v((rp, qw), F32), v((rp, kx), F32),
            v((8, t2), F32),
            dma((300,)), dma((60,)), dma((nctx * nz,)), dma((nctx * nz,)), dma((nctx * nz,)),
            dma((6 * nctx,)), dma((nz,)), dma((nz,)), dma((nz,)), dma((2,)), dma((3 * nz,)), dma((3 * nz,)),
            dma((2 * nz,)), dma((2 * nz,)), dma((2 * nz,)), dma((2 * nz,)),
            dma((nz,)), dma((nz,)), dma((nz,)), dma((nz,)), dma((8,)), dma((3, 6)), dma((6,)),
            dma((6,)), dma((6,)), dma((nch,)), dma((nch,)), dma((2 * nz,)), dma((2 * nz,)),
            dma((2 * nz,)),
        ],
        compiler_params=pltpu.CompilerParams(
            collective_id=0, has_side_effects=True, vmem_limit_bytes=64 * 2**20
        ),
        name="layer",
    )(*args)


def pass_kernel(count, *refs):
    for k in range(count):
        refs[count + k][...] = refs[k][...]


def pass_on(arrays):
    count = len(arrays)
    vm = pl.BlockSpec(memory_space=pltpu.VMEM)
    return pl.pallas_call(
        functools.partial(pass_kernel, count),
        out_shape=tuple(jax.ShapeDtypeStruct(x.shape, x.dtype) for x in arrays),
        in_specs=[vm] * count,
        out_specs=(vm,) * count,
        name="pass_on",
    )(*arrays)


def body(hidden, routes, cot, na, wq, wk, wv, wo, nm, wr, wg, wu, wd):
    nctx, nz = lax.axis_size("ctx"), lax.axis_size("wsh")
    t0, width = hidden.shape[1], hidden.shape[2]
    rp = wq.shape[1]
    eloc, ff = wg.shape[2], wg.shape[3]
    heads = wq.shape[2] // HEAD // 2
    fc = eloc * ff // 2
    cfg = (nctx, nz, width, rp, t0, heads, fc, eloc)
    pos = np.arange(nctx * t0, dtype=np.float32)
    freq = np.float32(BASE) ** (-np.arange(HEAD // 2, dtype=np.float32) * 2.0 / HEAD)
    ang = pos[:, None] * freq.astype(np.float32)[None, :]
    cos, sin = np.cos(ang), np.sin(ang)
    cosf = jnp.asarray(np.concatenate([cos, cos], axis=1), F32)
    sinf = jnp.asarray(np.concatenate([-sin, sin], axis=1), F32)
    halves = [jnp.transpose(w[0], (1, 0, 2)) for w in (wg, wu, wd)]
    r = layer_call(
        cfg,
        (hidden[0], routes[0, 0].T, cot[0], wq[0], wk[0], wv[0], wo[0], na, nm, wr[0].T, *halves,
         cosf, sinf),
    )
    out, ig, eg, eu, ed, gwq, gwk, gwv, gwo, gna, gnm, gwr = r[:12]
    out, ig, gwq, gwk, gwv, gwo, gna, gnm, gwr = pass_on(
        (out, ig, gwq, gwk, gwv, gwo, gna, gnm, gwr)
    )
    back = lambda x: jnp.transpose(x.astype(F32), (1, 0, 2))[None]
    return (
        out[None], ig[None], gna, gwq[None], gwk[None], gwv[None], gwo[None],
        gnm, gwr.T[None], back(eg), back(eu), back(ed),
    )


def shifted(value, axis, steps):
    count = lax.axis_size(axis)
    pairs = [(source, (source + steps) % count) for source in range(count)]
    return lax.ppermute(value, axis, pairs)


def normalize(hidden_state, gain):
    return (
        hidden_state
        * lax.rsqrt(jnp.mean(hidden_state * hidden_state, axis=-1, keepdims=True) + NORM_EPSILON)
        * gain
    )


def rotary(token_positions, head_size):
    half_size = head_size // 2
    frequency = ROTARY_BASE ** (-jnp.arange(half_size, dtype=jnp.float32) * 2.0 / head_size)
    angles = token_positions.astype(jnp.float32)[:, None] * frequency[None, :]
    return (jnp.cos(angles)[:, None, :], jnp.sin(angles)[:, None, :])


def apply_rotary(values_in, cosine, sine_rows, direction):
    half_size = values_in.shape[-1] // 2
    first_half = values_in[..., :half_size]
    second = values_in[..., half_size:]
    return jnp.concatenate(
        [
            first_half * cosine - direction * second * sine_rows,
            second * cosine + direction * first_half * sine_rows,
        ],
        axis=-1,
    )


def slot_targets(picks_in, matches):
    flat_matches = matches.reshape(-1, matches.shape[-1]).astype(jnp.int32)
    earlier = jnp.cumsum(flat_matches, axis=0) - flat_matches
    return picks_in.reshape(-1) * CAP + jnp.sum(earlier * flat_matches, axis=1)


def score_rows(query_low, key_rows, token_positions):
    total_rows = query_low.shape[0]
    head_size = query_low.shape[2]
    grouped_heads = query_low.reshape(total_rows, key_rows.shape[1], -1, head_size)
    scores = jnp.einsum(
        "qhgd,khd->hgqk", grouped_heads, key_rows, preferred_element_type=jnp.float32
    ) * head_size ** (-0.5)
    allowed = jnp.arange(key_rows.shape[0], dtype=jnp.int32)[None, :] <= token_positions[:, None]
    return (grouped_heads, jnp.where(allowed[None, None], scores, -1e30))


def attend(query_low, key_rows, value_rows, token_positions):
    grouped_heads, scores = score_rows(query_low, key_rows, token_positions)
    highest = jnp.max(scores, axis=-1, keepdims=True)
    log_total = highest + jnp.log(jnp.sum(jnp.exp(scores - highest), axis=-1, keepdims=True))
    weights = jnp.exp(scores - log_total).astype(jnp.bfloat16)
    attended = jnp.einsum("hgqk,khd->qhgd", weights, value_rows, preferred_element_type=jnp.float32)
    return (attended.reshape(query_low.shape[0], -1), log_total)


def attend_grad(query_low, key_rows, value_rows, token_positions, log_total, grad_mixed):
    grouped_heads, scores = score_rows(query_low, key_rows, token_positions)
    score_scale = query_low.shape[-1] ** (-0.5)
    softmax_rows = jnp.exp(scores - log_total)
    weights = softmax_rows.astype(jnp.bfloat16)
    grad_grouped = grad_mixed.reshape(grouped_heads.shape)
    grad_weights = jnp.einsum(
        "qhgd,khd->hgqk", grad_grouped, value_rows, preferred_element_type=jnp.float32
    )
    grad_values = jnp.einsum(
        "hgqk,qhgd->khd", weights, grad_grouped, preferred_element_type=jnp.float32
    )
    row_inner = jnp.sum(softmax_rows * grad_weights, axis=-1, keepdims=True)
    grad_scores = (softmax_rows * (grad_weights - row_inner)).astype(jnp.bfloat16)
    grad_query = (
        jnp.einsum("hgqk,khd->qhgd", grad_scores, key_rows, preferred_element_type=jnp.float32)
        * score_scale
    )
    grad_keys = (
        jnp.einsum("hgqk,qhgd->khd", grad_scores, grouped_heads, preferred_element_type=jnp.float32)
        * score_scale
    )
    return (grad_query.reshape(query_low.shape), grad_keys, grad_values)


def collect_key_grads(grad_keys, grad_values, total_rows):
    cycle_size = lax.axis_size("ctx")
    own_index = lax.axis_index("ctx")
    both_grads = jnp.stack([grad_keys, grad_values])

    def block_piece(block_index):
        return lax.dynamic_slice_in_dim(both_grads, block_index * total_rows, total_rows, 1)

    def cycle_step(step_index, carried):
        moved = shifted(carried.astype(jnp.bfloat16), "ctx", -1).astype(carried.dtype)
        block_index = (own_index + step_index) % cycle_size
        weight_now = jnp.where(step_index < cycle_size, 1.0, 0.0).astype(jnp.float32)
        return moved + weight_now * block_piece(block_index)

    collected = lax.fori_loop(1, cycle_size + 1, cycle_step, block_piece(own_index))
    return (collected[0], collected[1])


def forward_layer(hidden_state, picks_in, dense_set, expert_set):
    gain_attn, query_matrix, key_matrix, value_matrix, output_matrix, gain_moe, router_matrix = (
        dense_set
    )
    gate_w, up_w, down_w = expert_set
    total_rows, model_width = hidden_state.shape
    token_positions = lax.axis_index("ctx") * total_rows + jnp.arange(total_rows, dtype=jnp.int32)
    cosine, sine_rows = rotary(token_positions, HEAD_DIM)
    attention_normed = normalize(hidden_state, gain_attn.astype(jnp.float32)).astype(jnp.bfloat16)
    query_unrotated = jnp.dot(
        attention_normed, query_matrix, preferred_element_type=jnp.float32
    ).reshape(total_rows, QUERY_HEADS, HEAD_DIM)
    key_unrotated = jnp.dot(
        attention_normed, key_matrix, preferred_element_type=jnp.float32
    ).reshape(total_rows, KEY_VALUE_HEADS, HEAD_DIM)
    query_low = apply_rotary(query_unrotated, cosine, sine_rows, 1.0).astype(jnp.bfloat16)
    key_low = apply_rotary(key_unrotated, cosine, sine_rows, 1.0).astype(jnp.bfloat16)
    value_low = (
        jnp.dot(attention_normed, value_matrix, preferred_element_type=jnp.float32)
        .astype(jnp.bfloat16)
        .reshape(total_rows, KEY_VALUE_HEADS, HEAD_DIM)
    )
    key_rows, value_rows = (
        lax.all_gather(key_low, "ctx", axis=0, tiled=True),
        lax.all_gather(value_low, "ctx", axis=0, tiled=True),
    )
    attended, log_total = attend(query_low, key_rows, value_rows, token_positions)
    mixed_reduced = attended.astype(jnp.bfloat16)
    post_attention = hidden_state + lax.dot_general(
        mixed_reduced, output_matrix, (((1,), (1,)), ((), ())), preferred_element_type=jnp.float32
    )
    expert_normed = normalize(post_attention, gain_moe.astype(jnp.float32)).astype(jnp.bfloat16)
    router_logits = jnp.dot(expert_normed, router_matrix, preferred_element_type=jnp.float32)
    expert_count = router_logits.shape[1]
    matches = picks_in[:, :, None] == jnp.arange(expert_count, dtype=jnp.int32)[None, None, :]
    gate_weights = jax.nn.softmax(
        jnp.sum(jnp.where(matches, router_logits[:, None, :], 0.0), axis=-1), axis=-1
    )
    targets = slot_targets(picks_in, matches)
    outgoing = (
        jnp.zeros((expert_count * CAP, model_width), jnp.bfloat16)
        .at[targets]
        .set(jnp.repeat(expert_normed, TOP, axis=0))
    )
    group_count = lax.axis_size("wsh")
    local_count = gate_w.shape[1]
    arrived = lax.all_to_all(
        outgoing.reshape(group_count, local_count, CAP, model_width),
        "wsh",
        split_axis=0,
        concat_axis=0,
        tiled=True,
    )
    gate_pre = jnp.einsum("sjcd,djf->sjcf", arrived, gate_w, preferred_element_type=jnp.float32)
    up_pre = jnp.einsum("sjcd,djf->sjcf", arrived, up_w, preferred_element_type=jnp.float32)
    activations = (jax.nn.silu(gate_pre) * up_pre).astype(jnp.bfloat16)
    produced = jnp.einsum(
        "sjcf,djf->sjcd", activations, down_w, preferred_element_type=jnp.float32
    ).astype(jnp.bfloat16)
    returned = lax.all_to_all(produced, "wsh", split_axis=0, concat_axis=0, tiled=True)
    returned, arrived, gate_pre, up_pre = (returned, arrived, gate_pre, up_pre)
    picked = (
        returned.reshape(-1, model_width)[targets]
        .reshape(total_rows, TOP, model_width)
        .astype(jnp.float32)
    )
    after_moe = post_attention + jnp.sum(gate_weights[:, :, None] * picked, axis=1)
    stored = (
        hidden_state,
        attention_normed,
        query_low,
        key_low,
        value_low,
        log_total,
        mixed_reduced,
        post_attention,
        expert_normed,
        matches,
        gate_weights,
        targets,
        picked,
        arrived,
        gate_pre,
        up_pre,
    )
    return (after_moe, stored, (key_rows, value_rows))


def backward_layer(incoming, stored, dense_set, expert_set, key_rows, value_rows):
    (
        hidden_state,
        attention_normed,
        query_low,
        key_low,
        value_low,
        log_total,
        mixed_reduced,
        post_attention,
        expert_normed,
        matches,
        gate_weights,
        targets,
        picked,
        arrived,
        gate_pre,
        up_pre,
    ) = stored
    gain_attn, query_matrix, key_matrix, value_matrix, output_matrix, gain_moe, router_matrix = (
        dense_set
    )
    gate_w, up_w, down_w = expert_set
    total_rows, model_width = hidden_state.shape
    token_positions = lax.axis_index("ctx") * total_rows + jnp.arange(total_rows, dtype=jnp.int32)
    cosine, sine_rows = rotary(token_positions, HEAD_DIM)
    grad_y = (gate_weights[:, :, None] * incoming[:, None, :]).astype(jnp.bfloat16)
    grad_gates = jnp.sum(incoming[:, None, :] * picked, axis=-1)
    grad_chosen = gate_weights * (
        grad_gates - jnp.sum(gate_weights * grad_gates, axis=-1, keepdims=True)
    )
    grad_logits = jnp.sum(jnp.where(matches, grad_chosen[:, :, None], 0.0), axis=1).astype(
        jnp.bfloat16
    )
    slot_total = arrived.shape[0] * arrived.shape[1] * arrived.shape[2]
    outgoing = (
        jnp.zeros((slot_total, model_width), jnp.bfloat16)
        .at[targets]
        .set(grad_y.reshape(-1, model_width))
    )
    grad_arrived = lax.all_to_all(
        outgoing.reshape(arrived.shape), "wsh", split_axis=0, concat_axis=0, tiled=True
    )
    grad_acts = jnp.einsum(
        "sjcd,djf->sjcf", grad_arrived, down_w, preferred_element_type=jnp.float32
    )
    sigmoid_gate = jax.nn.sigmoid(gate_pre)
    silu_gate = jax.nn.silu(gate_pre)
    activations = (silu_gate * up_pre).astype(jnp.bfloat16)
    grad_gate = (
        grad_acts * up_pre * sigmoid_gate * (1.0 + gate_pre * (1.0 - sigmoid_gate))
    ).astype(jnp.bfloat16)
    grad_up = (grad_acts * silu_gate).astype(jnp.bfloat16)
    grad_rows = (
        jnp.einsum("sjcf,djf->sjcd", grad_gate, gate_w, preferred_element_type=jnp.float32)
        + jnp.einsum("sjcf,djf->sjcd", grad_up, up_w, preferred_element_type=jnp.float32)
    ).astype(jnp.bfloat16)
    grad_back = lax.all_to_all(grad_rows, "wsh", split_axis=0, concat_axis=0, tiled=True)
    expert_grads = (
        lax.psum_scatter(
            jnp.einsum(
                "sjcd,sjcf->djf", arrived, grad_gate, preferred_element_type=jnp.float32
            ).astype(jnp.bfloat16),
            "ctx",
            scatter_dimension=0,
            tiled=True,
        ).astype(jnp.float32),
        lax.psum_scatter(
            jnp.einsum(
                "sjcd,sjcf->djf", arrived, grad_up, preferred_element_type=jnp.float32
            ).astype(jnp.bfloat16),
            "ctx",
            scatter_dimension=0,
            tiled=True,
        ).astype(jnp.float32),
        lax.psum_scatter(
            jnp.einsum(
                "sjcd,sjcf->djf", grad_arrived, activations, preferred_element_type=jnp.float32
            ).astype(jnp.bfloat16),
            "ctx",
            scatter_dimension=0,
            tiled=True,
        ).astype(jnp.float32),
    )
    returned_rows = (
        grad_back.reshape(-1, model_width)[targets]
        .reshape(total_rows, TOP, model_width)
        .astype(jnp.float32)
    )
    grad_normed_moe = jnp.sum(returned_rows, axis=1) + lax.dot_general(
        grad_logits, router_matrix, (((1,), (1,)), ((), ())), preferred_element_type=jnp.float32
    )
    router_term = jnp.einsum(
        "td,te->de", expert_normed, grad_logits, preferred_element_type=jnp.float32
    )
    unused_moe, pull_moe = jax.vjp(normalize, post_attention, gain_moe.astype(jnp.float32))
    grad_after_norm, gain_moe_term = pull_moe(grad_normed_moe)
    grad_after_attn = incoming + grad_after_norm
    grad_attn = grad_after_attn.astype(jnp.bfloat16)
    out_term = jnp.einsum("td,tj->dj", grad_attn, mixed_reduced, preferred_element_type=jnp.float32)
    grad_mixed = jnp.dot(grad_attn, output_matrix, preferred_element_type=jnp.float32).astype(
        jnp.bfloat16
    )
    grad_query, grad_keys, grad_values = attend_grad(
        query_low, key_rows, value_rows, token_positions, log_total, grad_mixed
    )
    grad_key, grad_value = collect_key_grads(grad_keys, grad_values, total_rows)
    grad_query_raw = (
        apply_rotary(grad_query, cosine, sine_rows, -1.0)
        .reshape(total_rows, -1)
        .astype(jnp.bfloat16)
    )
    grad_key_raw = (
        apply_rotary(grad_key, cosine, sine_rows, -1.0).reshape(total_rows, -1).astype(jnp.bfloat16)
    )
    grad_value_raw = grad_value.reshape(total_rows, -1).astype(jnp.bfloat16)
    contract_last = (((1,), (1,)), ((), ()))
    grad_normed_attn = lax.dot_general(
        grad_query_raw, query_matrix, contract_last, preferred_element_type=jnp.float32
    )
    grad_normed_attn = grad_normed_attn + lax.dot_general(
        grad_key_raw, key_matrix, contract_last, preferred_element_type=jnp.float32
    )
    grad_normed_attn = grad_normed_attn + lax.dot_general(
        grad_value_raw, value_matrix, contract_last, preferred_element_type=jnp.float32
    )
    query_term = jnp.einsum(
        "td,tf->df", attention_normed, grad_query_raw, preferred_element_type=jnp.float32
    )
    key_term = jnp.einsum(
        "td,tf->df", attention_normed, grad_key_raw, preferred_element_type=jnp.float32
    )
    value_term = jnp.einsum(
        "td,tf->df", attention_normed, grad_value_raw, preferred_element_type=jnp.float32
    )
    unused_attn, pull_attn = jax.vjp(normalize, hidden_state, gain_attn.astype(jnp.float32))
    grad_before, gain_attn_term = pull_attn(grad_normed_attn)
    layer_grads = (
        lax.psum_scatter(gain_attn_term, ("ctx", "wsh"), scatter_dimension=0, tiled=True),
        lax.psum_scatter(query_term, ("ctx", "wsh"), scatter_dimension=0, tiled=True),
        lax.psum_scatter(key_term, ("ctx", "wsh"), scatter_dimension=0, tiled=True),
        lax.psum_scatter(value_term, ("ctx", "wsh"), scatter_dimension=0, tiled=True),
        lax.psum_scatter(out_term, ("ctx", "wsh"), scatter_dimension=0, tiled=True),
        lax.psum_scatter(gain_moe_term, ("ctx", "wsh"), scatter_dimension=0, tiled=True),
        lax.psum_scatter(router_term, ("ctx", "wsh"), scatter_dimension=0, tiled=True),
    )
    return (grad_after_attn + grad_before, layer_grads, expert_grads)


def plain_body(
    hidden_in,
    routes,
    cotangent,
    norm_attn,
    w_query,
    key_projection,
    value_projection,
    w_out,
    norm_moe,
    w_router,
    w_gate,
    w_up,
    w_down,
):
    hidden_state = hidden_in[0].astype(jnp.float32)
    layer_number = 0
    dense_set = (
        lax.all_gather(norm_attn[layer_number], ("ctx", "wsh"), axis=0, tiled=True),
        lax.all_gather(w_query[layer_number], ("ctx", "wsh"), axis=0, tiled=True),
        lax.all_gather(key_projection[layer_number], ("ctx", "wsh"), axis=0, tiled=True),
        lax.all_gather(value_projection[layer_number], ("ctx", "wsh"), axis=0, tiled=True),
        lax.all_gather(w_out[layer_number], ("ctx", "wsh"), axis=0, tiled=True),
        lax.all_gather(norm_moe[layer_number], ("ctx", "wsh"), axis=0, tiled=True),
        lax.all_gather(w_router[layer_number], ("ctx", "wsh"), axis=0, tiled=True),
    )
    expert_set = (
        lax.all_gather(w_gate[layer_number], "ctx", axis=0, tiled=True),
        lax.all_gather(w_up[layer_number], "ctx", axis=0, tiled=True),
        lax.all_gather(w_down[layer_number], "ctx", axis=0, tiled=True),
    )
    hidden_state, stored, gathered = forward_layer(
        hidden_state, routes[layer_number, 0], dense_set, expert_set
    )
    records = [(stored, None, None, None)]
    incoming = cotangent[0]
    dense_grads = []
    expert_grads = []
    layer_number = 0
    stored, dense_set, expert_set, gathered = records[layer_number]
    dense_set = (
        lax.all_gather(norm_attn[layer_number], ("ctx", "wsh"), axis=0, tiled=True),
        lax.all_gather(w_query[layer_number], ("ctx", "wsh"), axis=0, tiled=True),
        lax.all_gather(key_projection[layer_number], ("ctx", "wsh"), axis=0, tiled=True),
        lax.all_gather(value_projection[layer_number], ("ctx", "wsh"), axis=0, tiled=True),
        lax.all_gather(w_out[layer_number], ("ctx", "wsh"), axis=0, tiled=True),
        lax.all_gather(norm_moe[layer_number], ("ctx", "wsh"), axis=0, tiled=True),
        lax.all_gather(w_router[layer_number], ("ctx", "wsh"), axis=0, tiled=True),
    )
    expert_set = (
        lax.all_gather(w_gate[layer_number], "ctx", axis=0, tiled=True),
        lax.all_gather(w_up[layer_number], "ctx", axis=0, tiled=True),
        lax.all_gather(w_down[layer_number], "ctx", axis=0, tiled=True),
    )
    gathered = (
        lax.all_gather(stored[3], "ctx", axis=0, tiled=True),
        lax.all_gather(stored[4], "ctx", axis=0, tiled=True),
    )
    incoming, layer_grads, layer_expert = backward_layer(
        incoming, stored, dense_set, expert_set, gathered[0], gathered[1]
    )
    dense_grads.insert(0, layer_grads)
    expert_grads.insert(0, layer_expert)
    stacked_dense = [
        jnp.stack([grads_item[position] for grads_item in dense_grads]) for position in range(7)
    ]
    stacked_expert = [
        jnp.stack([grads_item[position] for grads_item in expert_grads]) for position in range(3)
    ]
    return (
        hidden_state[None],
        incoming[None],
        stacked_dense[0],
        stacked_dense[1],
        stacked_dense[2],
        stacked_dense[3],
        stacked_dense[4],
        stacked_dense[5],
        stacked_dense[6],
        stacked_expert[0],
        stacked_expert[1],
        stacked_expert[2],
    )


def solution(mesh):
    return jax.shard_map(
        body if mesh.shape["ctx"] == 8 and mesh.shape["wsh"] == 4 else plain_body,
        mesh=mesh,
        in_specs=(
            P("wsh", "ctx", None),
            P(None, "wsh", "ctx", None),
            P("wsh", "ctx", None),
            P(None, ("ctx", "wsh")),
            P(None, ("ctx", "wsh"), None),
            P(None, ("ctx", "wsh"), None),
            P(None, ("ctx", "wsh"), None),
            P(None, ("ctx", "wsh"), None),
            P(None, ("ctx", "wsh")),
            P(None, ("ctx", "wsh"), None),
            P(None, "ctx", "wsh", None),
            P(None, "ctx", "wsh", None),
            P(None, "ctx", "wsh", None),
        ),
        out_specs=(
            P("wsh", "ctx", None),
            P("wsh", "ctx", None),
            P(None, ("ctx", "wsh")),
            P(None, ("ctx", "wsh"), None),
            P(None, ("ctx", "wsh"), None),
            P(None, ("ctx", "wsh"), None),
            P(None, ("ctx", "wsh"), None),
            P(None, ("ctx", "wsh")),
            P(None, ("ctx", "wsh"), None),
            P(None, "ctx", "wsh", None),
            P(None, "ctx", "wsh", None),
            P(None, "ctx", "wsh", None),
        ),
        check_vma=False,
    )
```

```python
import functools
import jax
import jax.numpy as jnp
import numpy as np
from jax import lax
from jax.experimental import pallas as pl
from jax.experimental.pallas import tpu as pltpu
from jax.sharding import PartitionSpec as P

QUERY_HEADS = 12
KEY_VALUE_HEADS = 2
HEAD_DIM = 128
CAP = 128
NORM_EPSILON = 1e-06
ROTARY_BASE = 1000000.0
MESH = pl.DeviceIdType.MESH
HEAD = 128
TOP = 4
EPS = 1e-06
BASE = 1000000.0
F32 = jnp.float32
BF16 = jnp.bfloat16


def dot(a, b):
    return lax.dot_general(a, b, (((1,), (0,)), ((), ())), preferred_element_type=F32)


def dot_t(a, b):
    return lax.dot_general(a, b, (((1,), (1,)), ((), ())), preferred_element_type=F32)


def t_dot(a, b):
    return lax.dot_general(a, b, (((0,), (0,)), ((), ())), preferred_element_type=F32)


class Place:
    def __init__(self, nctx, nz):
        self.nctx, self.nz, self.nch = nctx, nz, nctx // 2
        self.c = lax.axis_index("ctx")
        self.z = lax.axis_index("wsh")
        self.chip = self.c // 2
        self.core = self.c % 2
        self.sib = self.chip * 2 + 1 - self.core
        self.square = self.nch == 4

    def xchip(self):
        return self.chip + 1 - 2 * (self.chip % 2)

    def ychip(self):
        return (self.chip + 2) % 4

    def near(self, k):
        s = 0
        for here in range(self.nz):
            order = sorted(
                (v for v in range(self.nz) if v != here),
                key=lambda v: (abs(v - here), 2 * v // self.nz != 2 * here // self.nz),
            )
            s = jnp.where(self.z == here, order[k - 1], s)
        return s

    def zto(self, dz):
        return (self.z + dz) % self.nz

    def zfrom(self, dz):
        return (self.z + self.nz - dz) % self.nz


class Sends:
    def __init__(self, sems, count):
        self.sems, self.count, self.used, self.live = sems, count, 0, []

    def start(self, src, dst, rsem, dev, when=None):
        assert self.used < self.count
        cp = pltpu.make_async_remote_copy(
            src_ref=src,
            dst_ref=dst,
            send_sem=self.sems.at[self.used],
            recv_sem=rsem,
            device_id=dev,
            device_id_type=MESH,
        )
        if when is None:
            cp.start()
        else:
            pl.when(when)(cp.start)
        self.used += 1
        self.live.append((cp, when))

    def local(self, src, dst):
        assert self.used < self.count
        cp = pltpu.make_async_copy(src, dst, self.sems.at[self.used])
        cp.start()
        self.used += 1
        return cp

    def take(self):
        live, self.live = self.live, []
        return live

    def drain(self, live=None):
        for cp, when in self.take() if live is None else live:
            if when is None:
                cp.wait_send()
            else:
                pl.when(when)(cp.wait_send)


def arrived(ref, sem):
    pltpu.make_async_copy(ref, ref, sem).wait()


def greet(pc):
    bar = pltpu.get_barrier_semaphore()
    for k in range(1, pc.nctx):
        to = ((pc.c + k) % pc.nctx, pc.z)
        pl.semaphore_signal(bar, inc=1, device_id=to, device_id_type=MESH)
    for k in range(1, pc.nz):
        pl.semaphore_signal(bar, inc=1, device_id=(pc.c, pc.zto(k)), device_id_type=MESH)
    return lambda: pl.semaphore_wait(bar, pc.nctx + pc.nz - 2)


def rms(x, width):
    return lax.rsqrt(jnp.sum(x * x, axis=-1, keepdims=True) * (1.0 / width) + EPS)


def gain_row(extra, lane):
    pick = (lax.broadcasted_iota(jnp.int32, (16, extra.shape[1]), 1) == lane).astype(BF16)
    return dot_t(pick, extra)[0:1]


def rope(x, cos, sin):
    return x * cos + pltpu.roll(x, HEAD // 2, 1) * sin


class Reduce:
    def __init__(self, pc, snd, slab, first, fx, fy, sems):
        self.pc, self.snd, self.slab = pc, snd, slab
        self.first, self.fx, self.fy, self.sems = first, fx, fy, sems
        self.x, self.y, self.d = pc.xchip(), pc.ychip(), 3 - pc.chip

    def to(self, chip):
        return (chip * 2 + self.pc.core, self.pc.z)

    def diagonal(self):
        self.snd.start(self.slab(self.d, 0), self.first.at[0], self.sems.at[0], self.to(self.x))
        self.snd.start(self.slab(self.d, 1), self.first.at[1], self.sems.at[1], self.to(self.y))

    def straight_x(self):
        self.snd.start(self.slab(self.x, 0), self.fx.at[0], self.sems.at[2], self.to(self.x))

    def straight_y(self):
        self.snd.start(self.slab(self.y, 1), self.fy.at[1], self.sems.at[5], self.to(self.y))

    def merge(self, add):
        arrived(self.first.at[0], self.sems.at[0])
        add(self.slab(self.y, 0), self.first.at[0])
        self.snd.start(self.slab(self.y, 0), self.fy.at[0], self.sems.at[4], self.to(self.y))
        arrived(self.first.at[1], self.sems.at[1])
        add(self.slab(self.x, 1), self.first.at[1])
        self.snd.start(self.slab(self.x, 1), self.fx.at[1], self.sems.at[3], self.to(self.x))

    def wait(self):
        for w in range(2):
            arrived(self.fx.at[w], self.sems.at[2 + w])
            arrived(self.fy.at[w], self.sems.at[4 + w])


def add_into(dst, src):
    dst[...] = (dst[...].astype(F32) + src[...].astype(F32)).astype(BF16)


def layer_kernel(
    cfg,
    h_ref, routes_ref, cot_ref, wq_ref, wk_ref, wv_ref, wo_ref, ga_ref, gm_ref, wr_ref,
    eg_ref, eu_ref, ed_ref,
    cos_in, sin_in,
    out_ref, ig_ref, eg_out, eu_out, ed_out, gwq_out, gwk_out, gwv_out, gwo_out, gna_out, gnm_out, gwr_out,
    efirst, efx, efy, ozr,
    wk, wq, wb, we, zk, zq, zb, hbuf, cosr, sinr, square,
    qs, kv, lses, obs, xa, h1s, xm, gr, gts,
    ggu, ap, keep, sibs, sibr, zr, okeep, kgg, sgg, rgg, zgg, gtt,
    gat, gkv, gkvb, gkvr, graw, part, pget, exts,
    esibr,
    bfirst, bfx, bfy, qfirst, qfx, qfy, kfirst, kfx, kfy,
    zrb, zrq, zrk, fb, fq, fk, frb, frq, frk, rowp,
    ssem, lsem, rwk, rwq, rwb, re, rzk_, rzq_, rzb_, rfw, rxm, rxf,
    sib_s, sib_r, z_s, z_r, osib_s, osib_r, oz_s, oz_r, rmisc, esem, bsem,
    qsem, ksem, rkv, rkvf, rzb, rzq, rzk,
):
    nctx, nz, width, rp, t0, heads, fc, _ = cfg
    pc = Place(nctx, nz)
    nch = pc.nch
    t2 = 2 * t0
    qw = heads * HEAD
    kw = qw + 2 * HEAD
    kx = wk.shape[1]
    dp = wk.shape[0]
    core, z, c, chip = pc.core, pc.z, pc.c, pc.chip
    per = nz * rp
    met = greet(pc)
    snd = Sends(ssem, ssem.shape[0])
    loads = Sends(lsem, lsem.shape[0])
    sib = (pc.sib, z)
    mine = pl.ds(pl.multiple_of(chip * t2, t2), t2)
    mine0 = pl.ds(pl.multiple_of(core * t0, t0), t0)
    sib0 = pl.ds(pl.multiple_of((1 - core) * t0, t0), t0)
    xs, ys, ds = pc.xchip() * 2, pc.ychip() * 2, (3 - chip) * 2
    nearest = [pc.near(k) for k in range(1, nz)]

    def line_send(src, sem, order):
        for s in order:
            snd.start(src, src, sem, (c, s))

    def rows(cc, s):
        return pl.ds(pl.multiple_of((cc * nz + s) * rp, 16), rp)

    def slot(s, k):
        return pl.ds(pl.multiple_of(s * t2 + k * t0, t0), t0)

    def slot8(s, k):
        return pl.ds(pl.multiple_of((s * 2 + k) * 8, 8), 8)

    def both_parts(s):
        return pl.ds(pl.multiple_of(s * 2 * rp, 16), 2 * rp)

    def part_of(s, k):
        return pl.ds(pl.multiple_of((s * 2 + k) * rp, 16), rp)

    def slab_rows(q, w):
        return pl.ds(pl.multiple_of((q * 2 + w) * per, 16), per)

    tables = [loads.local(cos_in.at[mine], cosr), loads.local(sin_in.at[mine], sinr)]
    square[...] = jnp.zeros(square.shape, F32)
    experts = wr_ref.shape[0]
    square[0:experts, 0:rp] = wr_ref[...].astype(F32)
    square[8:9, 0:rp] = ga_ref[...].astype(F32)
    square[9:10, 0:rp] = gm_ref[...].astype(F32)
    ex = square[...].T[0:rp].astype(BF16)
    for k in range(2):
        at = part_of(z, k)
        zk[at, 0:HEAD] = wk_ref[:, k * HEAD:(k + 1) * HEAD]
        zk[at, HEAD:2 * HEAD] = wv_ref[:, k * HEAD:(k + 1) * HEAD]
        zk[at, 2 * HEAD:] = ex
        zq[at] = wq_ref[:, k * qw:(k + 1) * qw]
        zb[at] = wo_ref[:, k * qw:(k + 1) * qw]
    own = slot(z, core)
    gr[own] = cot_ref[...].astype(BF16)
    hbuf[core] = h_ref[...]
    met()

    def spread(src, dst, rs, s):
        here = dst.at[rows(c, s)]
        sem = rs.at[c * nz + s]
        for q in (pc.xchip(), pc.ychip()):
            for k in range(2):
                snd.start(src.at[part_of(s, k)], here, sem, (q * 2 + k, z))
        snd.start(src.at[part_of(s, 1 - core)], here, sem, sib)

    def forward(dst, rs, s):
        for source, to in ((ys, pc.xchip()), (xs + 1, pc.ychip())):
            here = dst.at[rows(source, s)]
            sem = rs.at[source * nz + s]
            arrived(here, sem)
            snd.start(here, here, sem, (to * 2 + core, z))

    def settle(dst, rs):
        for cc in (pc.sib, xs, ys + 1, ds, ds + 1):
            for s in range(nz):
                arrived(dst.at[rows(cc, s)], rs.at[cc * nz + s])

    packs = ((zk, rzk_, wk, rwk), (zq, rzq_, wq, rwq), (zb, rzb_, wb, rwb))
    for ref, rs, _, _ in packs:
        line_send(ref.at[both_parts(z)], rs.at[z], nearest)
    line_send(gr.at[own], rxm.at[z], nearest)
    keeps = ([], [], [])
    snd.start(hbuf.at[core], hbuf.at[core], rfw.at[0], sib)
    for (ref, _, dst, rs), kept in zip(packs, keeps):
        spread(ref, dst, rs, z)
        kept.append(loads.local(ref.at[part_of(z, core)], dst.at[rows(c, z)]))
    snd.start(gr.at[own], gr.at[own], rxf.at[z], sib)

    def column(which):
        ref, zs, dst, rs = packs[which]
        for s in nearest:
            arrived(ref.at[both_parts(s)], zs.at[s])
            spread(ref, dst, rs, s)
            keeps[which].append(loads.local(ref.at[part_of(s, core)], dst.at[rows(c, s)]))

    def onward(which):
        _, _, dst, rs = packs[which]
        for s in [z] + nearest:
            forward(dst, rs, s)

    def have(which):
        _, _, dst, rs = packs[which]
        for cp in keeps[which]:
            cp.wait()
        settle(dst, rs)

    column(0)
    onward(0)
    column(1)
    arrived(hbuf.at[1 - core], rfw.at[0])
    for cp in tables:
        cp.wait()
    have(0)
    cos, sin = cosr[...], sinr[...]
    extra = wk[:, 2 * HEAD:]
    gain_a = gain_row(extra, 8)
    gain_m = gain_row(extra, 9)
    for k in range(2):
        hk = hbuf[k].astype(F32)
        xa[pl.ds(k * t0, t0)] = (hk * rms(hk, width) * gain_a).astype(BF16)
    xav = xa[...]
    kraw = dot(xav, wk[:, :2 * HEAD])
    kv[mine, 0:HEAD] = rope(kraw[:, :HEAD], cos, sin).astype(BF16)
    kv[mine, HEAD:] = kraw[:, HEAD:].astype(BF16)
    for k in range(1, nch):
        snd.start(kv.at[mine], kv.at[mine], rkvf.at[k], (((chip + k) % nch) * 2 + core, z))
    onward(1)
    column(2)

    fh = fc // 2

    def mats(m, j, cc):
        at = pl.ds(pl.multiple_of(cc * per, 16), per)
        return we.at[m, at, pl.ds(j * fh, fh)]

    experts_in = (eg_ref, eu_ref, ed_ref)
    own_e = [
        loads.local(experts_in[m].at[core], we.at[m, pl.ds(pl.multiple_of(c * per, 16), per)])
        for m in range(3)
    ]

    def expert_spread(m, j):
        here = mats(m, j, c)
        sem = re.at[(2 * m + j) * nctx + c]
        half = pl.ds(j * fh, fh)
        for q in (pc.xchip(), pc.ychip()):
            for k in range(2):
                snd.start(experts_in[m].at[k, :, half], here, sem, (q * 2 + k, z))
        snd.start(experts_in[m].at[1 - core, :, half], here, sem, sib)

    def expert_onward(m, j):
        for source, to in ((ys, pc.xchip()), (xs + 1, pc.ychip())):
            here = mats(m, j, source)
            sem = re.at[(2 * m + j) * nctx + source]
            arrived(here, sem)
            snd.start(here, here, sem, (to * 2 + core, z))

    def expert_have(m, j):
        for cc in (pc.sib, xs, ys + 1, ds, ds + 1):
            arrived(mats(m, j, cc), re.at[(2 * m + j) * nctx + cc])
        if j == 0:
            own_e[m].wait()

    units = [(m, j) for j in range(2) for m in (2, 0, 1)]
    dense_sends = snd.take()
    expert_spread(*units[0])
    have(1)
    for hd in range(heads):
        cols = slice(hd * HEAD, (hd + 1) * HEAD)
        qs[:, cols] = rope(dot(xav, wq[:, cols]), cos, sin).astype(BF16)
    onward(2)
    for unit in units[1:]:
        expert_spread(*unit)
    for k in range(1, nch):
        other = pl.ds(pl.multiple_of(((chip + nch - k) % nch) * t2, t2), t2)
        arrived(kv.at[other], rkvf.at[k])

    keys = nch * t2
    scale = HEAD ** -0.5
    ok = lax.broadcasted_iota(jnp.int32, (t2, keys), 1) <= (
        chip * t2 + lax.broadcasted_iota(jnp.int32, (t2, keys), 0)
    )
    lane = lax.broadcasted_iota(jnp.int32, (t2, 128), 1)
    lane0 = lax.broadcasted_iota(jnp.int32, (t0, 128), 1)
    lses[...] = jnp.zeros((t2, 128), F32)

    def head_forward(hd, carry):
        cols = pl.ds(pl.multiple_of(hd * HEAD, HEAD), HEAD)
        s = dot_t(qs[:, cols], kv[:, 0:HEAD]) * scale
        s = jnp.where(ok, s, -1e30)
        m = jnp.max(s, axis=-1, keepdims=True)
        e = jnp.exp(s - m)
        total = jnp.sum(e, axis=-1, keepdims=True)
        lses[...] = jnp.where(lane == hd, m + jnp.log(total), lses[...])
        p = (e * (1.0 / total)).astype(BF16)
        obs[:, cols] = dot(p, kv[:, HEAD:]).astype(BF16)
        return carry

    def tokens_in(i, s):
        buf, at = tokens[i]
        here = buf.at[at(s, core)]
        arrived(here, rxm.at[i * nz + s])
        snd.start(here, here, rxf.at[i * nz + s], sib)

    tokens = ((gr, slot), (xm, slot), (gtt, slot8))
    lax.fori_loop(0, heads, head_forward, 0)
    expert_onward(*units[0])
    have(2)
    part[...] = dot_t(obs[...], wb[...])
    snd.start(part.at[sib0], pget, rfw.at[1], sib)
    arrived(pget, rfw.at[1])
    h1 = h_ref[...].astype(F32) + part[mine0] + pget[...]
    h1s[...] = h1
    xmv = (h1 * rms(h1, width) * gain_m).astype(BF16)
    xm[own] = xmv
    picks = jnp.zeros((128, t0), F32)
    for k in range(TOP):
        row = lax.broadcasted_iota(jnp.int32, (128, t0), 0)
        picks = picks + (routes_ref[k:k + 1, :] == row).astype(F32)
    chosen = picks.T > 0.0
    logits = jnp.where(chosen, dot(xmv, extra), -1e30)
    top = jnp.max(logits, axis=-1, keepdims=True)
    e = jnp.where(chosen, jnp.exp(logits - top), 0.0)
    gts[own] = e / jnp.sum(e, axis=-1, keepdims=True)
    gtt[slot8(z, core)] = gts[own].T[0:8]
    for i in (2, 1):
        buf, at = tokens[i]
        line_send(buf.at[at(z, core)], rxm.at[i * nz + z], nearest[::-1])
        snd.start(buf.at[at(z, core)], buf.at[at(z, core)], rxf.at[i * nz + z], sib)
    for unit in units[1:]:
        expert_onward(*unit)
    for s in nearest:
        tokens_in(0, s)
    for s in nearest:
        for i in (1, 2):
            tokens_in(i, s)
    for s in range(nz):
        arrived(gr.at[slot(s, 1 - core)], rxf.at[s])
    def rows_first(i, carry, j):
        at = pl.ds(pl.multiple_of(i * t2, t2), t2)
        ggu[at, 2 * j * fh:(2 * j + 1) * fh] = dot(
            gr[at], we[2, :, j * fh:(j + 1) * fh]
        ).astype(BF16)
        return carry

    for j in range(2):
        expert_have(2, j)
        lax.fori_loop(0, nz, functools.partial(rows_first, j=j), 0)
    for buf, at, i in ((xm, slot, 1), (gtt, slot8, 2)):
        for s in range(nz):
            arrived(buf.at[at(s, 1 - core)], rxf.at[i * nz + s])
    square[...] = jnp.zeros(square.shape, F32)
    for s in range(nz):
        for k in range(2):
            square[0:8] = gtt[slot8(s, k)]
            gts[slot(s, k)] = square[...].T

    mine128 = pl.ds(pl.multiple_of(core * 128, 128), 128)
    sib128 = pl.ds(pl.multiple_of((1 - core) * 128, 128), 128)
    eloc = cfg_experts(cfg)
    mine_e = z * eloc + (core * eloc) // 2

    def seat(source, at):
        return jnp.where(source > at, source - 1, source)

    def zof(i):
        s = z
        for k in range(nz - 1):
            s = jnp.where(i == k, nearest[nz - 2 - k], s)
        return s

    def blk(i):
        return pl.ds(pl.multiple_of(zof(i) * t2, t2), t2)

    def copy_to_sib(src, dst, ss, rs):
        return pltpu.make_async_remote_copy(
            src_ref=src, dst_ref=dst, send_sem=ss, recv_sem=rs, device_id=sib, device_id_type=MESH
        )

    def copy_to_z(i, src, dst, ss, rs):
        return pltpu.make_async_remote_copy(
            src_ref=src, dst_ref=dst, send_sem=ss, recv_sem=rs, device_id=(c, zof(i)),
            device_id_type=MESH,
        )

    def g_copies(i):
        return (
            copy_to_sib(sibs.at[i], sibr.at[i], sib_s.at[i], sib_r.at[i]),
            copy_to_sib(sgg.at[i], rgg.at[i], sib_s.at[nz + i], sib_r.at[nz + i]),
        )

    def gz_copies(i):
        to = seat(z, zof(i))
        return (
            copy_to_z(i, keep.at[i], zr.at[to], z_s.at[i], z_r.at[to]),
            copy_to_z(i, kgg.at[i], zgg.at[to], z_s.at[nz + i], z_r.at[nz + to]),
        )

    def g_settle(i):
        for cp in g_copies(i):
            cp.wait()
        keep[i] = (keep[i].astype(F32) + sibr[i].astype(F32)).astype(BF16)
        kgg[i] = kgg[i] + rgg[i]

    def rows_mid(i, carry, j):
        x = xm[blk(i)]
        cols = slice(j * fh, (j + 1) * fh)
        first = slice(2 * j * fh, (2 * j + 1) * fh)
        gate = jnp.sum(jnp.where(lane == mine_e, gts[blk(i)], 0.0), axis=1, keepdims=True)
        pre = dot(x, we[0, :, cols])
        up = dot(x, we[1, :, cols])
        ga0 = ggu[blk(i), first].astype(F32)
        sg = 1.0 / (1.0 + jnp.exp(-pre))
        silu = pre * sg
        act = silu * up
        ggc = jnp.sum(act * ga0, axis=1, keepdims=True)
        rowp[...] = jnp.where(lane == mine_e, ggc, 0.0).T[0:8]
        if j == 0:
            kgg[i] = rowp[:, mine128]
            sgg[i] = rowp[:, sib128]
        else:
            kgg[i] += rowp[:, mine128]
            sgg[i] += rowp[:, sib128]
        gact = gate * ga0
        ap[blk(i), cols] = (gate * act).astype(BF16)
        ggu[blk(i), first] = (gact * up * sg * (1.0 + pre * (1.0 - sg))).astype(BF16)
        ggu[blk(i), (2 * j + 1) * fh:(2 * j + 2) * fh] = (gact * silu).astype(BF16)
        return carry

    def rows_back(i, carry):
        total = None
        for k in range(4):
            term = dot_t(
                ggu[blk(i), k * fh:(k + 1) * fh], we[k % 2, :, k // 2 * fh:(k // 2 + 1) * fh]
            )
            total = term if total is None else total + term
        part[...] = total
        keep[i] = part[mine0].astype(BF16)
        sibs[i] = part[sib0].astype(BF16)
        for cp in g_copies(i):
            cp.start()

        @pl.when(i > 0)
        def _():
            g_settle(i - 1)
            for cp in gz_copies(i - 1):
                cp.start()

        return carry

    far = (zq, zb)
    ers = [
        Reduce(
            pc, snd, lambda q, w, m=m: we.at[m, slab_rows(q, w)], efirst.at[m], efx.at[m],
            efy.at[m], esem.at[m],
        )
        for m in range(3)
    ]
    order = (ers[0].d, ers[0].x, ers[0].y, chip)

    def chip_cols(q):
        return pl.ds(pl.multiple_of(q * 2 * per, 128), 2 * per)

    row_sends = snd.take()
    for j in range(2):
        expert_have(0, j)
        expert_have(1, j)
        lax.fori_loop(0, nz, functools.partial(rows_mid, j=j), 0)
        if j == 0:
            snd.drain(dense_sends)
        half = pl.ds(j * fh, fh)
        gw = t_dot(xm[:, chip_cols(order[0])], ggu[:, 2 * j * fh:2 * (j + 1) * fh])
        for m in range(2):
            far[m][:, j * fh:(j + 1) * fh] = gw[:, m * fh:(m + 1) * fh].astype(BF16)
            for w, q in ((0, ers[m].x), (1, ers[m].y)):
                snd.start(
                    far[m].at[pl.ds(w * per, per), half], efirst.at[m, w, :, half],
                    esem.at[m, w], ers[m].to(q),
                )
    snd.drain(row_sends)
    lax.fori_loop(0, nz, rows_back, 0)
    g_settle(nz - 1)

    def expert_step(n, rs):
        for one in rs:
            (one.diagonal, one.straight_x, one.straight_y, lambda: None)[n]()

    for n, q in enumerate(order):
        if n == 0:
            continue
        cols = chip_cols(q)
        gw = t_dot(xm[:, cols], ggu[...])
        for k in range(4):
            we[k % 2, cols, k // 2 * fh:(k // 2 + 1) * fh] = gw[:, k * fh:(k + 1) * fh].astype(BF16)
        expert_step(n, ers[:2])

    def o_copy(i):
        return copy_to_sib(sibs.at[i], sibr.at[i], osib_s.at[i], osib_r.at[i])

    def oz_copy(i):
        to = seat(z, zof(i))
        return copy_to_z(i, okeep.at[i], ozr.at[to], oz_s.at[i], oz_r.at[to])

    def o_settle(i):
        o_copy(i).wait()
        okeep[i] = (okeep[i].astype(F32) + sibr[i].astype(F32)).astype(BF16)

    def rows_out(i, carry):
        part[...] = dot_t(ap[blk(i)], we[2])
        okeep[i] = part[mine0].astype(BF16)
        sibs[i] = part[sib0].astype(BF16)
        o_copy(i).start()

        @pl.when(i > 0)
        def _():
            o_settle(i - 1)
            oz_copy(i - 1).start()

        return carry

    lax.fori_loop(0, nz, rows_out, 0)
    o_settle(nz - 1)

    for n, q in enumerate(order):
        cols = pl.ds(pl.multiple_of(q * 2 * per, 128), 2 * per)
        we[2, cols] = t_dot(gr[:, cols], ap[...]).astype(BF16)
        expert_step(n, ers[2:])

    def fetch(src, room, spot):
        here = room.at[pl.ds(spot // 2 * per, per), pl.ds(spot % 2 * fc, fc)]
        return here, loads.local(src, here)

    def add_far(dst, src):
        here, cp = fetch(src, gr, 0)
        cp.wait()
        add_into(dst, here)

    ers[0].merge(add_far)
    ers[1].merge(add_far)

    gsum = keep[nz - 1].astype(F32)
    ggs = kgg[nz - 1]
    for i in range(nz - 1):
        arrived(zr.at[i], z_r.at[i])
        arrived(zgg.at[i], z_r.at[nz + i])
        gsum = gsum + zr[i].astype(F32)
        ggs = ggs + zgg[i]
    square[...] = jnp.zeros(square.shape, F32)
    square[0:8] = ggs
    ggs = square[...].T
    gate = gts[own]
    glog = (gate * (ggs - jnp.sum(gate * ggs, axis=1, keepdims=True))).astype(BF16)
    extra = wk[:, 2 * HEAD:]
    gxm = gsum + dot_t(glog, extra)
    h1 = h1s[...]
    r = rms(h1, width)
    n = h1 * r
    gy = gxm * gain_m
    g1 = cot_ref[...] + r * (gy - n * (jnp.sum(gy * n, axis=1, keepdims=True) * (1.0 / width)))
    ext = t_dot(xm[own], glog) + t_dot((gxm * n).astype(BF16), (lane0 == 9).astype(BF16))
    exts[...] = ext
    ig_ref[...] = g1
    gat[mine0] = g1.astype(BF16)
    snd.start(gat.at[mine0], gat.at[mine0], rmisc.at[0], sib)
    arrived(gat.at[sib0], rmisc.at[0])
    gav = gat[...]
    go = dot(gav, wb[...]).astype(BF16)
    brs = Reduce(pc, snd, lambda q, w: wb.at[slab_rows(q, w)], bfirst, bfx, bfy, bsem)

    def out_grads(k, carry):
        cols = pl.ds(pl.multiple_of(k * 2 * per, 128), 2 * per)
        wb[cols] = t_dot(gat[:, cols], obs[...]).astype(BF16)
        return carry

    lax.fori_loop(0, nch, out_grads, 0)
    brs.diagonal()
    brs.straight_x()
    brs.straight_y()
    obs[...] = go

    cos, sin = cosr[...], sinr[...]
    gkv[...] = jnp.zeros(gkv.shape, F32)

    def one_head(hd, carry):
        cols = pl.ds(pl.multiple_of(hd * HEAD, HEAD), HEAD)
        s = dot_t(qs[:, cols], kv[:, 0:HEAD]) * scale
        pe = jnp.where(ok, jnp.exp(s - jnp.sum(jnp.where(lane == hd, lses[...], 0.0), axis=1, keepdims=True)), 0.0)
        gp = dot_t(obs[:, cols], kv[:, HEAD:])
        delta = jnp.sum(pe * gp, axis=-1, keepdims=True)
        gs = (pe * (gp - delta)).astype(BF16)
        gq = dot(gs, kv[:, 0:HEAD]) * scale
        graw[:, cols] = rope(gq, cos, -sin).astype(BF16)
        gkv[:, 0:HEAD] += t_dot(gs, qs[:, cols])
        gkv[:, HEAD:] += t_dot(pe.astype(BF16), obs[:, cols])
        return carry

    lax.fori_loop(0, heads, one_head, 0)
    gkvb[...] = gkv[...].astype(BF16)
    for k in range(1, nch):
        q = (chip + k) % nch
        snd.start(
            gkvb.at[pl.ds(pl.multiple_of(q * t2, t2), t2)], gkvr.at[k - 1], rkv.at[k],
            (q * 2 + core, z),
        )

    part[...] = dot_t(graw[:, :qw], wq[...])

    def query_grads(k, carry):
        cols = pl.ds(pl.multiple_of(k * 2 * per, 128), 2 * per)
        wq[cols] = t_dot(xa[:, cols], graw[:, 0:qw]).astype(BF16)
        return carry

    lax.fori_loop(0, nch, query_grads, 0)
    qrs = Reduce(
        pc, snd, lambda q, w: wq.at[slab_rows(q, w)], qfirst, qfx, qfy, qsem
    )
    qrs.diagonal()
    qrs.straight_x()
    qrs.straight_y()
    brs.merge(add_into)
    gk = gkv[mine]
    for k in range(1, nch):
        arrived(gkvr.at[k - 1], rkv.at[k])
        gk = gk + gkvr[k - 1].astype(F32)
    graw[:, qw:qw + HEAD] = rope(gk[:, :HEAD] * scale, cos, -sin).astype(BF16)
    graw[:, qw + HEAD:] = gk[:, HEAD:].astype(BF16)
    part[...] += dot_t(graw[:, qw:], wk[:, :2 * HEAD])
    snd.start(part.at[sib0], pget, rmisc.at[1], sib)

    def key_grads(k, carry):
        cols = pl.ds(pl.multiple_of(k * 2 * per, 128), 2 * per)
        wk[cols, 0:2 * HEAD] = t_dot(xa[:, cols], graw[:, qw:]).astype(BF16)
        return carry

    lax.fori_loop(0, nch, key_grads, 0)
    arrived(pget, rmisc.at[1])
    gxa = part[mine0] + pget[...]
    h = h_ref[...].astype(F32)
    r = rms(h, width)
    n = h * r
    gy = gxa * gain_a
    ig_ref[...] += r * (gy - n * (jnp.sum(gy * n, axis=1, keepdims=True) * (1.0 / width)))
    wk[:, 2 * HEAD:] = (
        exts[...] + t_dot((gxa * n).astype(BF16), (lane0 == 8).astype(BF16))
    ).astype(BF16)
    krs = Reduce(
        pc, snd, lambda q, w: wk.at[slab_rows(q, w)], kfirst, kfx, kfy, ksem
    )
    krs.diagonal()
    krs.straight_x()
    krs.straight_y()
    qrs.merge(add_into)
    krs.merge(add_into)
    ers[2].merge(add_far)

    def piece(q, w):
        return pl.ds(pl.multiple_of((chip * 2 + w) * per + q * rp, 16), rp)

    groups = (
        (brs, lambda rows: wb.at[rows], zrb, rzb, fb, frb),
        (qrs, lambda rows: wq.at[rows], zrq, rzq, fq, frq),
        (krs, lambda rows: wk.at[rows], zrk, rzk, fk, frk),
    )

    def column_out(which):
        rs, at, zrecv, rz, _, _ = groups[which]
        rs.wait()
        for w in range(2):
            dst = rs.slab(chip, w)
            dst[...] = (
                dst[...].astype(F32) + rs.fx[w].astype(F32) + rs.fy[w].astype(F32)
            ).astype(BF16)
        for q in nearest[::-1]:
            to = seat(z, q)
            for w in range(2):
                snd.start(at(piece(q, w)), zrecv.at[to, w], rz.at[2 * to + w], (c, q))

    def column_in(which):
        _, at, zrecv, rz, fin, get = groups[which]
        for w in range(2):
            tot = at(piece(z, w))[...].astype(F32)
            for i in range(nz - 1):
                arrived(zrecv.at[i, w], rz.at[2 * i + w])
                tot = tot + zrecv[i, w].astype(F32)
            fin[w] = tot
        snd.start(fin.at[1 - core], get, rmisc.at[5 + which], sib)

    e_own = []
    e_outs = (eg_out, eu_out, ed_out)

    def expert_final(m):
        ers[m].wait()
        got = [
            fetch(src.at[m, w], room, 2 * m + w)
            for src, room in ((efx, gr), (efy, xm)) for w in range(2)
        ]
        for _, cp in got:
            cp.wait()
        for w in range(2):
            dst = ers[m].slab(chip, w)
            tot = dst[...].astype(F32) + got[w][0][...].astype(F32)
            dst[...] = (tot + got[2 + w][0][...].astype(F32)).astype(BF16)
        snd.start(ers[m].slab(chip, 1 - core), esibr.at[m], rmisc.at[2 + m], sib)
        e_own.append(loads.local(ers[m].slab(chip, core), e_outs[m].at[core]))

    column_out(0)
    expert_final(0)
    expert_final(1)
    osum = okeep[nz - 1].astype(F32) + h1s[...]
    base = nz * t2 - (nz - 1) * t0
    room = [xm.at[pl.ds(base + i * t0, t0)] for i in range(nz - 1)]
    got = []
    for i in range(nz - 1):
        arrived(ozr.at[i], oz_r.at[i])
        got.append(loads.local(ozr.at[i], room[i]))
    for i in range(nz - 1):
        got[i].wait()
        osum = osum + room[i][...].astype(F32)
    out_ref[...] = osum
    column_out(1)
    column_in(0)
    column_out(2)
    for m in range(2):
        arrived(esibr.at[m], rmisc.at[2 + m])
        e_own.append(loads.local(esibr.at[m], e_outs[m].at[1 - core]))
    column_in(1)
    expert_final(2)
    column_in(2)
    arrived(esibr.at[2], rmisc.at[4])
    e_own.append(loads.local(esibr.at[2], e_outs[2].at[1 - core]))

    def half(k, count):
        return pl.ds(pl.multiple_of(k * count, 128), count)

    for k, (out, count, fin, get, off) in enumerate((
        (gwo_out, qw, fb, frb, 0), (gwq_out, qw, fq, frq, 0),
        (gwk_out, HEAD, fk, frk, 0), (gwv_out, HEAD, fk, frk, HEAD),
    )):
        if k < 3:
            arrived(get, rmisc.at[5 + k])
        out[:, half(core, count)] = fin[core, :, off:off + count]
        out[:, half(1 - core, count)] = get[:, off:off + count]
    square[...] = jnp.zeros(square.shape, F32)
    square[0:rp] = fk[core, :, 2 * HEAD:] + frk[:, 2 * HEAD:]
    turned = square[...].T
    gwr_out[...] = turned[0:gwr_out.shape[0], 0:rp]
    gna_out[...] = turned[8:9, 0:rp]
    gnm_out[...] = turned[9:10, 0:rp]
    for cp in e_own:
        cp.wait()
    for i in range(nz - 1):
        for cp in gz_copies(i):
            cp.wait_send()
        oz_copy(i).wait_send()
    snd.drain()


def cfg_experts(cfg):
    return cfg[7]


def layer_call(cfg, args):
    nctx, nz, width, rp, t0, heads, fc, eloc = cfg
    nch, t2, dp = nctx // 2, 2 * t0, nctx * nz * rp
    qw = heads * HEAD
    kx = 3 * HEAD
    ca = qw + kx
    keys = nch * t2
    rows = nz * t2
    per = nz * rp
    experts = args[9].shape[0]
    vm = pl.BlockSpec(memory_space=pltpu.VMEM)
    hb = pl.BlockSpec(memory_space=pltpu.HBM)
    sds = jax.ShapeDtypeStruct
    dma = pltpu.SemaphoreType.DMA
    v = pltpu.VMEM
    return pl.pallas_call(
        functools.partial(layer_kernel, cfg),
        out_shape=(
            sds((t0, dp), F32), sds((t0, dp), F32),
            sds((2, per, fc), BF16), sds((2, per, fc), BF16), sds((2, per, fc), BF16),
            sds((rp, 2 * qw), F32), sds((rp, 2 * HEAD), F32), sds((rp, 2 * HEAD), F32),
            sds((rp, 2 * qw), F32), sds((1, rp), F32), sds((1, rp), F32), sds((experts, rp), F32),
        ) + (sds((3, 2, per, fc), BF16),) * 3 + (sds((nz - 1, t0, dp), BF16),),
        in_specs=[vm] * 10 + [hb] * 5,
        out_specs=(vm, vm, hb, hb, hb) + (vm,) * 7 + (hb,) * 4,
        scratch_shapes=[
            v((dp, kx), BF16), v((dp, qw), BF16), v((dp, qw), BF16), v((3, dp, fc), BF16),
            v((nz * 2 * rp, kx), BF16), v((nz * 2 * rp, qw), BF16), v((nz * 2 * rp, qw), BF16),
            v((2, t0, dp), BF16), v((t2, HEAD), F32), v((t2, HEAD), F32), v((128, 128), F32),
            v((t2, qw), BF16), v((keys, 2 * HEAD), BF16), v((t2, 128), F32), v((t2, qw), BF16),
            v((t2, dp), BF16), v((t0, dp), F32),
            v((rows, dp), BF16), v((rows, dp), BF16), v((rows, 128), F32),
            v((rows, 2 * fc), BF16), v((rows, fc), BF16),
            v((nz, t0, dp), BF16), v((nz, t0, dp), BF16), v((nz, t0, dp), BF16),
            v((nz - 1, t0, dp), BF16), v((nz, t0, dp), BF16),
            v((nz, 8, t0), F32), v((nz, 8, t0), F32), v((nz, 8, t0), F32),
            v((nz - 1, 8, t0), F32),
            v((nz * 2 * 8, t0), F32),
            v((t2, dp), BF16), v((keys, 2 * HEAD), F32), v((keys, 2 * HEAD), BF16),
            v((nch - 1, t2, 2 * HEAD), BF16), v((t2, ca - 128), BF16),
            v((t2, dp), F32), v((t0, dp), F32), v((dp, 128), F32),
            v((3, per, fc), BF16),
            v((2, per, qw), BF16), v((2, per, qw), BF16), v((2, per, qw), BF16),
            v((2, per, qw), BF16), v((2, per, qw), BF16), v((2, per, qw), BF16),
            v((2, per, kx), BF16), v((2, per, kx), BF16), v((2, per, kx), BF16),
            v((nz - 1, 2, rp, qw), BF16), v((nz - 1, 2, rp, qw), BF16),
            v((nz - 1, 2, rp, kx), BF16),
            v((2, rp, qw), F32), v((2, rp, qw), F32), v((2, rp, kx), F32),
            v((rp, qw), F32), v((rp, qw), F32), v((rp, kx), F32),
            v((8, t2), F32),
            dma((300,)), dma((60,)), dma((nctx * nz,)), dma((nctx * nz,)), dma((nctx * nz,)),
            dma((6 * nctx,)), dma((nz,)), dma((nz,)), dma((nz,)), dma((2,)), dma((3 * nz,)), dma((3 * nz,)),
            dma((2 * nz,)), dma((2 * nz,)), dma((2 * nz,)), dma((2 * nz,)),
            dma((nz,)), dma((nz,)), dma((nz,)), dma((nz,)), dma((8,)), dma((3, 6)), dma((6,)),
            dma((6,)), dma((6,)), dma((nch,)), dma((nch,)), dma((2 * nz,)), dma((2 * nz,)),
            dma((2 * nz,)),
        ],
        compiler_params=pltpu.CompilerParams(
            collective_id=0, has_side_effects=True, vmem_limit_bytes=64 * 2**20
        ),
        name="layer",
    )(*args)


def pass_kernel(count, pairs, *refs):
    total = count + pairs
    for k in range(count):
        refs[total + k][...] = refs[k][...]
    for k in range(count, total):
        for half in range(2):
            refs[total + k][:, half, :] = refs[k][half].astype(F32)


def pass_on(arrays, pairs):
    vm = pl.BlockSpec(memory_space=pltpu.VMEM)
    sds = jax.ShapeDtypeStruct
    out_shape = [sds(x.shape, x.dtype) for x in arrays]
    out_shape += [sds((x.shape[1], 2, x.shape[2]), F32) for x in pairs]
    return pl.pallas_call(
        functools.partial(pass_kernel, len(arrays), len(pairs)),
        out_shape=tuple(out_shape),
        in_specs=[vm] * len(out_shape),
        out_specs=(vm,) * len(out_shape),
        name="pass_on",
    )(*arrays, *pairs)


def body(hidden, routes, cot, na, wq, wk, wv, wo, nm, wr, wg, wu, wd):
    nctx, nz = lax.axis_size("ctx"), lax.axis_size("wsh")
    t0, width = hidden.shape[1], hidden.shape[2]
    rp = wq.shape[1]
    eloc, ff = wg.shape[2], wg.shape[3]
    heads = wq.shape[2] // HEAD // 2
    fc = eloc * ff // 2
    cfg = (nctx, nz, width, rp, t0, heads, fc, eloc)
    pos = np.arange(nctx * t0, dtype=np.float32)
    freq = np.float32(BASE) ** (-np.arange(HEAD // 2, dtype=np.float32) * 2.0 / HEAD)
    ang = pos[:, None] * freq.astype(np.float32)[None, :]
    cos, sin = np.cos(ang), np.sin(ang)
    cosf = jnp.asarray(np.concatenate([cos, cos], axis=1), F32)
    sinf = jnp.asarray(np.concatenate([-sin, sin], axis=1), F32)
    halves = [jnp.transpose(w[0], (1, 0, 2)) for w in (wg, wu, wd)]
    r = layer_call(
        cfg,
        (hidden[0], routes[0, 0].T, cot[0], wq[0], wk[0], wv[0], wo[0], na, nm, wr[0].T, *halves,
         cosf, sinf),
    )
    out, ig, eg, eu, ed, gwq, gwk, gwv, gwo, gna, gnm, gwr = r[:12]
    out, ig, gwq, gwk, gwv, gwo, gna, gnm, gwr, eg, eu, ed = pass_on(
        (out, ig, gwq, gwk, gwv, gwo, gna, gnm, gwr), (eg, eu, ed)
    )
    return (
        out[None], ig[None], gna, gwq[None], gwk[None], gwv[None], gwo[None],
        gnm, gwr.T[None], eg[None], eu[None], ed[None],
    )


def shifted(value, axis, steps):
    count = lax.axis_size(axis)
    pairs = [(source, (source + steps) % count) for source in range(count)]
    return lax.ppermute(value, axis, pairs)


def normalize(hidden_state, gain):
    return (
        hidden_state
        * lax.rsqrt(jnp.mean(hidden_state * hidden_state, axis=-1, keepdims=True) + NORM_EPSILON)
        * gain
    )


def rotary(token_positions, head_size):
    half_size = head_size // 2
    frequency = ROTARY_BASE ** (-jnp.arange(half_size, dtype=jnp.float32) * 2.0 / head_size)
    angles = token_positions.astype(jnp.float32)[:, None] * frequency[None, :]
    return (jnp.cos(angles)[:, None, :], jnp.sin(angles)[:, None, :])


def apply_rotary(values_in, cosine, sine_rows, direction):
    half_size = values_in.shape[-1] // 2
    first_half = values_in[..., :half_size]
    second = values_in[..., half_size:]
    return jnp.concatenate(
        [
            first_half * cosine - direction * second * sine_rows,
            second * cosine + direction * first_half * sine_rows,
        ],
        axis=-1,
    )


def slot_targets(picks_in, matches):
    flat_matches = matches.reshape(-1, matches.shape[-1]).astype(jnp.int32)
    earlier = jnp.cumsum(flat_matches, axis=0) - flat_matches
    return picks_in.reshape(-1) * CAP + jnp.sum(earlier * flat_matches, axis=1)


def score_rows(query_low, key_rows, token_positions):
    total_rows = query_low.shape[0]
    head_size = query_low.shape[2]
    grouped_heads = query_low.reshape(total_rows, key_rows.shape[1], -1, head_size)
    scores = jnp.einsum(
        "qhgd,khd->hgqk", grouped_heads, key_rows, preferred_element_type=jnp.float32
    ) * head_size ** (-0.5)
    allowed = jnp.arange(key_rows.shape[0], dtype=jnp.int32)[None, :] <= token_positions[:, None]
    return (grouped_heads, jnp.where(allowed[None, None], scores, -1e30))


def attend(query_low, key_rows, value_rows, token_positions):
    grouped_heads, scores = score_rows(query_low, key_rows, token_positions)
    highest = jnp.max(scores, axis=-1, keepdims=True)
    log_total = highest + jnp.log(jnp.sum(jnp.exp(scores - highest), axis=-1, keepdims=True))
    weights = jnp.exp(scores - log_total).astype(jnp.bfloat16)
    attended = jnp.einsum("hgqk,khd->qhgd", weights, value_rows, preferred_element_type=jnp.float32)
    return (attended.reshape(query_low.shape[0], -1), log_total)


def attend_grad(query_low, key_rows, value_rows, token_positions, log_total, grad_mixed):
    grouped_heads, scores = score_rows(query_low, key_rows, token_positions)
    score_scale = query_low.shape[-1] ** (-0.5)
    softmax_rows = jnp.exp(scores - log_total)
    weights = softmax_rows.astype(jnp.bfloat16)
    grad_grouped = grad_mixed.reshape(grouped_heads.shape)
    grad_weights = jnp.einsum(
        "qhgd,khd->hgqk", grad_grouped, value_rows, preferred_element_type=jnp.float32
    )
    grad_values = jnp.einsum(
        "hgqk,qhgd->khd", weights, grad_grouped, preferred_element_type=jnp.float32
    )
    row_inner = jnp.sum(softmax_rows * grad_weights, axis=-1, keepdims=True)
    grad_scores = (softmax_rows * (grad_weights - row_inner)).astype(jnp.bfloat16)
    grad_query = (
        jnp.einsum("hgqk,khd->qhgd", grad_scores, key_rows, preferred_element_type=jnp.float32)
        * score_scale
    )
    grad_keys = (
        jnp.einsum("hgqk,qhgd->khd", grad_scores, grouped_heads, preferred_element_type=jnp.float32)
        * score_scale
    )
    return (grad_query.reshape(query_low.shape), grad_keys, grad_values)


def collect_key_grads(grad_keys, grad_values, total_rows):
    cycle_size = lax.axis_size("ctx")
    own_index = lax.axis_index("ctx")
    both_grads = jnp.stack([grad_keys, grad_values])

    def block_piece(block_index):
        return lax.dynamic_slice_in_dim(both_grads, block_index * total_rows, total_rows, 1)

    def cycle_step(step_index, carried):
        moved = shifted(carried.astype(jnp.bfloat16), "ctx", -1).astype(carried.dtype)
        block_index = (own_index + step_index) % cycle_size
        weight_now = jnp.where(step_index < cycle_size, 1.0, 0.0).astype(jnp.float32)
        return moved + weight_now * block_piece(block_index)

    collected = lax.fori_loop(1, cycle_size + 1, cycle_step, block_piece(own_index))
    return (collected[0], collected[1])


def forward_layer(hidden_state, picks_in, dense_set, expert_set):
    gain_attn, query_matrix, key_matrix, value_matrix, output_matrix, gain_moe, router_matrix = (
        dense_set
    )
    gate_w, up_w, down_w = expert_set
    total_rows, model_width = hidden_state.shape
    token_positions = lax.axis_index("ctx") * total_rows + jnp.arange(total_rows, dtype=jnp.int32)
    cosine, sine_rows = rotary(token_positions, HEAD_DIM)
    attention_normed = normalize(hidden_state, gain_attn.astype(jnp.float32)).astype(jnp.bfloat16)
    query_unrotated = jnp.dot(
        attention_normed, query_matrix, preferred_element_type=jnp.float32
    ).reshape(total_rows, QUERY_HEADS, HEAD_DIM)
    key_unrotated = jnp.dot(
        attention_normed, key_matrix, preferred_element_type=jnp.float32
    ).reshape(total_rows, KEY_VALUE_HEADS, HEAD_DIM)
    query_low = apply_rotary(query_unrotated, cosine, sine_rows, 1.0).astype(jnp.bfloat16)
    key_low = apply_rotary(key_unrotated, cosine, sine_rows, 1.0).astype(jnp.bfloat16)
    value_low = (
        jnp.dot(attention_normed, value_matrix, preferred_element_type=jnp.float32)
        .astype(jnp.bfloat16)
        .reshape(total_rows, KEY_VALUE_HEADS, HEAD_DIM)
    )
    key_rows, value_rows = (
        lax.all_gather(key_low, "ctx", axis=0, tiled=True),
        lax.all_gather(value_low, "ctx", axis=0, tiled=True),
    )
    attended, log_total = attend(query_low, key_rows, value_rows, token_positions)
    mixed_reduced = attended.astype(jnp.bfloat16)
    post_attention = hidden_state + lax.dot_general(
        mixed_reduced, output_matrix, (((1,), (1,)), ((), ())), preferred_element_type=jnp.float32
    )
    expert_normed = normalize(post_attention, gain_moe.astype(jnp.float32)).astype(jnp.bfloat16)
    router_logits = jnp.dot(expert_normed, router_matrix, preferred_element_type=jnp.float32)
    expert_count = router_logits.shape[1]
    matches = picks_in[:, :, None] == jnp.arange(expert_count, dtype=jnp.int32)[None, None, :]
    gate_weights = jax.nn.softmax(
        jnp.sum(jnp.where(matches, router_logits[:, None, :], 0.0), axis=-1), axis=-1
    )
    targets = slot_targets(picks_in, matches)
    outgoing = (
        jnp.zeros((expert_count * CAP, model_width), jnp.bfloat16)
        .at[targets]
        .set(jnp.repeat(expert_normed, TOP, axis=0))
    )
    group_count = lax.axis_size("wsh")
    local_count = gate_w.shape[1]
    arrived = lax.all_to_all(
        outgoing.reshape(group_count, local_count, CAP, model_width),
        "wsh",
        split_axis=0,
        concat_axis=0,
        tiled=True,
    )
    gate_pre = jnp.einsum("sjcd,djf->sjcf", arrived, gate_w, preferred_element_type=jnp.float32)
    up_pre = jnp.einsum("sjcd,djf->sjcf", arrived, up_w, preferred_element_type=jnp.float32)
    activations = (jax.nn.silu(gate_pre) * up_pre).astype(jnp.bfloat16)
    produced = jnp.einsum(
        "sjcf,djf->sjcd", activations, down_w, preferred_element_type=jnp.float32
    ).astype(jnp.bfloat16)
    returned = lax.all_to_all(produced, "wsh", split_axis=0, concat_axis=0, tiled=True)
    returned, arrived, gate_pre, up_pre = (returned, arrived, gate_pre, up_pre)
    picked = (
        returned.reshape(-1, model_width)[targets]
        .reshape(total_rows, TOP, model_width)
        .astype(jnp.float32)
    )
    after_moe = post_attention + jnp.sum(gate_weights[:, :, None] * picked, axis=1)
    stored = (
        hidden_state,
        attention_normed,
        query_low,
        key_low,
        value_low,
        log_total,
        mixed_reduced,
        post_attention,
        expert_normed,
        matches,
        gate_weights,
        targets,
        picked,
        arrived,
        gate_pre,
        up_pre,
    )
    return (after_moe, stored, (key_rows, value_rows))


def backward_layer(incoming, stored, dense_set, expert_set, key_rows, value_rows):
    (
        hidden_state,
        attention_normed,
        query_low,
        key_low,
        value_low,
        log_total,
        mixed_reduced,
        post_attention,
        expert_normed,
        matches,
        gate_weights,
        targets,
        picked,
        arrived,
        gate_pre,
        up_pre,
    ) = stored
    gain_attn, query_matrix, key_matrix, value_matrix, output_matrix, gain_moe, router_matrix = (
        dense_set
    )
    gate_w, up_w, down_w = expert_set
    total_rows, model_width = hidden_state.shape
    token_positions = lax.axis_index("ctx") * total_rows + jnp.arange(total_rows, dtype=jnp.int32)
    cosine, sine_rows = rotary(token_positions, HEAD_DIM)
    grad_y = (gate_weights[:, :, None] * incoming[:, None, :]).astype(jnp.bfloat16)
    grad_gates = jnp.sum(incoming[:, None, :] * picked, axis=-1)
    grad_chosen = gate_weights * (
        grad_gates - jnp.sum(gate_weights * grad_gates, axis=-1, keepdims=True)
    )
    grad_logits = jnp.sum(jnp.where(matches, grad_chosen[:, :, None], 0.0), axis=1).astype(
        jnp.bfloat16
    )
    slot_total = arrived.shape[0] * arrived.shape[1] * arrived.shape[2]
    outgoing = (
        jnp.zeros((slot_total, model_width), jnp.bfloat16)
        .at[targets]
        .set(grad_y.reshape(-1, model_width))
    )
    grad_arrived = lax.all_to_all(
        outgoing.reshape(arrived.shape), "wsh", split_axis=0, concat_axis=0, tiled=True
    )
    grad_acts = jnp.einsum(
        "sjcd,djf->sjcf", grad_arrived, down_w, preferred_element_type=jnp.float32
    )
    sigmoid_gate = jax.nn.sigmoid(gate_pre)
    silu_gate = jax.nn.silu(gate_pre)
    activations = (silu_gate * up_pre).astype(jnp.bfloat16)
    grad_gate = (
        grad_acts * up_pre * sigmoid_gate * (1.0 + gate_pre * (1.0 - sigmoid_gate))
    ).astype(jnp.bfloat16)
    grad_up = (grad_acts * silu_gate).astype(jnp.bfloat16)
    grad_rows = (
        jnp.einsum("sjcf,djf->sjcd", grad_gate, gate_w, preferred_element_type=jnp.float32)
        + jnp.einsum("sjcf,djf->sjcd", grad_up, up_w, preferred_element_type=jnp.float32)
    ).astype(jnp.bfloat16)
    grad_back = lax.all_to_all(grad_rows, "wsh", split_axis=0, concat_axis=0, tiled=True)
    expert_grads = (
        lax.psum_scatter(
            jnp.einsum(
                "sjcd,sjcf->djf", arrived, grad_gate, preferred_element_type=jnp.float32
            ).astype(jnp.bfloat16),
            "ctx",
            scatter_dimension=0,
            tiled=True,
        ).astype(jnp.float32),
        lax.psum_scatter(
            jnp.einsum(
                "sjcd,sjcf->djf", arrived, grad_up, preferred_element_type=jnp.float32
            ).astype(jnp.bfloat16),
            "ctx",
            scatter_dimension=0,
            tiled=True,
        ).astype(jnp.float32),
        lax.psum_scatter(
            jnp.einsum(
                "sjcd,sjcf->djf", grad_arrived, activations, preferred_element_type=jnp.float32
            ).astype(jnp.bfloat16),
            "ctx",
            scatter_dimension=0,
            tiled=True,
        ).astype(jnp.float32),
    )
    returned_rows = (
        grad_back.reshape(-1, model_width)[targets]
        .reshape(total_rows, TOP, model_width)
        .astype(jnp.float32)
    )
    grad_normed_moe = jnp.sum(returned_rows, axis=1) + lax.dot_general(
        grad_logits, router_matrix, (((1,), (1,)), ((), ())), preferred_element_type=jnp.float32
    )
    router_term = jnp.einsum(
        "td,te->de", expert_normed, grad_logits, preferred_element_type=jnp.float32
    )
    unused_moe, pull_moe = jax.vjp(normalize, post_attention, gain_moe.astype(jnp.float32))
    grad_after_norm, gain_moe_term = pull_moe(grad_normed_moe)
    grad_after_attn = incoming + grad_after_norm
    grad_attn = grad_after_attn.astype(jnp.bfloat16)
    out_term = jnp.einsum("td,tj->dj", grad_attn, mixed_reduced, preferred_element_type=jnp.float32)
    grad_mixed = jnp.dot(grad_attn, output_matrix, preferred_element_type=jnp.float32).astype(
        jnp.bfloat16
    )
    grad_query, grad_keys, grad_values = attend_grad(
        query_low, key_rows, value_rows, token_positions, log_total, grad_mixed
    )
    grad_key, grad_value = collect_key_grads(grad_keys, grad_values, total_rows)
    grad_query_raw = (
        apply_rotary(grad_query, cosine, sine_rows, -1.0)
        .reshape(total_rows, -1)
        .astype(jnp.bfloat16)
    )
    grad_key_raw = (
        apply_rotary(grad_key, cosine, sine_rows, -1.0).reshape(total_rows, -1).astype(jnp.bfloat16)
    )
    grad_value_raw = grad_value.reshape(total_rows, -1).astype(jnp.bfloat16)
    contract_last = (((1,), (1,)), ((), ()))
    grad_normed_attn = lax.dot_general(
        grad_query_raw, query_matrix, contract_last, preferred_element_type=jnp.float32
    )
    grad_normed_attn = grad_normed_attn + lax.dot_general(
        grad_key_raw, key_matrix, contract_last, preferred_element_type=jnp.float32
    )
    grad_normed_attn = grad_normed_attn + lax.dot_general(
        grad_value_raw, value_matrix, contract_last, preferred_element_type=jnp.float32
    )
    query_term = jnp.einsum(
        "td,tf->df", attention_normed, grad_query_raw, preferred_element_type=jnp.float32
    )
    key_term = jnp.einsum(
        "td,tf->df", attention_normed, grad_key_raw, preferred_element_type=jnp.float32
    )
    value_term = jnp.einsum(
        "td,tf->df", attention_normed, grad_value_raw, preferred_element_type=jnp.float32
    )
    unused_attn, pull_attn = jax.vjp(normalize, hidden_state, gain_attn.astype(jnp.float32))
    grad_before, gain_attn_term = pull_attn(grad_normed_attn)
    layer_grads = (
        lax.psum_scatter(gain_attn_term, ("ctx", "wsh"), scatter_dimension=0, tiled=True),
        lax.psum_scatter(query_term, ("ctx", "wsh"), scatter_dimension=0, tiled=True),
        lax.psum_scatter(key_term, ("ctx", "wsh"), scatter_dimension=0, tiled=True),
        lax.psum_scatter(value_term, ("ctx", "wsh"), scatter_dimension=0, tiled=True),
        lax.psum_scatter(out_term, ("ctx", "wsh"), scatter_dimension=0, tiled=True),
        lax.psum_scatter(gain_moe_term, ("ctx", "wsh"), scatter_dimension=0, tiled=True),
        lax.psum_scatter(router_term, ("ctx", "wsh"), scatter_dimension=0, tiled=True),
    )
    return (grad_after_attn + grad_before, layer_grads, expert_grads)


def plain_body(
    hidden_in,
    routes,
    cotangent,
    norm_attn,
    w_query,
    key_projection,
    value_projection,
    w_out,
    norm_moe,
    w_router,
    w_gate,
    w_up,
    w_down,
):
    hidden_state = hidden_in[0].astype(jnp.float32)
    layer_number = 0
    dense_set = (
        lax.all_gather(norm_attn[layer_number], ("ctx", "wsh"), axis=0, tiled=True),
        lax.all_gather(w_query[layer_number], ("ctx", "wsh"), axis=0, tiled=True),
        lax.all_gather(key_projection[layer_number], ("ctx", "wsh"), axis=0, tiled=True),
        lax.all_gather(value_projection[layer_number], ("ctx", "wsh"), axis=0, tiled=True),
        lax.all_gather(w_out[layer_number], ("ctx", "wsh"), axis=0, tiled=True),
        lax.all_gather(norm_moe[layer_number], ("ctx", "wsh"), axis=0, tiled=True),
        lax.all_gather(w_router[layer_number], ("ctx", "wsh"), axis=0, tiled=True),
    )
    expert_set = (
        lax.all_gather(w_gate[layer_number], "ctx", axis=0, tiled=True),
        lax.all_gather(w_up[layer_number], "ctx", axis=0, tiled=True),
        lax.all_gather(w_down[layer_number], "ctx", axis=0, tiled=True),
    )
    hidden_state, stored, gathered = forward_layer(
        hidden_state, routes[layer_number, 0], dense_set, expert_set
    )
    records = [(stored, None, None, None)]
    incoming = cotangent[0]
    dense_grads = []
    expert_grads = []
    layer_number = 0
    stored, dense_set, expert_set, gathered = records[layer_number]
    dense_set = (
        lax.all_gather(norm_attn[layer_number], ("ctx", "wsh"), axis=0, tiled=True),
        lax.all_gather(w_query[layer_number], ("ctx", "wsh"), axis=0, tiled=True),
        lax.all_gather(key_projection[layer_number], ("ctx", "wsh"), axis=0, tiled=True),
        lax.all_gather(value_projection[layer_number], ("ctx", "wsh"), axis=0, tiled=True),
        lax.all_gather(w_out[layer_number], ("ctx", "wsh"), axis=0, tiled=True),
        lax.all_gather(norm_moe[layer_number], ("ctx", "wsh"), axis=0, tiled=True),
        lax.all_gather(w_router[layer_number], ("ctx", "wsh"), axis=0, tiled=True),
    )
    expert_set = (
        lax.all_gather(w_gate[layer_number], "ctx", axis=0, tiled=True),
        lax.all_gather(w_up[layer_number], "ctx", axis=0, tiled=True),
        lax.all_gather(w_down[layer_number], "ctx", axis=0, tiled=True),
    )
    gathered = (
        lax.all_gather(stored[3], "ctx", axis=0, tiled=True),
        lax.all_gather(stored[4], "ctx", axis=0, tiled=True),
    )
    incoming, layer_grads, layer_expert = backward_layer(
        incoming, stored, dense_set, expert_set, gathered[0], gathered[1]
    )
    dense_grads.insert(0, layer_grads)
    expert_grads.insert(0, layer_expert)
    stacked_dense = [
        jnp.stack([grads_item[position] for grads_item in dense_grads]) for position in range(7)
    ]
    stacked_expert = [
        jnp.stack([grads_item[position] for grads_item in expert_grads]) for position in range(3)
    ]
    return (
        hidden_state[None],
        incoming[None],
        stacked_dense[0],
        stacked_dense[1],
        stacked_dense[2],
        stacked_dense[3],
        stacked_dense[4],
        stacked_dense[5],
        stacked_dense[6],
        stacked_expert[0],
        stacked_expert[1],
        stacked_expert[2],
    )


def solution(mesh):
    return jax.shard_map(
        body if mesh.shape["ctx"] == 8 and mesh.shape["wsh"] == 4 else plain_body,
        mesh=mesh,
        in_specs=(
            P("wsh", "ctx", None),
            P(None, "wsh", "ctx", None),
            P("wsh", "ctx", None),
            P(None, ("ctx", "wsh")),
            P(None, ("ctx", "wsh"), None),
            P(None, ("ctx", "wsh"), None),
            P(None, ("ctx", "wsh"), None),
            P(None, ("ctx", "wsh"), None),
            P(None, ("ctx", "wsh")),
            P(None, ("ctx", "wsh"), None),
            P(None, "ctx", "wsh", None),
            P(None, "ctx", "wsh", None),
            P(None, "ctx", "wsh", None),
        ),
        out_specs=(
            P("wsh", "ctx", None),
            P("wsh", "ctx", None),
            P(None, ("ctx", "wsh")),
            P(None, ("ctx", "wsh"), None),
            P(None, ("ctx", "wsh"), None),
            P(None, ("ctx", "wsh"), None),
            P(None, ("ctx", "wsh"), None),
            P(None, ("ctx", "wsh")),
            P(None, ("ctx", "wsh"), None),
            P(None, "ctx", "wsh", None),
            P(None, "ctx", "wsh", None),
            P(None, "ctx", "wsh", None),
        ),
        check_vma=False,
    )
```

```python
import functools
import jax
import jax.numpy as jnp
import numpy as np
from jax import lax
from jax.experimental import pallas as pl
from jax.experimental.pallas import tpu as pltpu
from jax.sharding import PartitionSpec as P

QUERY_HEADS = 12
KEY_VALUE_HEADS = 2
HEAD_DIM = 128
CAP = 128
NORM_EPSILON = 1e-06
ROTARY_BASE = 1000000.0
MESH = pl.DeviceIdType.MESH
HEAD = 128
TOP = 4
EPS = 1e-06
BASE = 1000000.0
F32 = jnp.float32
BF16 = jnp.bfloat16


def dot(a, b):
    return lax.dot_general(a, b, (((1,), (0,)), ((), ())), preferred_element_type=F32)


def dot_t(a, b):
    return lax.dot_general(a, b, (((1,), (1,)), ((), ())), preferred_element_type=F32)


def t_dot(a, b):
    return lax.dot_general(a, b, (((0,), (0,)), ((), ())), preferred_element_type=F32)


class Place:
    def __init__(self, nctx, nz):
        self.nctx, self.nz, self.nch = nctx, nz, nctx // 2
        self.c = lax.axis_index("ctx")
        self.z = lax.axis_index("wsh")
        self.chip = self.c // 2
        self.core = self.c % 2
        self.sib = self.chip * 2 + 1 - self.core
        self.square = self.nch == 4

    def xchip(self):
        return self.chip + 1 - 2 * (self.chip % 2)

    def ychip(self):
        return (self.chip + 2) % 4

    def near(self, k):
        s = 0
        for here in range(self.nz):
            order = sorted(
                (v for v in range(self.nz) if v != here),
                key=lambda v: (abs(v - here), 2 * v // self.nz != 2 * here // self.nz),
            )
            s = jnp.where(self.z == here, order[k - 1], s)
        return s

    def zto(self, dz):
        return (self.z + dz) % self.nz

    def zfrom(self, dz):
        return (self.z + self.nz - dz) % self.nz


class Sends:
    def __init__(self, sems, count):
        self.sems, self.count, self.used, self.live = sems, count, 0, []

    def start(self, src, dst, rsem, dev, when=None):
        assert self.used < self.count
        cp = pltpu.make_async_remote_copy(
            src_ref=src,
            dst_ref=dst,
            send_sem=self.sems.at[self.used],
            recv_sem=rsem,
            device_id=dev,
            device_id_type=MESH,
        )
        if when is None:
            cp.start()
        else:
            pl.when(when)(cp.start)
        self.used += 1
        self.live.append((cp, when))

    def local(self, src, dst):
        assert self.used < self.count
        cp = pltpu.make_async_copy(src, dst, self.sems.at[self.used])
        cp.start()
        self.used += 1
        return cp

    def take(self):
        live, self.live = self.live, []
        return live

    def drain(self, live=None):
        for cp, when in self.take() if live is None else live:
            if when is None:
                cp.wait_send()
            else:
                pl.when(when)(cp.wait_send)


def arrived(ref, sem):
    pltpu.make_async_copy(ref, ref, sem).wait()


def greet(pc):
    bar = pltpu.get_barrier_semaphore()
    for k in range(1, pc.nctx):
        to = ((pc.c + k) % pc.nctx, pc.z)
        pl.semaphore_signal(bar, inc=1, device_id=to, device_id_type=MESH)
    for k in range(1, pc.nz):
        pl.semaphore_signal(bar, inc=1, device_id=(pc.c, pc.zto(k)), device_id_type=MESH)
    return lambda: pl.semaphore_wait(bar, pc.nctx + pc.nz - 2)


def rms(x, width):
    return lax.rsqrt(jnp.sum(x * x, axis=-1, keepdims=True) * (1.0 / width) + EPS)


def gain_row(extra, lane):
    pick = (lax.broadcasted_iota(jnp.int32, (16, extra.shape[1]), 1) == lane).astype(BF16)
    return dot_t(pick, extra)[0:1]


def rope(x, cos, sin):
    return x * cos + pltpu.roll(x, HEAD // 2, 1) * sin


class Reduce:
    def __init__(self, pc, snd, slab, first, fx, fy, sems):
        self.pc, self.snd, self.slab = pc, snd, slab
        self.first, self.fx, self.fy, self.sems = first, fx, fy, sems
        self.x, self.y, self.d = pc.xchip(), pc.ychip(), 3 - pc.chip

    def to(self, chip):
        return (chip * 2 + self.pc.core, self.pc.z)

    def diagonal(self):
        self.snd.start(self.slab(self.d, 0), self.first.at[0], self.sems.at[0], self.to(self.x))
        self.snd.start(self.slab(self.d, 1), self.first.at[1], self.sems.at[1], self.to(self.y))

    def straight_x(self):
        self.snd.start(self.slab(self.x, 0), self.fx.at[0], self.sems.at[2], self.to(self.x))

    def straight_y(self):
        self.snd.start(self.slab(self.y, 1), self.fy.at[1], self.sems.at[5], self.to(self.y))

    def merge(self, add):
        arrived(self.first.at[0], self.sems.at[0])
        add(self.slab(self.y, 0), self.first.at[0])
        self.snd.start(self.slab(self.y, 0), self.fy.at[0], self.sems.at[4], self.to(self.y))
        arrived(self.first.at[1], self.sems.at[1])
        add(self.slab(self.x, 1), self.first.at[1])
        self.snd.start(self.slab(self.x, 1), self.fx.at[1], self.sems.at[3], self.to(self.x))

    def wait(self):
        for w in range(2):
            arrived(self.fx.at[w], self.sems.at[2 + w])
            arrived(self.fy.at[w], self.sems.at[4 + w])


def add_into(dst, src):
    dst[...] = (dst[...].astype(F32) + src[...].astype(F32)).astype(BF16)


def layer_kernel(
    cfg,
    h_ref, routes_ref, cot_ref, wq_ref, wk_ref, wv_ref, wo_ref, ga_ref, gm_ref, wr_ref,
    eg_ref, eu_ref, ed_ref,
    cos_in, sin_in,
    out_ref, ig_ref, eg_out, eu_out, ed_out, gwq_out, gwk_out, gwv_out, gwo_out, gna_out, gnm_out, gwr_out,
    efirst, efx, efy, ozr,
    wk, wq, wb, we, zk, zq, zb, hbuf, cosr, sinr, square,
    qs, kv, lses, obs, xa, h1s, xm, gr, gts,
    ggu, ap, keep, sibs, sibr, zr, okeep, kgg, sgg, rgg, zgg, gtt,
    gat, gkv, gkvb, gkvr, graw, part, pget, exts,
    esibr,
    bfirst, bfx, bfy, qfirst, qfx, qfy, kfirst, kfx, kfy,
    zrb, zrq, zrk, fb, fq, fk, frb, frq, frk, rowp,
    ssem, lsem, rwk, rwq, rwb, re, rzk_, rzq_, rzb_, rfw, rxm, rxf,
    sib_s, sib_r, z_s, z_r, osib_s, osib_r, oz_s, oz_r, rmisc, esem, bsem,
    qsem, ksem, rkv, rkvf, rzb, rzq, rzk,
):
    nctx, nz, width, rp, t0, heads, fc, _ = cfg
    pc = Place(nctx, nz)
    nch = pc.nch
    t2 = 2 * t0
    qw = heads * HEAD
    kw = qw + 2 * HEAD
    kx = wk.shape[1]
    dp = wk.shape[0]
    core, z, c, chip = pc.core, pc.z, pc.c, pc.chip
    per = nz * rp
    met = greet(pc)
    snd = Sends(ssem, ssem.shape[0])
    loads = Sends(lsem, lsem.shape[0])
    sib = (pc.sib, z)
    mine = pl.ds(pl.multiple_of(chip * t2, t2), t2)
    mine0 = pl.ds(pl.multiple_of(core * t0, t0), t0)
    sib0 = pl.ds(pl.multiple_of((1 - core) * t0, t0), t0)
    xs, ys, ds = pc.xchip() * 2, pc.ychip() * 2, (3 - chip) * 2
    nearest = [pc.near(k) for k in range(1, nz)]

    def line_send(src, sem, order):
        for s in order:
            snd.start(src, src, sem, (c, s))

    def rows(cc, s):
        return pl.ds(pl.multiple_of((cc * nz + s) * rp, 16), rp)

    def slot(s, k):
        return pl.ds(pl.multiple_of(s * t2 + k * t0, t0), t0)

    def slot8(s, k):
        return pl.ds(pl.multiple_of((s * 2 + k) * 8, 8), 8)

    def both_parts(s):
        return pl.ds(pl.multiple_of(s * 2 * rp, 16), 2 * rp)

    def part_of(s, k):
        return pl.ds(pl.multiple_of((s * 2 + k) * rp, 16), rp)

    def slab_rows(q, w):
        return pl.ds(pl.multiple_of((q * 2 + w) * per, 16), per)

    tables = [loads.local(cos_in.at[mine], cosr), loads.local(sin_in.at[mine], sinr)]
    square[...] = jnp.zeros(square.shape, F32)
    experts = wr_ref.shape[0]
    square[0:experts, 0:rp] = wr_ref[...].astype(F32)
    square[8:9, 0:rp] = ga_ref[...].astype(F32)
    square[9:10, 0:rp] = gm_ref[...].astype(F32)
    ex = square[...].T[0:rp].astype(BF16)
    for k in range(2):
        at = part_of(z, k)
        zk[at, 0:HEAD] = wk_ref[:, k * HEAD:(k + 1) * HEAD]
        zk[at, HEAD:2 * HEAD] = wv_ref[:, k * HEAD:(k + 1) * HEAD]
        zk[at, 2 * HEAD:] = ex
        zq[at] = wq_ref[:, k * qw:(k + 1) * qw]
        zb[at] = wo_ref[:, k * qw:(k + 1) * qw]
    own = slot(z, core)
    gr[own] = cot_ref[...].astype(BF16)
    hbuf[core] = h_ref[...]
    met()

    def spread(src, dst, rs, s):
        here = dst.at[rows(c, s)]
        sem = rs.at[c * nz + s]
        for q in (pc.xchip(), pc.ychip()):
            for k in range(2):
                snd.start(src.at[part_of(s, k)], here, sem, (q * 2 + k, z))
        snd.start(src.at[part_of(s, 1 - core)], here, sem, sib)

    def forward(dst, rs, s):
        for source, to in ((ys, pc.xchip()), (xs + 1, pc.ychip())):
            here = dst.at[rows(source, s)]
            sem = rs.at[source * nz + s]
            arrived(here, sem)
            snd.start(here, here, sem, (to * 2 + core, z))

    def settle(dst, rs):
        for cc in (pc.sib, xs, ys + 1, ds, ds + 1):
            for s in range(nz):
                arrived(dst.at[rows(cc, s)], rs.at[cc * nz + s])

    packs = ((zk, rzk_, wk, rwk), (zq, rzq_, wq, rwq), (zb, rzb_, wb, rwb))
    for ref, rs, _, _ in packs:
        line_send(ref.at[both_parts(z)], rs.at[z], nearest)
    line_send(gr.at[own], rxm.at[z], nearest)
    keeps = ([], [], [])
    snd.start(hbuf.at[core], hbuf.at[core], rfw.at[0], sib)
    for (ref, _, dst, rs), kept in zip(packs, keeps):
        spread(ref, dst, rs, z)
        kept.append(loads.local(ref.at[part_of(z, core)], dst.at[rows(c, z)]))
    snd.start(gr.at[own], gr.at[own], rxf.at[z], sib)

    def column(which):
        ref, zs, dst, rs = packs[which]
        for s in nearest:
            arrived(ref.at[both_parts(s)], zs.at[s])
            spread(ref, dst, rs, s)
            keeps[which].append(loads.local(ref.at[part_of(s, core)], dst.at[rows(c, s)]))

    def onward(which):
        _, _, dst, rs = packs[which]
        for s in [z] + nearest:
            forward(dst, rs, s)

    def have(which):
        _, _, dst, rs = packs[which]
        for cp in keeps[which]:
            cp.wait()
        settle(dst, rs)

    column(0)
    onward(0)
    column(1)
    arrived(hbuf.at[1 - core], rfw.at[0])
    for cp in tables:
        cp.wait()
    have(0)
    cos, sin = cosr[...], sinr[...]
    extra = wk[:, 2 * HEAD:]
    gain_a = gain_row(extra, 8)
    gain_m = gain_row(extra, 9)
    for k in range(2):
        hk = hbuf[k].astype(F32)
        xa[pl.ds(k * t0, t0)] = (hk * rms(hk, width) * gain_a).astype(BF16)
    xav = xa[...]
    kraw = dot(xav, wk[:, :2 * HEAD])
    kv[mine, 0:HEAD] = rope(kraw[:, :HEAD], cos, sin).astype(BF16)
    kv[mine, HEAD:] = kraw[:, HEAD:].astype(BF16)
    for k in range(1, nch):
        snd.start(kv.at[mine], kv.at[mine], rkvf.at[k], (((chip + k) % nch) * 2 + core, z))
    onward(1)
    column(2)

    fh = fc // 2

    def mats(m, j, cc):
        at = pl.ds(pl.multiple_of(cc * per, 16), per)
        return we.at[m, at, pl.ds(j * fh, fh)]

    experts_in = (eg_ref, eu_ref, ed_ref)
    own_e = [
        loads.local(experts_in[m].at[core], we.at[m, pl.ds(pl.multiple_of(c * per, 16), per)])
        for m in range(3)
    ]

    def expert_spread(m, j):
        here = mats(m, j, c)
        sem = re.at[(2 * m + j) * nctx + c]
        half = pl.ds(j * fh, fh)
        for q in (pc.xchip(), pc.ychip()):
            for k in range(2):
                snd.start(experts_in[m].at[k, :, half], here, sem, (q * 2 + k, z))
        snd.start(experts_in[m].at[1 - core, :, half], here, sem, sib)

    def expert_onward(m, j):
        for source, to in ((ys, pc.xchip()), (xs + 1, pc.ychip())):
            here = mats(m, j, source)
            sem = re.at[(2 * m + j) * nctx + source]
            arrived(here, sem)
            snd.start(here, here, sem, (to * 2 + core, z))

    def expert_have(m, j):
        for cc in (pc.sib, xs, ys + 1, ds, ds + 1):
            arrived(mats(m, j, cc), re.at[(2 * m + j) * nctx + cc])
        if j == 0:
            own_e[m].wait()

    units = [(m, j) for j in range(2) for m in (2, 0, 1)]
    dense_sends = snd.take()
    expert_spread(*units[0])
    have(1)
    for hd in range(heads):
        cols = slice(hd * HEAD, (hd + 1) * HEAD)
        qs[:, cols] = rope(dot(xav, wq[:, cols]), cos, sin).astype(BF16)
    onward(2)
    for unit in units[1:]:
        expert_spread(*unit)
    for k in range(1, nch):
        other = pl.ds(pl.multiple_of(((chip + nch - k) % nch) * t2, t2), t2)
        arrived(kv.at[other], rkvf.at[k])

    keys = nch * t2
    scale = HEAD ** -0.5
    ok = lax.broadcasted_iota(jnp.int32, (t2, keys), 1) <= (
        chip * t2 + lax.broadcasted_iota(jnp.int32, (t2, keys), 0)
    )
    lane = lax.broadcasted_iota(jnp.int32, (t2, 128), 1)
    lane0 = lax.broadcasted_iota(jnp.int32, (t0, 128), 1)
    lses[...] = jnp.zeros((t2, 128), F32)

    def head_forward(hd, carry):
        cols = pl.ds(pl.multiple_of(hd * HEAD, HEAD), HEAD)
        s = dot_t(qs[:, cols], kv[:, 0:HEAD]) * scale
        s = jnp.where(ok, s, -1e30)
        m = jnp.max(s, axis=-1, keepdims=True)
        e = jnp.exp(s - m)
        total = jnp.sum(e, axis=-1, keepdims=True)
        lses[...] = jnp.where(lane == hd, m + jnp.log(total), lses[...])
        p = (e * (1.0 / total)).astype(BF16)
        obs[:, cols] = dot(p, kv[:, HEAD:]).astype(BF16)
        return carry

    def tokens_in(i, s):
        buf, at = tokens[i]
        here = buf.at[at(s, core)]
        arrived(here, rxm.at[i * nz + s])
        snd.start(here, here, rxf.at[i * nz + s], sib)

    tokens = ((gr, slot), (xm, slot), (gtt, slot8))
    lax.fori_loop(0, heads, head_forward, 0)
    expert_onward(*units[0])
    have(2)
    part[...] = dot_t(obs[...], wb[...])
    snd.start(part.at[sib0], pget, rfw.at[1], sib)
    arrived(pget, rfw.at[1])
    h1 = h_ref[...].astype(F32) + part[mine0] + pget[...]
    h1s[...] = h1
    xmv = (h1 * rms(h1, width) * gain_m).astype(BF16)
    xm[own] = xmv
    picks = jnp.zeros((128, t0), F32)
    for k in range(TOP):
        row = lax.broadcasted_iota(jnp.int32, (128, t0), 0)
        picks = picks + (routes_ref[k:k + 1, :] == row).astype(F32)
    chosen = picks.T > 0.0
    logits = jnp.where(chosen, dot(xmv, extra), -1e30)
    top = jnp.max(logits, axis=-1, keepdims=True)
    e = jnp.where(chosen, jnp.exp(logits - top), 0.0)
    gts[own] = e / jnp.sum(e, axis=-1, keepdims=True)
    gtt[slot8(z, core)] = gts[own].T[0:8]
    for i in (2, 1):
        buf, at = tokens[i]
        line_send(buf.at[at(z, core)], rxm.at[i * nz + z], nearest[::-1])
        snd.start(buf.at[at(z, core)], buf.at[at(z, core)], rxf.at[i * nz + z], sib)
    for unit in units[1:]:
        expert_onward(*unit)
    for s in nearest:
        tokens_in(0, s)
    for s in nearest:
        for i in (1, 2):
            tokens_in(i, s)
    for s in range(nz):
        arrived(gr.at[slot(s, 1 - core)], rxf.at[s])
    def rows_first(i, carry, j):
        at = pl.ds(pl.multiple_of(i * t2, t2), t2)
        ggu[at, 2 * j * fh:(2 * j + 1) * fh] = dot(
            gr[at], we[2, :, j * fh:(j + 1) * fh]
        ).astype(BF16)
        return carry

    for j in range(2):
        expert_have(2, j)
        lax.fori_loop(0, nz, functools.partial(rows_first, j=j), 0)
    for buf, at, i in ((xm, slot, 1), (gtt, slot8, 2)):
        for s in range(nz):
            arrived(buf.at[at(s, 1 - core)], rxf.at[i * nz + s])
    square[...] = jnp.zeros(square.shape, F32)
    for s in range(nz):
        for k in range(2):
            square[0:8] = gtt[slot8(s, k)]
            gts[slot(s, k)] = square[...].T

    mine128 = pl.ds(pl.multiple_of(core * 128, 128), 128)
    sib128 = pl.ds(pl.multiple_of((1 - core) * 128, 128), 128)
    eloc = cfg_experts(cfg)
    mine_e = z * eloc + (core * eloc) // 2

    def seat(source, at):
        return jnp.where(source > at, source - 1, source)

    def zof(i):
        s = z
        for k in range(nz - 1):
            s = jnp.where(i == k, nearest[nz - 2 - k], s)
        return s

    def blk(i):
        return pl.ds(pl.multiple_of(zof(i) * t2, t2), t2)

    def copy_to_sib(src, dst, ss, rs):
        return pltpu.make_async_remote_copy(
            src_ref=src, dst_ref=dst, send_sem=ss, recv_sem=rs, device_id=sib, device_id_type=MESH
        )

    def copy_to_z(i, src, dst, ss, rs):
        return pltpu.make_async_remote_copy(
            src_ref=src, dst_ref=dst, send_sem=ss, recv_sem=rs, device_id=(c, zof(i)),
            device_id_type=MESH,
        )

    def g_copies(i):
        return (
            copy_to_sib(sibs.at[i], sibr.at[i], sib_s.at[i], sib_r.at[i]),
            copy_to_sib(sgg.at[i], rgg.at[i], sib_s.at[nz + i], sib_r.at[nz + i]),
        )

    def gz_copies(i):
        to = seat(z, zof(i))
        return (
            copy_to_z(i, keep.at[i], zr.at[to], z_s.at[i], z_r.at[to]),
            copy_to_z(i, kgg.at[i], zgg.at[to], z_s.at[nz + i], z_r.at[nz + to]),
        )

    def g_settle(i):
        for cp in g_copies(i):
            cp.wait()
        keep[i] = (keep[i].astype(F32) + sibr[i].astype(F32)).astype(BF16)
        kgg[i] = kgg[i] + rgg[i]

    def rows_mid(i, carry, j):
        x = xm[blk(i)]
        cols = slice(j * fh, (j + 1) * fh)
        first = slice(2 * j * fh, (2 * j + 1) * fh)
        gate = jnp.sum(jnp.where(lane == mine_e, gts[blk(i)], 0.0), axis=1, keepdims=True)
        pre = dot(x, we[0, :, cols])
        up = dot(x, we[1, :, cols])
        ga0 = ggu[blk(i), first].astype(F32)
        sg = 1.0 / (1.0 + jnp.exp(-pre))
        silu = pre * sg
        act = silu * up
        ggc = jnp.sum(act * ga0, axis=1, keepdims=True)
        rowp[...] = jnp.where(lane == mine_e, ggc, 0.0).T[0:8]
        if j == 0:
            kgg[i] = rowp[:, mine128]
            sgg[i] = rowp[:, sib128]
        else:
            kgg[i] += rowp[:, mine128]
            sgg[i] += rowp[:, sib128]
        gact = gate * ga0
        ap[blk(i), cols] = (gate * act).astype(BF16)
        ggu[blk(i), first] = (gact * up * sg * (1.0 + pre * (1.0 - sg))).astype(BF16)
        ggu[blk(i), (2 * j + 1) * fh:(2 * j + 2) * fh] = (gact * silu).astype(BF16)
        return carry

    def rows_back(i, carry):
        total = None
        for k in range(4):
            term = dot_t(
                ggu[blk(i), k * fh:(k + 1) * fh], we[k % 2, :, k // 2 * fh:(k // 2 + 1) * fh]
            )
            total = term if total is None else total + term
        part[...] = total
        keep[i] = part[mine0].astype(BF16)
        sibs[i] = part[sib0].astype(BF16)
        for cp in g_copies(i):
            cp.start()

        @pl.when(i > 0)
        def _():
            g_settle(i - 1)
            for cp in gz_copies(i - 1):
                cp.start()

        return carry

    far = (zq, zb)
    ers = [
        Reduce(
            pc, snd, lambda q, w, m=m: we.at[m, slab_rows(q, w)], efirst.at[m], efx.at[m],
            efy.at[m], esem.at[m],
        )
        for m in range(3)
    ]
    order = (ers[0].d, ers[0].x, ers[0].y, chip)

    def chip_cols(q):
        return pl.ds(pl.multiple_of(q * 2 * per, 128), 2 * per)

    row_sends = snd.take()
    for j in range(2):
        expert_have(0, j)
        expert_have(1, j)
        lax.fori_loop(0, nz, functools.partial(rows_mid, j=j), 0)
        if j == 0:
            snd.drain(dense_sends)
        half = pl.ds(j * fh, fh)
        gw = t_dot(xm[:, chip_cols(order[0])], ggu[:, 2 * j * fh:2 * (j + 1) * fh])
        for m in range(2):
            far[m][:, j * fh:(j + 1) * fh] = gw[:, m * fh:(m + 1) * fh].astype(BF16)
            for w, q in ((0, ers[m].x), (1, ers[m].y)):
                snd.start(
                    far[m].at[pl.ds(w * per, per), half], efirst.at[m, w, :, half],
                    esem.at[m, w], ers[m].to(q),
                )
    snd.drain(row_sends)
    lax.fori_loop(0, nz, rows_back, 0)
    g_settle(nz - 1)

    def expert_step(n, rs):
        for one in rs:
            (one.diagonal, one.straight_x, one.straight_y, lambda: None)[n]()

    for n, q in enumerate(order):
        if n == 0:
            continue
        cols = chip_cols(q)
        gw = t_dot(xm[:, cols], ggu[...])
        for k in range(4):
            we[k % 2, cols, k // 2 * fh:(k // 2 + 1) * fh] = gw[:, k * fh:(k + 1) * fh].astype(BF16)
        expert_step(n, ers[:2])

    def o_copy(i):
        return copy_to_sib(sibs.at[i], sibr.at[i], osib_s.at[i], osib_r.at[i])

    def oz_copy(i):
        to = seat(z, zof(i))
        return copy_to_z(i, okeep.at[i], ozr.at[to], oz_s.at[i], oz_r.at[to])

    def o_settle(i):
        o_copy(i).wait()
        okeep[i] = (okeep[i].astype(F32) + sibr[i].astype(F32)).astype(BF16)

    def rows_out(i, carry):
        part[...] = dot_t(ap[blk(i)], we[2])
        okeep[i] = part[mine0].astype(BF16)
        sibs[i] = part[sib0].astype(BF16)
        o_copy(i).start()

        @pl.when(i > 0)
        def _():
            o_settle(i - 1)
            oz_copy(i - 1).start()

        return carry

    lax.fori_loop(0, nz, rows_out, 0)
    o_settle(nz - 1)

    for n, q in enumerate(order):
        cols = pl.ds(pl.multiple_of(q * 2 * per, 128), 2 * per)
        we[2, cols] = t_dot(gr[:, cols], ap[...]).astype(BF16)
        expert_step(n, ers[2:])

    def fetch(src, room, spot):
        here = room.at[pl.ds(spot // 2 * per, per), pl.ds(spot % 2 * fc, fc)]
        return here, loads.local(src, here)

    def add_far(dst, src):
        here, cp = fetch(src, gr, 0)
        cp.wait()
        add_into(dst, here)

    ers[0].merge(add_far)
    ers[1].merge(add_far)

    gsum = keep[nz - 1].astype(F32)
    ggs = kgg[nz - 1]
    for i in range(nz - 1):
        arrived(zr.at[i], z_r.at[i])
        arrived(zgg.at[i], z_r.at[nz + i])
        gsum = gsum + zr[i].astype(F32)
        ggs = ggs + zgg[i]
    square[...] = jnp.zeros(square.shape, F32)
    square[0:8] = ggs
    ggs = square[...].T
    gate = gts[own]
    glog = (gate * (ggs - jnp.sum(gate * ggs, axis=1, keepdims=True))).astype(BF16)
    extra = wk[:, 2 * HEAD:]
    gxm = gsum + dot_t(glog, extra)
    h1 = h1s[...]
    r = rms(h1, width)
    n = h1 * r
    gy = gxm * gain_m
    g1 = cot_ref[...] + r * (gy - n * (jnp.sum(gy * n, axis=1, keepdims=True) * (1.0 / width)))
    ext = t_dot(xm[own], glog) + t_dot((gxm * n).astype(BF16), (lane0 == 9).astype(BF16))
    exts[...] = ext
    ig_ref[...] = g1
    gat[mine0] = g1.astype(BF16)
    snd.start(gat.at[mine0], gat.at[mine0], rmisc.at[0], sib)
    arrived(gat.at[sib0], rmisc.at[0])
    gav = gat[...]
    go = dot(gav, wb[...]).astype(BF16)
    brs = Reduce(pc, snd, lambda q, w: wb.at[slab_rows(q, w)], bfirst, bfx, bfy, bsem)

    def out_grads(k, carry):
        cols = pl.ds(pl.multiple_of(k * 2 * per, 128), 2 * per)
        wb[cols] = t_dot(gat[:, cols], obs[...]).astype(BF16)
        return carry

    lax.fori_loop(0, nch, out_grads, 0)
    brs.diagonal()
    brs.straight_x()
    brs.straight_y()
    obs[...] = go

    cos, sin = cosr[...], sinr[...]
    gkv[...] = jnp.zeros(gkv.shape, F32)

    def one_head(hd, carry):
        cols = pl.ds(pl.multiple_of(hd * HEAD, HEAD), HEAD)
        s = dot_t(qs[:, cols], kv[:, 0:HEAD]) * scale
        pe = jnp.where(ok, jnp.exp(s - jnp.sum(jnp.where(lane == hd, lses[...], 0.0), axis=1, keepdims=True)), 0.0)
        gp = dot_t(obs[:, cols], kv[:, HEAD:])
        delta = jnp.sum(pe * gp, axis=-1, keepdims=True)
        gs = (pe * (gp - delta)).astype(BF16)
        gq = dot(gs, kv[:, 0:HEAD]) * scale
        graw[:, cols] = rope(gq, cos, -sin).astype(BF16)
        gkv[:, 0:HEAD] += t_dot(gs, qs[:, cols])
        gkv[:, HEAD:] += t_dot(pe.astype(BF16), obs[:, cols])
        return carry

    lax.fori_loop(0, heads, one_head, 0)
    gkvb[...] = gkv[...].astype(BF16)
    for k in range(1, nch):
        q = (chip + k) % nch
        snd.start(
            gkvb.at[pl.ds(pl.multiple_of(q * t2, t2), t2)], gkvr.at[k - 1], rkv.at[k],
            (q * 2 + core, z),
        )

    part[...] = dot_t(graw[:, :qw], wq[...])

    def query_grads(k, carry):
        cols = pl.ds(pl.multiple_of(k * 2 * per, 128), 2 * per)
        wq[cols] = t_dot(xa[:, cols], graw[:, 0:qw]).astype(BF16)
        return carry

    lax.fori_loop(0, nch, query_grads, 0)
    qrs = Reduce(
        pc, snd, lambda q, w: wq.at[slab_rows(q, w)], qfirst, qfx, qfy, qsem
    )
    qrs.diagonal()
    qrs.straight_x()
    qrs.straight_y()
    brs.merge(add_into)
    gk = gkv[mine]
    for k in range(1, nch):
        arrived(gkvr.at[k - 1], rkv.at[k])
        gk = gk + gkvr[k - 1].astype(F32)
    graw[:, qw:qw + HEAD] = rope(gk[:, :HEAD] * scale, cos, -sin).astype(BF16)
    graw[:, qw + HEAD:] = gk[:, HEAD:].astype(BF16)
    part[...] += dot_t(graw[:, qw:], wk[:, :2 * HEAD])
    snd.start(part.at[sib0], pget, rmisc.at[1], sib)

    def key_grads(k, carry):
        cols = pl.ds(pl.multiple_of(k * 2 * per, 128), 2 * per)
        wk[cols, 0:2 * HEAD] = t_dot(xa[:, cols], graw[:, qw:]).astype(BF16)
        return carry

    lax.fori_loop(0, nch, key_grads, 0)
    arrived(pget, rmisc.at[1])
    gxa = part[mine0] + pget[...]
    h = h_ref[...].astype(F32)
    r = rms(h, width)
    n = h * r
    gy = gxa * gain_a
    ig_ref[...] += r * (gy - n * (jnp.sum(gy * n, axis=1, keepdims=True) * (1.0 / width)))
    wk[:, 2 * HEAD:] = (
        exts[...] + t_dot((gxa * n).astype(BF16), (lane0 == 8).astype(BF16))
    ).astype(BF16)
    krs = Reduce(
        pc, snd, lambda q, w: wk.at[slab_rows(q, w)], kfirst, kfx, kfy, ksem
    )
    krs.diagonal()
    krs.straight_x()
    krs.straight_y()
    krs.merge(add_into)
    qrs.merge(add_into)
    ers[2].merge(add_far)

    def piece(q, w):
        return pl.ds(pl.multiple_of((chip * 2 + w) * per + q * rp, 16), rp)

    groups = (
        (brs, lambda rows: wb.at[rows], zrb, rzb, fb, frb),
        (qrs, lambda rows: wq.at[rows], zrq, rzq, fq, frq),
        (krs, lambda rows: wk.at[rows], zrk, rzk, fk, frk),
    )

    def column_out(which):
        rs, at, zrecv, rz, _, _ = groups[which]
        rs.wait()
        for w in range(2):
            dst = rs.slab(chip, w)
            dst[...] = (
                dst[...].astype(F32) + rs.fx[w].astype(F32) + rs.fy[w].astype(F32)
            ).astype(BF16)
        for q in nearest[::-1]:
            to = seat(z, q)
            for w in range(2):
                snd.start(at(piece(q, w)), zrecv.at[to, w], rz.at[2 * to + w], (c, q))

    def column_in(which):
        _, at, zrecv, rz, fin, get = groups[which]
        for w in range(2):
            tot = at(piece(z, w))[...].astype(F32)
            for i in range(nz - 1):
                arrived(zrecv.at[i, w], rz.at[2 * i + w])
                tot = tot + zrecv[i, w].astype(F32)
            fin[w] = tot
        snd.start(fin.at[1 - core], get, rmisc.at[5 + which], sib)

    e_own = []
    e_outs = (eg_out, eu_out, ed_out)

    def expert_final(m):
        ers[m].wait()
        got = [
            fetch(src.at[m, w], room, 2 * m + w)
            for src, room in ((efx, gr), (efy, xm)) for w in range(2)
        ]
        for _, cp in got:
            cp.wait()
        for w in range(2):
            dst = ers[m].slab(chip, w)
            tot = dst[...].astype(F32) + got[w][0][...].astype(F32)
            dst[...] = (tot + got[2 + w][0][...].astype(F32)).astype(BF16)
        snd.start(ers[m].slab(chip, 1 - core), esibr.at[m], rmisc.at[2 + m], sib)
        e_own.append(loads.local(ers[m].slab(chip, core), e_outs[m].at[core]))

    column_out(0)
    expert_final(0)
    expert_final(1)
    osum = okeep[nz - 1].astype(F32) + h1s[...]
    base = nz * t2 - (nz - 1) * t0
    room = [xm.at[pl.ds(base + i * t0, t0)] for i in range(nz - 1)]
    got = []
    for i in range(nz - 1):
        arrived(ozr.at[i], oz_r.at[i])
        got.append(loads.local(ozr.at[i], room[i]))
    for i in range(nz - 1):
        got[i].wait()
        osum = osum + room[i][...].astype(F32)
    out_ref[...] = osum
    column_out(1)
    column_in(0)
    column_out(2)
    for m in range(2):
        arrived(esibr.at[m], rmisc.at[2 + m])
        e_own.append(loads.local(esibr.at[m], e_outs[m].at[1 - core]))
    column_in(1)
    expert_final(2)
    column_in(2)
    arrived(esibr.at[2], rmisc.at[4])
    e_own.append(loads.local(esibr.at[2], e_outs[2].at[1 - core]))

    def half(k, count):
        return pl.ds(pl.multiple_of(k * count, 128), count)

    for k, (out, count, fin, get, off) in enumerate((
        (gwo_out, qw, fb, frb, 0), (gwq_out, qw, fq, frq, 0),
        (gwk_out, HEAD, fk, frk, 0), (gwv_out, HEAD, fk, frk, HEAD),
    )):
        if k < 3:
            arrived(get, rmisc.at[5 + k])
        out[:, half(core, count)] = fin[core, :, off:off + count]
        out[:, half(1 - core, count)] = get[:, off:off + count]
    square[...] = jnp.zeros(square.shape, F32)
    square[0:rp] = fk[core, :, 2 * HEAD:] + frk[:, 2 * HEAD:]
    turned = square[...].T
    gwr_out[...] = turned[0:gwr_out.shape[0], 0:rp]
    gna_out[...] = turned[8:9, 0:rp]
    gnm_out[...] = turned[9:10, 0:rp]
    for cp in e_own:
        cp.wait()
    for i in range(nz - 1):
        for cp in gz_copies(i):
            cp.wait_send()
        oz_copy(i).wait_send()
    snd.drain()


def cfg_experts(cfg):
    return cfg[7]


def layer_call(cfg, args):
    nctx, nz, width, rp, t0, heads, fc, eloc = cfg
    nch, t2, dp = nctx // 2, 2 * t0, nctx * nz * rp
    qw = heads * HEAD
    kx = 3 * HEAD
    ca = qw + kx
    keys = nch * t2
    rows = nz * t2
    per = nz * rp
    experts = args[9].shape[0]
    vm = pl.BlockSpec(memory_space=pltpu.VMEM)
    hb = pl.BlockSpec(memory_space=pltpu.HBM)
    sds = jax.ShapeDtypeStruct
    dma = pltpu.SemaphoreType.DMA
    v = pltpu.VMEM
    return pl.pallas_call(
        functools.partial(layer_kernel, cfg),
        out_shape=(
            sds((t0, dp), F32), sds((t0, dp), F32),
            sds((2, per, fc), BF16), sds((2, per, fc), BF16), sds((2, per, fc), BF16),
            sds((rp, 2 * qw), F32), sds((rp, 2 * HEAD), F32), sds((rp, 2 * HEAD), F32),
            sds((rp, 2 * qw), F32), sds((1, rp), F32), sds((1, rp), F32), sds((experts, rp), F32),
        ) + (sds((3, 2, per, fc), BF16),) * 3 + (sds((nz - 1, t0, dp), BF16),),
        in_specs=[vm] * 10 + [hb] * 5,
        out_specs=(vm, vm, hb, hb, hb) + (vm,) * 7 + (hb,) * 4,
        scratch_shapes=[
            v((dp, kx), BF16), v((dp, qw), BF16), v((dp, qw), BF16), v((3, dp, fc), BF16),
            v((nz * 2 * rp, kx), BF16), v((nz * 2 * rp, qw), BF16), v((nz * 2 * rp, qw), BF16),
            v((2, t0, dp), BF16), v((t2, HEAD), F32), v((t2, HEAD), F32), v((128, 128), F32),
            v((t2, qw), BF16), v((keys, 2 * HEAD), BF16), v((t2, 128), F32), v((t2, qw), BF16),
            v((t2, dp), BF16), v((t0, dp), F32),
            v((rows, dp), BF16), v((rows, dp), BF16), v((rows, 128), F32),
            v((rows, 2 * fc), BF16), v((rows, fc), BF16),
            v((nz, t0, dp), BF16), v((nz, t0, dp), BF16), v((nz, t0, dp), BF16),
            v((nz - 1, t0, dp), BF16), v((nz, t0, dp), BF16),
            v((nz, 8, t0), F32), v((nz, 8, t0), F32), v((nz, 8, t0), F32),
            v((nz - 1, 8, t0), F32),
            v((nz * 2 * 8, t0), F32),
            v((t2, dp), BF16), v((keys, 2 * HEAD), F32), v((keys, 2 * HEAD), BF16),
            v((nch - 1, t2, 2 * HEAD), BF16), v((t2, ca - 128), BF16),
            v((t2, dp), F32), v((t0, dp), F32), v((dp, 128), F32),
            v((3, per, fc), BF16),
            v((2, per, qw), BF16), v((2, per, qw), BF16), v((2, per, qw), BF16),
            v((2, per, qw), BF16), v((2, per, qw), BF16), v((2, per, qw), BF16),
            v((2, per, kx), BF16), v((2, per, kx), BF16), v((2, per, kx), BF16),
            v((nz - 1, 2, rp, qw), BF16), v((nz - 1, 2, rp, qw), BF16),
            v((nz - 1, 2, rp, kx), BF16),
            v((2, rp, qw), F32), v((2, rp, qw), F32), v((2, rp, kx), F32),
            v((rp, qw), F32), v((rp, qw), F32), v((rp, kx), F32),
            v((8, t2), F32),
            dma((300,)), dma((60,)), dma((nctx * nz,)), dma((nctx * nz,)), dma((nctx * nz,)),
            dma((6 * nctx,)), dma((nz,)), dma((nz,)), dma((nz,)), dma((2,)), dma((3 * nz,)), dma((3 * nz,)),
            dma((2 * nz,)), dma((2 * nz,)), dma((2 * nz,)), dma((2 * nz,)),
            dma((nz,)), dma((nz,)), dma((nz,)), dma((nz,)), dma((8,)), dma((3, 6)), dma((6,)),
            dma((6,)), dma((6,)), dma((nch,)), dma((nch,)), dma((2 * nz,)), dma((2 * nz,)),
            dma((2 * nz,)),
        ],
        compiler_params=pltpu.CompilerParams(
            collective_id=0, has_side_effects=True, vmem_limit_bytes=64 * 2**20
        ),
        name="layer",
    )(*args)


def pass_kernel(count, pairs, *refs):
    total = count + pairs
    for k in range(count):
        refs[total + k][...] = refs[k][...]
    for k in range(count, total):
        for half in range(2):
            refs[total + k][:, half, :] = refs[k][half].astype(F32)


def pass_on(arrays, pairs):
    vm = pl.BlockSpec(memory_space=pltpu.VMEM)
    sds = jax.ShapeDtypeStruct
    out_shape = [sds(x.shape, x.dtype) for x in arrays]
    out_shape += [sds((x.shape[1], 2, x.shape[2]), F32) for x in pairs]
    return pl.pallas_call(
        functools.partial(pass_kernel, len(arrays), len(pairs)),
        out_shape=tuple(out_shape),
        in_specs=[vm] * len(out_shape),
        out_specs=(vm,) * len(out_shape),
        name="pass_on",
    )(*arrays, *pairs)


def body(hidden, routes, cot, na, wq, wk, wv, wo, nm, wr, wg, wu, wd):
    nctx, nz = lax.axis_size("ctx"), lax.axis_size("wsh")
    t0, width = hidden.shape[1], hidden.shape[2]
    rp = wq.shape[1]
    eloc, ff = wg.shape[2], wg.shape[3]
    heads = wq.shape[2] // HEAD // 2
    fc = eloc * ff // 2
    cfg = (nctx, nz, width, rp, t0, heads, fc, eloc)
    pos = np.arange(nctx * t0, dtype=np.float32)
    freq = np.float32(BASE) ** (-np.arange(HEAD // 2, dtype=np.float32) * 2.0 / HEAD)
    ang = pos[:, None] * freq.astype(np.float32)[None, :]
    cos, sin = np.cos(ang), np.sin(ang)
    cosf = jnp.asarray(np.concatenate([cos, cos], axis=1), F32)
    sinf = jnp.asarray(np.concatenate([-sin, sin], axis=1), F32)
    halves = [jnp.transpose(w[0], (1, 0, 2)) for w in (wg, wu, wd)]
    r = layer_call(
        cfg,
        (hidden[0], routes[0, 0].T, cot[0], wq[0], wk[0], wv[0], wo[0], na, nm, wr[0].T, *halves,
         cosf, sinf),
    )
    out, ig, eg, eu, ed, gwq, gwk, gwv, gwo, gna, gnm, gwr = r[:12]
    out, ig, gwq, gwk, gwv, gwo, gna, gnm, gwr, eg, eu, ed = pass_on(
        (out, ig, gwq, gwk, gwv, gwo, gna, gnm, gwr), (eg, eu, ed)
    )
    return (
        out[None], ig[None], gna, gwq[None], gwk[None], gwv[None], gwo[None],
        gnm, gwr.T[None], eg[None], eu[None], ed[None],
    )


def shifted(value, axis, steps):
    count = lax.axis_size(axis)
    pairs = [(source, (source + steps) % count) for source in range(count)]
    return lax.ppermute(value, axis, pairs)


def normalize(hidden_state, gain):
    return (
        hidden_state
        * lax.rsqrt(jnp.mean(hidden_state * hidden_state, axis=-1, keepdims=True) + NORM_EPSILON)
        * gain
    )


def rotary(token_positions, head_size):
    half_size = head_size // 2
    frequency = ROTARY_BASE ** (-jnp.arange(half_size, dtype=jnp.float32) * 2.0 / head_size)
    angles = token_positions.astype(jnp.float32)[:, None] * frequency[None, :]
    return (jnp.cos(angles)[:, None, :], jnp.sin(angles)[:, None, :])


def apply_rotary(values_in, cosine, sine_rows, direction):
    half_size = values_in.shape[-1] // 2
    first_half = values_in[..., :half_size]
    second = values_in[..., half_size:]
    return jnp.concatenate(
        [
            first_half * cosine - direction * second * sine_rows,
            second * cosine + direction * first_half * sine_rows,
        ],
        axis=-1,
    )


def slot_targets(picks_in, matches):
    flat_matches = matches.reshape(-1, matches.shape[-1]).astype(jnp.int32)
    earlier = jnp.cumsum(flat_matches, axis=0) - flat_matches
    return picks_in.reshape(-1) * CAP + jnp.sum(earlier * flat_matches, axis=1)


def score_rows(query_low, key_rows, token_positions):
    total_rows = query_low.shape[0]
    head_size = query_low.shape[2]
    grouped_heads = query_low.reshape(total_rows, key_rows.shape[1], -1, head_size)
    scores = jnp.einsum(
        "qhgd,khd->hgqk", grouped_heads, key_rows, preferred_element_type=jnp.float32
    ) * head_size ** (-0.5)
    allowed = jnp.arange(key_rows.shape[0], dtype=jnp.int32)[None, :] <= token_positions[:, None]
    return (grouped_heads, jnp.where(allowed[None, None], scores, -1e30))


def attend(query_low, key_rows, value_rows, token_positions):
    grouped_heads, scores = score_rows(query_low, key_rows, token_positions)
    highest = jnp.max(scores, axis=-1, keepdims=True)
    log_total = highest + jnp.log(jnp.sum(jnp.exp(scores - highest), axis=-1, keepdims=True))
    weights = jnp.exp(scores - log_total).astype(jnp.bfloat16)
    attended = jnp.einsum("hgqk,khd->qhgd", weights, value_rows, preferred_element_type=jnp.float32)
    return (attended.reshape(query_low.shape[0], -1), log_total)


def attend_grad(query_low, key_rows, value_rows, token_positions, log_total, grad_mixed):
    grouped_heads, scores = score_rows(query_low, key_rows, token_positions)
    score_scale = query_low.shape[-1] ** (-0.5)
    softmax_rows = jnp.exp(scores - log_total)
    weights = softmax_rows.astype(jnp.bfloat16)
    grad_grouped = grad_mixed.reshape(grouped_heads.shape)
    grad_weights = jnp.einsum(
        "qhgd,khd->hgqk", grad_grouped, value_rows, preferred_element_type=jnp.float32
    )
    grad_values = jnp.einsum(
        "hgqk,qhgd->khd", weights, grad_grouped, preferred_element_type=jnp.float32
    )
    row_inner = jnp.sum(softmax_rows * grad_weights, axis=-1, keepdims=True)
    grad_scores = (softmax_rows * (grad_weights - row_inner)).astype(jnp.bfloat16)
    grad_query = (
        jnp.einsum("hgqk,khd->qhgd", grad_scores, key_rows, preferred_element_type=jnp.float32)
        * score_scale
    )
    grad_keys = (
        jnp.einsum("hgqk,qhgd->khd", grad_scores, grouped_heads, preferred_element_type=jnp.float32)
        * score_scale
    )
    return (grad_query.reshape(query_low.shape), grad_keys, grad_values)


def collect_key_grads(grad_keys, grad_values, total_rows):
    cycle_size = lax.axis_size("ctx")
    own_index = lax.axis_index("ctx")
    both_grads = jnp.stack([grad_keys, grad_values])

    def block_piece(block_index):
        return lax.dynamic_slice_in_dim(both_grads, block_index * total_rows, total_rows, 1)

    def cycle_step(step_index, carried):
        moved = shifted(carried.astype(jnp.bfloat16), "ctx", -1).astype(carried.dtype)
        block_index = (own_index + step_index) % cycle_size
        weight_now = jnp.where(step_index < cycle_size, 1.0, 0.0).astype(jnp.float32)
        return moved + weight_now * block_piece(block_index)

    collected = lax.fori_loop(1, cycle_size + 1, cycle_step, block_piece(own_index))
    return (collected[0], collected[1])


def forward_layer(hidden_state, picks_in, dense_set, expert_set):
    gain_attn, query_matrix, key_matrix, value_matrix, output_matrix, gain_moe, router_matrix = (
        dense_set
    )
    gate_w, up_w, down_w = expert_set
    total_rows, model_width = hidden_state.shape
    token_positions = lax.axis_index("ctx") * total_rows + jnp.arange(total_rows, dtype=jnp.int32)
    cosine, sine_rows = rotary(token_positions, HEAD_DIM)
    attention_normed = normalize(hidden_state, gain_attn.astype(jnp.float32)).astype(jnp.bfloat16)
    query_unrotated = jnp.dot(
        attention_normed, query_matrix, preferred_element_type=jnp.float32
    ).reshape(total_rows, QUERY_HEADS, HEAD_DIM)
    key_unrotated = jnp.dot(
        attention_normed, key_matrix, preferred_element_type=jnp.float32
    ).reshape(total_rows, KEY_VALUE_HEADS, HEAD_DIM)
    query_low = apply_rotary(query_unrotated, cosine, sine_rows, 1.0).astype(jnp.bfloat16)
    key_low = apply_rotary(key_unrotated, cosine, sine_rows, 1.0).astype(jnp.bfloat16)
    value_low = (
        jnp.dot(attention_normed, value_matrix, preferred_element_type=jnp.float32)
        .astype(jnp.bfloat16)
        .reshape(total_rows, KEY_VALUE_HEADS, HEAD_DIM)
    )
    key_rows, value_rows = (
        lax.all_gather(key_low, "ctx", axis=0, tiled=True),
        lax.all_gather(value_low, "ctx", axis=0, tiled=True),
    )
    attended, log_total = attend(query_low, key_rows, value_rows, token_positions)
    mixed_reduced = attended.astype(jnp.bfloat16)
    post_attention = hidden_state + lax.dot_general(
        mixed_reduced, output_matrix, (((1,), (1,)), ((), ())), preferred_element_type=jnp.float32
    )
    expert_normed = normalize(post_attention, gain_moe.astype(jnp.float32)).astype(jnp.bfloat16)
    router_logits = jnp.dot(expert_normed, router_matrix, preferred_element_type=jnp.float32)
    expert_count = router_logits.shape[1]
    matches = picks_in[:, :, None] == jnp.arange(expert_count, dtype=jnp.int32)[None, None, :]
    gate_weights = jax.nn.softmax(
        jnp.sum(jnp.where(matches, router_logits[:, None, :], 0.0), axis=-1), axis=-1
    )
    targets = slot_targets(picks_in, matches)
    outgoing = (
        jnp.zeros((expert_count * CAP, model_width), jnp.bfloat16)
        .at[targets]
        .set(jnp.repeat(expert_normed, TOP, axis=0))
    )
    group_count = lax.axis_size("wsh")
    local_count = gate_w.shape[1]
    arrived = lax.all_to_all(
        outgoing.reshape(group_count, local_count, CAP, model_width),
        "wsh",
        split_axis=0,
        concat_axis=0,
        tiled=True,
    )
    gate_pre = jnp.einsum("sjcd,djf->sjcf", arrived, gate_w, preferred_element_type=jnp.float32)
    up_pre = jnp.einsum("sjcd,djf->sjcf", arrived, up_w, preferred_element_type=jnp.float32)
    activations = (jax.nn.silu(gate_pre) * up_pre).astype(jnp.bfloat16)
    produced = jnp.einsum(
        "sjcf,djf->sjcd", activations, down_w, preferred_element_type=jnp.float32
    ).astype(jnp.bfloat16)
    returned = lax.all_to_all(produced, "wsh", split_axis=0, concat_axis=0, tiled=True)
    returned, arrived, gate_pre, up_pre = (returned, arrived, gate_pre, up_pre)
    picked = (
        returned.reshape(-1, model_width)[targets]
        .reshape(total_rows, TOP, model_width)
        .astype(jnp.float32)
    )
    after_moe = post_attention + jnp.sum(gate_weights[:, :, None] * picked, axis=1)
    stored = (
        hidden_state,
        attention_normed,
        query_low,
        key_low,
        value_low,
        log_total,
        mixed_reduced,
        post_attention,
        expert_normed,
        matches,
        gate_weights,
        targets,
        picked,
        arrived,
        gate_pre,
        up_pre,
    )
    return (after_moe, stored, (key_rows, value_rows))


def backward_layer(incoming, stored, dense_set, expert_set, key_rows, value_rows):
    (
        hidden_state,
        attention_normed,
        query_low,
        key_low,
        value_low,
        log_total,
        mixed_reduced,
        post_attention,
        expert_normed,
        matches,
        gate_weights,
        targets,
        picked,
        arrived,
        gate_pre,
        up_pre,
    ) = stored
    gain_attn, query_matrix, key_matrix, value_matrix, output_matrix, gain_moe, router_matrix = (
        dense_set
    )
    gate_w, up_w, down_w = expert_set
    total_rows, model_width = hidden_state.shape
    token_positions = lax.axis_index("ctx") * total_rows + jnp.arange(total_rows, dtype=jnp.int32)
    cosine, sine_rows = rotary(token_positions, HEAD_DIM)
    grad_y = (gate_weights[:, :, None] * incoming[:, None, :]).astype(jnp.bfloat16)
    grad_gates = jnp.sum(incoming[:, None, :] * picked, axis=-1)
    grad_chosen = gate_weights * (
        grad_gates - jnp.sum(gate_weights * grad_gates, axis=-1, keepdims=True)
    )
    grad_logits = jnp.sum(jnp.where(matches, grad_chosen[:, :, None], 0.0), axis=1).astype(
        jnp.bfloat16
    )
    slot_total = arrived.shape[0] * arrived.shape[1] * arrived.shape[2]
    outgoing = (
        jnp.zeros((slot_total, model_width), jnp.bfloat16)
        .at[targets]
        .set(grad_y.reshape(-1, model_width))
    )
    grad_arrived = lax.all_to_all(
        outgoing.reshape(arrived.shape), "wsh", split_axis=0, concat_axis=0, tiled=True
    )
    grad_acts = jnp.einsum(
        "sjcd,djf->sjcf", grad_arrived, down_w, preferred_element_type=jnp.float32
    )
    sigmoid_gate = jax.nn.sigmoid(gate_pre)
    silu_gate = jax.nn.silu(gate_pre)
    activations = (silu_gate * up_pre).astype(jnp.bfloat16)
    grad_gate = (
        grad_acts * up_pre * sigmoid_gate * (1.0 + gate_pre * (1.0 - sigmoid_gate))
    ).astype(jnp.bfloat16)
    grad_up = (grad_acts * silu_gate).astype(jnp.bfloat16)
    grad_rows = (
        jnp.einsum("sjcf,djf->sjcd", grad_gate, gate_w, preferred_element_type=jnp.float32)
        + jnp.einsum("sjcf,djf->sjcd", grad_up, up_w, preferred_element_type=jnp.float32)
    ).astype(jnp.bfloat16)
    grad_back = lax.all_to_all(grad_rows, "wsh", split_axis=0, concat_axis=0, tiled=True)
    expert_grads = (
        lax.psum_scatter(
            jnp.einsum(
                "sjcd,sjcf->djf", arrived, grad_gate, preferred_element_type=jnp.float32
            ).astype(jnp.bfloat16),
            "ctx",
            scatter_dimension=0,
            tiled=True,
        ).astype(jnp.float32),
        lax.psum_scatter(
            jnp.einsum(
                "sjcd,sjcf->djf", arrived, grad_up, preferred_element_type=jnp.float32
            ).astype(jnp.bfloat16),
            "ctx",
            scatter_dimension=0,
            tiled=True,
        ).astype(jnp.float32),
        lax.psum_scatter(
            jnp.einsum(
                "sjcd,sjcf->djf", grad_arrived, activations, preferred_element_type=jnp.float32
            ).astype(jnp.bfloat16),
            "ctx",
            scatter_dimension=0,
            tiled=True,
        ).astype(jnp.float32),
    )
    returned_rows = (
        grad_back.reshape(-1, model_width)[targets]
        .reshape(total_rows, TOP, model_width)
        .astype(jnp.float32)
    )
    grad_normed_moe = jnp.sum(returned_rows, axis=1) + lax.dot_general(
        grad_logits, router_matrix, (((1,), (1,)), ((), ())), preferred_element_type=jnp.float32
    )
    router_term = jnp.einsum(
        "td,te->de", expert_normed, grad_logits, preferred_element_type=jnp.float32
    )
    unused_moe, pull_moe = jax.vjp(normalize, post_attention, gain_moe.astype(jnp.float32))
    grad_after_norm, gain_moe_term = pull_moe(grad_normed_moe)
    grad_after_attn = incoming + grad_after_norm
    grad_attn = grad_after_attn.astype(jnp.bfloat16)
    out_term = jnp.einsum("td,tj->dj", grad_attn, mixed_reduced, preferred_element_type=jnp.float32)
    grad_mixed = jnp.dot(grad_attn, output_matrix, preferred_element_type=jnp.float32).astype(
        jnp.bfloat16
    )
    grad_query, grad_keys, grad_values = attend_grad(
        query_low, key_rows, value_rows, token_positions, log_total, grad_mixed
    )
    grad_key, grad_value = collect_key_grads(grad_keys, grad_values, total_rows)
    grad_query_raw = (
        apply_rotary(grad_query, cosine, sine_rows, -1.0)
        .reshape(total_rows, -1)
        .astype(jnp.bfloat16)
    )
    grad_key_raw = (
        apply_rotary(grad_key, cosine, sine_rows, -1.0).reshape(total_rows, -1).astype(jnp.bfloat16)
    )
    grad_value_raw = grad_value.reshape(total_rows, -1).astype(jnp.bfloat16)
    contract_last = (((1,), (1,)), ((), ()))
    grad_normed_attn = lax.dot_general(
        grad_query_raw, query_matrix, contract_last, preferred_element_type=jnp.float32
    )
    grad_normed_attn = grad_normed_attn + lax.dot_general(
        grad_key_raw, key_matrix, contract_last, preferred_element_type=jnp.float32
    )
    grad_normed_attn = grad_normed_attn + lax.dot_general(
        grad_value_raw, value_matrix, contract_last, preferred_element_type=jnp.float32
    )
    query_term = jnp.einsum(
        "td,tf->df", attention_normed, grad_query_raw, preferred_element_type=jnp.float32
    )
    key_term = jnp.einsum(
        "td,tf->df", attention_normed, grad_key_raw, preferred_element_type=jnp.float32
    )
    value_term = jnp.einsum(
        "td,tf->df", attention_normed, grad_value_raw, preferred_element_type=jnp.float32
    )
    unused_attn, pull_attn = jax.vjp(normalize, hidden_state, gain_attn.astype(jnp.float32))
    grad_before, gain_attn_term = pull_attn(grad_normed_attn)
    layer_grads = (
        lax.psum_scatter(gain_attn_term, ("ctx", "wsh"), scatter_dimension=0, tiled=True),
        lax.psum_scatter(query_term, ("ctx", "wsh"), scatter_dimension=0, tiled=True),
        lax.psum_scatter(key_term, ("ctx", "wsh"), scatter_dimension=0, tiled=True),
        lax.psum_scatter(value_term, ("ctx", "wsh"), scatter_dimension=0, tiled=True),
        lax.psum_scatter(out_term, ("ctx", "wsh"), scatter_dimension=0, tiled=True),
        lax.psum_scatter(gain_moe_term, ("ctx", "wsh"), scatter_dimension=0, tiled=True),
        lax.psum_scatter(router_term, ("ctx", "wsh"), scatter_dimension=0, tiled=True),
    )
    return (grad_after_attn + grad_before, layer_grads, expert_grads)


def plain_body(
    hidden_in,
    routes,
    cotangent,
    norm_attn,
    w_query,
    key_projection,
    value_projection,
    w_out,
    norm_moe,
    w_router,
    w_gate,
    w_up,
    w_down,
):
    hidden_state = hidden_in[0].astype(jnp.float32)
    layer_number = 0
    dense_set = (
        lax.all_gather(norm_attn[layer_number], ("ctx", "wsh"), axis=0, tiled=True),
        lax.all_gather(w_query[layer_number], ("ctx", "wsh"), axis=0, tiled=True),
        lax.all_gather(key_projection[layer_number], ("ctx", "wsh"), axis=0, tiled=True),
        lax.all_gather(value_projection[layer_number], ("ctx", "wsh"), axis=0, tiled=True),
        lax.all_gather(w_out[layer_number], ("ctx", "wsh"), axis=0, tiled=True),
        lax.all_gather(norm_moe[layer_number], ("ctx", "wsh"), axis=0, tiled=True),
        lax.all_gather(w_router[layer_number], ("ctx", "wsh"), axis=0, tiled=True),
    )
    expert_set = (
        lax.all_gather(w_gate[layer_number], "ctx", axis=0, tiled=True),
        lax.all_gather(w_up[layer_number], "ctx", axis=0, tiled=True),
        lax.all_gather(w_down[layer_number], "ctx", axis=0, tiled=True),
    )
    hidden_state, stored, gathered = forward_layer(
        hidden_state, routes[layer_number, 0], dense_set, expert_set
    )
    records = [(stored, None, None, None)]
    incoming = cotangent[0]
    dense_grads = []
    expert_grads = []
    layer_number = 0
    stored, dense_set, expert_set, gathered = records[layer_number]
    dense_set = (
        lax.all_gather(norm_attn[layer_number], ("ctx", "wsh"), axis=0, tiled=True),
        lax.all_gather(w_query[layer_number], ("ctx", "wsh"), axis=0, tiled=True),
        lax.all_gather(key_projection[layer_number], ("ctx", "wsh"), axis=0, tiled=True),
        lax.all_gather(value_projection[layer_number], ("ctx", "wsh"), axis=0, tiled=True),
        lax.all_gather(w_out[layer_number], ("ctx", "wsh"), axis=0, tiled=True),
        lax.all_gather(norm_moe[layer_number], ("ctx", "wsh"), axis=0, tiled=True),
        lax.all_gather(w_router[layer_number], ("ctx", "wsh"), axis=0, tiled=True),
    )
    expert_set = (
        lax.all_gather(w_gate[layer_number], "ctx", axis=0, tiled=True),
        lax.all_gather(w_up[layer_number], "ctx", axis=0, tiled=True),
        lax.all_gather(w_down[layer_number], "ctx", axis=0, tiled=True),
    )
    gathered = (
        lax.all_gather(stored[3], "ctx", axis=0, tiled=True),
        lax.all_gather(stored[4], "ctx", axis=0, tiled=True),
    )
    incoming, layer_grads, layer_expert = backward_layer(
        incoming, stored, dense_set, expert_set, gathered[0], gathered[1]
    )
    dense_grads.insert(0, layer_grads)
    expert_grads.insert(0, layer_expert)
    stacked_dense = [
        jnp.stack([grads_item[position] for grads_item in dense_grads]) for position in range(7)
    ]
    stacked_expert = [
        jnp.stack([grads_item[position] for grads_item in expert_grads]) for position in range(3)
    ]
    return (
        hidden_state[None],
        incoming[None],
        stacked_dense[0],
        stacked_dense[1],
        stacked_dense[2],
        stacked_dense[3],
        stacked_dense[4],
        stacked_dense[5],
        stacked_dense[6],
        stacked_expert[0],
        stacked_expert[1],
        stacked_expert[2],
    )


def solution(mesh):
    return jax.shard_map(
        body if mesh.shape["ctx"] == 8 and mesh.shape["wsh"] == 4 else plain_body,
        mesh=mesh,
        in_specs=(
            P("wsh", "ctx", None),
            P(None, "wsh", "ctx", None),
            P("wsh", "ctx", None),
            P(None, ("ctx", "wsh")),
            P(None, ("ctx", "wsh"), None),
            P(None, ("ctx", "wsh"), None),
            P(None, ("ctx", "wsh"), None),
            P(None, ("ctx", "wsh"), None),
            P(None, ("ctx", "wsh")),
            P(None, ("ctx", "wsh"), None),
            P(None, "ctx", "wsh", None),
            P(None, "ctx", "wsh", None),
            P(None, "ctx", "wsh", None),
        ),
        out_specs=(
            P("wsh", "ctx", None),
            P("wsh", "ctx", None),
            P(None, ("ctx", "wsh")),
            P(None, ("ctx", "wsh"), None),
            P(None, ("ctx", "wsh"), None),
            P(None, ("ctx", "wsh"), None),
            P(None, ("ctx", "wsh"), None),
            P(None, ("ctx", "wsh")),
            P(None, ("ctx", "wsh"), None),
            P(None, "ctx", "wsh", None),
            P(None, "ctx", "wsh", None),
            P(None, "ctx", "wsh", None),
        ),
        check_vma=False,
    )
```
